512 devices in a mesh: dp: 64 (over z_lo, x, core), code: 8 (over z_hi, y).
Axes of the slice: x: 4, y: 4, z: 16 (z_hi: 2, z_lo: 8; z = z_hi * 8 + z_lo), core: 2. Of those that a mesh axis runs over, the one named last changes fastest.
Arguments:
- latents: bfloat16 [24576, 256], P('dp'), may hold values from -6 to 6
- codebook: bfloat16 [32768, 256], P('code'), may hold values from -6 to 6
Outputs:
- targets: float32 [32768, 256], P(('code', 'dp'))
- reconstruction: float32 [24576, 256], P('dp')
The draws below stay inside these ranges and needn't reach their ends.
All inputs are finite; a program needn't handle non-finite values.
Results may differ from the reference program's by a relative error of at most 0.0022.
Values sent between devices are 32-bit elements; how exact they have to be, the bound alone decides.
No kernel may reach another device: no remote copies, remote signals or barrier semaphores. Data moves between devices by JAX's collectives and lax.ppermute only.
A program may use at most 64 MiB of HBM per device.

```python
import jax
import jax.numpy as jnp
from jax import lax

D = 256
TOK_DEV = 384
ITERS = 3
TOKENS = 24576
CODES = 32768
N_DP = 64


def level_of(own_key, shape, pieces, low, largest):
    loudness = 1.0
    for dim, parts in pieces:
        draws = jax.random.uniform(jax.random.fold_in(jax.random.fold_in(own_key, 6), dim), (parts,), jnp.float32, low / len(pieces), largest / len(pieces))
        loudness = loudness * jnp.repeat(jnp.exp(draws), shape[dim] // parts).reshape((-1,) + (1,) * (len(shape) - 1 - dim))
    return loudness


def normal_values(rng, extent, scale, limit, shards=(), held_as=jnp.bfloat16):
    loudness = level_of(rng, extent, shards, -0.22, 0.18) if shards else 1.0
    drawn = jax.random.normal(rng, extent, jnp.float32) * scale * loudness
    return jnp.minimum(jnp.maximum(drawn, -limit), limit).astype(held_as)


def setup_inputs(seed: int = 0) -> dict:
    splits = jax.random.split(jax.random.key(seed), 3)
    return {
        "latents": normal_values(splits[0], (TOKENS, D), 1.0, 6.0, ((0, 64),)),
        "codebook": normal_values(splits[1], (CODES, D), 1.0, 6.0, ((0, 8),)),
    }


SHARP = 48.0
EPSILON = 1e-06

def scaled(values):
    floats = values.astype(jnp.float32)
    return lax.rsqrt(lax.optimization_barrier(jnp.mean(floats * floats, axis=-1)) + EPSILON)

def kernel_tile(token_rows, norm_rows, codebook, code_norm):
    inner = jnp.dot(token_rows, codebook.T, preferred_element_type=jnp.float32)
    return jnp.exp(inner * (SHARP / D) * norm_rows[:, None] * code_norm[None, :])

def reference(latents, codebook):
    row_norm = scaled(latents)
    code_norm = scaled(codebook)
    token_blocks = latents.reshape(N_DP, TOK_DEV, D)
    norm_blocks = row_norm.reshape(N_DP, TOK_DEV)
    col_scale = jnp.ones((CODES,), jnp.float32)
    row_scale = jnp.ones((N_DP, TOK_DEV), jnp.float32)
    for sweep_index in range(ITERS):

        def sweep(column_acc, blocks):
            token_rows, norm_rows = blocks
            kernel_now = kernel_tile(token_rows, norm_rows, codebook, code_norm)
            row_block = 1.0 / lax.optimization_barrier(jnp.sum(kernel_now * col_scale[None, :], axis=1))
            return (column_acc + lax.optimization_barrier(jnp.sum(kernel_now * row_block[:, None], axis=0)), row_block)
        column_acc, row_scale = lax.scan(sweep, jnp.zeros((CODES,), jnp.float32), (token_blocks, norm_blocks))
        col_scale = TOKENS / CODES / column_acc

    def finish(target_acc, blocks):
        token_rows, norm_rows, row_block = blocks
        kernel_now = kernel_tile(token_rows, norm_rows, codebook, code_norm)
        plan = (row_block[:, None] * kernel_now * col_scale[None, :]).astype(jnp.bfloat16)
        target_acc = target_acc + jnp.dot(plan.T, token_rows, preferred_element_type=jnp.float32)
        mass = lax.optimization_barrier(jnp.sum(plan.astype(jnp.float32), axis=1))
        rebuilt = jnp.dot(plan, codebook, preferred_element_type=jnp.float32) / mass[:, None]
        return (target_acc, rebuilt)
    target_acc, rebuilt = lax.scan(finish, jnp.zeros((CODES, D), jnp.float32), (token_blocks, norm_blocks, row_scale))
    targets = target_acc * (CODES / TOKENS)
    return (targets, rebuilt.reshape(TOKENS, D))
```

```python
import jax
import jax.numpy as jnp
from jax import lax
from jax.sharding import Mesh, PartitionSpec as P

ITERS = 3
SHARP = 48.0
EPSILON = 1e-06

AXES = ("z", "x", "c", "h", "y")
Z, X, C, H, Y = 8, 4, 2, 2, 4


def scaled(values):
    floats = values.astype(jnp.float32)
    return lax.rsqrt(jnp.mean(floats * floats, axis=-1) + EPSILON)


def exchange(blocks, axes):
    return lax.all_to_all(blocks, axes, 0, 0, tiled=True)


def spread(block, axes, count):
    return exchange(jnp.broadcast_to(block[None], (count,) + block.shape), axes)


def per_device(latents, codebook):
    token_count, width = latents.shape
    code_count = codebook.shape[0]
    total_tokens = token_count * Z * X * C
    total_codes = code_count * H * Y
    share = code_count // (Z * X * C)
    codebook = codebook.reshape(Z, X, C, share, width).transpose(2, 1, 0, 3, 4).reshape(code_count, width)
    row_norm = scaled(latents)
    code_norm = scaled(codebook)
    inner = jnp.dot(latents, codebook.T, preferred_element_type=jnp.float32)
    tile = jnp.exp(inner * (SHARP / width) * row_norm[:, None] * code_norm[None, :])

    def rows(col_scale):
        part = jnp.sum(tile * col_scale[None, :], axis=1)
        return 1.0 / jnp.sum(spread(part, ("h", "y"), H * Y), axis=0)

    def columns(row_scale):
        part = jnp.sum(tile * row_scale[:, None], axis=0).reshape(C * X, Z * share)
        part = jnp.sum(exchange(part, ("c", "x")), axis=0)
        total = jnp.sum(spread(part, ("z",), Z), axis=0)
        mine = total_tokens / total_codes / total
        return mine, spread(mine, ("c", "x"), C * X).reshape(code_count)

    col_scale = jnp.ones((code_count,), jnp.float32)
    for sweep_index in range(ITERS):
        row_scale = rows(col_scale)
        mine, col_scale = columns(row_scale)

    weighted = (row_scale[:, None] * tile).astype(jnp.bfloat16)
    summed = lax.dot_general(weighted, latents, (((0,), (0,)), ((), ())), preferred_element_type=jnp.float32)
    summed = jnp.sum(exchange(summed.reshape(C, code_count // C, width), "c"), axis=0)
    summed = jnp.sum(exchange(summed.reshape(X, Z * share, width), "x"), axis=0)
    summed = jnp.sum(exchange(summed.reshape(Z, share, width), "z"), axis=0)
    own = lax.dynamic_slice(mine, (lax.axis_index("z") * share,), (share,))
    targets = summed * (own * (total_codes / total_tokens))[:, None]

    plan = (row_scale[:, None] * tile * col_scale[None, :]).astype(jnp.bfloat16)
    mass = jnp.sum(plan.astype(jnp.float32), axis=1)
    numer = jnp.dot(plan, codebook, preferred_element_type=jnp.float32)
    group = token_count // Y
    packed = jnp.concatenate(
        [
            numer.reshape(Y, group, width),
            jnp.pad(mass.reshape(Y, 1, group), ((0, 0), (0, 7), (0, width - group))),
        ],
        axis=1,
    )
    packed = jnp.sum(exchange(packed, "y"), axis=0)
    packed = packed + lax.ppermute(packed, "h", [(0, 1), (1, 0)])
    part = packed[:group] / packed[group, :group][:, None]
    rebuilt = spread(part, ("y",), Y).reshape(token_count, width)
    return (targets, rebuilt)


def solution(mesh):
    fine = Mesh(mesh.devices.reshape(Z, X, C, H, Y), AXES)
    return jax.shard_map(
        per_device,
        mesh=fine,
        in_specs=(P(("z", "x", "c"), None), P(("h", "y"), None)),
        out_specs=(P(("h", "y", "z", "x", "c"), None), P(("z", "x", "c"), None)),
        check_vma=False,
    )
```

```python
import functools

import jax
import jax.numpy as jnp
from jax import lax
from jax.experimental import pallas as pl
from jax.experimental.pallas import tpu as pltpu
from jax.sharding import Mesh, PartitionSpec as P

ITERS = 3
SHARP = 48.0
EPSILON = 1e-06

AXES = ("z", "x", "c", "h", "y")
Z, X, C, H, Y = 8, 4, 2, 2, 4
BLOCKS = C * X
LANES = 128
PAD = 8


def exchange(blocks, axes):
    return lax.all_to_all(blocks, axes, 0, 0, tiled=True)


def spread(block, axes, count):
    return exchange(jnp.broadcast_to(block[None], (count,) + block.shape), axes)


def params():
    return pltpu.CompilerParams(vmem_limit_bytes=24 << 20)


def column_of(row):
    return jnp.broadcast_to(row, (LANES, row.shape[1])).T


def row_of(partial):
    return jnp.sum(partial.T, axis=0, keepdims=True)


def fold(product):
    total = product[:, :LANES]
    for start in range(LANES, product.shape[1], LANES):
        total = total + product[:, start : start + LANES]
    return total


def widen(column, width):
    return jnp.concatenate([column] * (width // LANES), axis=1)


def place(b):
    return (b % X) * C + b // X


def setup_kernel(latents_ref, codes_ref, tile_ref, rows_ref, scale_ref, total_ref):
    step = pl.program_id(0)
    latents = latents_ref[...]
    width = latents.shape[1]

    @pl.when(step == 0)
    def _():
        floats = latents.astype(jnp.float32)
        mean = jnp.sum(floats * floats, axis=1, keepdims=True) * (1.0 / width)
        scale_ref[...] = jnp.broadcast_to(lax.rsqrt(mean + EPSILON) * (SHARP / width), scale_ref.shape)
        total_ref[...] = jnp.zeros_like(total_ref)

    codes = codes_ref[...].reshape(-1, width)
    count = codes.shape[0]
    floats = codes.astype(jnp.float32)
    squares = floats * floats
    high = squares.astype(jnp.bfloat16)
    low = (squares - high.astype(jnp.float32)).astype(jnp.bfloat16)
    ones = jnp.ones((8, width), jnp.bfloat16)
    across = (((1,), (1,)), ((), ()))
    dot = functools.partial(lax.dot_general, dimension_numbers=across, preferred_element_type=jnp.float32)
    sums = dot(ones, high) + dot(ones, low)
    code_norm = lax.rsqrt(sums[:1] * (1.0 / width) + EPSILON)
    inner = dot(latents, codes)
    tile = jnp.exp(inner * widen(scale_ref[...], count) * code_norm)
    tile_ref[...] = tile
    total_ref[...] += fold(tile)

    @pl.when(step == pl.num_programs(0) - 1)
    def _():
        rows_ref[...] = jnp.broadcast_to(row_of(total_ref[...])[None], rows_ref.shape)


def rows_kernel(columns_ref, tile_ref, rows_ref, total_ref):
    step = pl.program_id(0)

    @pl.when(step == 0)
    def _():
        total_ref[...] = jnp.zeros_like(total_ref)

    total_ref[...] += fold(tile_ref[...] * columns_ref[...])

    @pl.when(step == pl.num_programs(0) - 1)
    def _():
        rows_ref[...] = jnp.broadcast_to(row_of(total_ref[...])[None], rows_ref.shape)


def row_scale_of(parts_ref):
    return column_of(1.0 / jnp.sum(parts_ref[...], axis=0))


def columns_kernel(parts_ref, tile_ref, columns_ref, scale_ref):
    @pl.when(pl.program_id(0) == 0)
    def _():
        scale_ref[...] = row_scale_of(parts_ref)

    tile = tile_ref[...]
    columns_ref[...] = jnp.sum(tile * widen(scale_ref[...], tile.shape[1]), axis=0, keepdims=True)


def targets_kernel(half_ref, parts_ref, latents_ref, tile_ref, *refs):
    added_ref, out_ref, scale_ref = refs if len(refs) == 3 else (None,) + refs

    @pl.when(pl.program_id(0) == 0)
    def _():
        scale_ref[...] = row_scale_of(parts_ref)

    tile = tile_ref[...]
    weighted = (tile * widen(scale_ref[...], tile.shape[1])).astype(jnp.bfloat16)
    summed = lax.dot_general(
        weighted, latents_ref[...], (((0,), (0,)), ((), ())), preferred_element_type=jnp.float32
    )
    out_ref[...] = summed if added_ref is None else summed + added_ref[...]


def final_kernel(parts_ref, columns_ref, codes_ref, tile_ref, out_ref, scale_ref, numer_ref, mass_ref):
    step = pl.program_id(0)

    @pl.when(step == 0)
    def _():
        scale_ref[...] = row_scale_of(parts_ref)
        numer_ref[...] = jnp.zeros_like(numer_ref)
        mass_ref[...] = jnp.zeros_like(mass_ref)

    tile = tile_ref[...]
    plan = (widen(scale_ref[...], tile.shape[1]) * tile * columns_ref[...]).astype(jnp.bfloat16)
    mass_ref[...] += fold(plan.astype(jnp.float32))
    codes = codes_ref[...].reshape(tile.shape[1], -1)
    numer_ref[...] += jnp.dot(plan, codes, preferred_element_type=jnp.float32)

    @pl.when(step == pl.num_programs(0) - 1)
    def _():
        tokens, width = numer_ref.shape
        group = tokens // Y
        mass = row_of(mass_ref[...])
        mass = jnp.concatenate([mass, jnp.zeros((1, 2 * width - tokens), jnp.float32)], axis=1)
        extra = jnp.concatenate(
            [mass[:, :width], mass[:, width:], jnp.zeros((PAD - 2, width), jnp.float32)], axis=0
        )
        for y in range(Y):
            out_ref[y, :group, :] = numer_ref[y * group : (y + 1) * group, :]
            out_ref[y, group:, :] = extra


def f32(*shape):
    return jax.ShapeDtypeStruct(shape, jnp.float32)


def whole(*shape):
    return pl.BlockSpec(shape, lambda *_: (0,) * len(shape))


def cost(flops, moved, exps=0):
    return pl.CostEstimate(flops=flops, bytes_accessed=moved, transcendentals=exps)


def per_device(latents, codebook):
    token_count, width = latents.shape
    code_count = codebook.shape[0]
    total_tokens = token_count * Z * X * C
    total_codes = code_count * H * Y
    share = code_count // (Z * X * C)
    block = code_count // BLOCKS
    size = token_count * code_count

    codes = codebook.reshape(Z, X * C, share, width)
    codes_spec = pl.BlockSpec((Z, None, share, width), lambda b: (0, place(b), 0, 0))
    latents_spec = whole(token_count, width)
    tile_spec = pl.BlockSpec((token_count, block), lambda b: (0, b))
    rows_spec = whole(H * Y, 1, token_count)
    columns_spec = pl.BlockSpec((None, 1, block), lambda b: (b, 0, 0))
    per_token = pltpu.VMEM((token_count, LANES), jnp.float32)
    rows_shape = f32(H * Y, 1, token_count)
    columns_shape = f32(BLOCKS, 1, block)

    tile, part = pl.pallas_call(
        setup_kernel,
        grid=(BLOCKS,),
        in_specs=[latents_spec, codes_spec],
        out_specs=[tile_spec, rows_spec],
        out_shape=[f32(token_count, code_count), rows_shape],
        scratch_shapes=[per_token, per_token],
        compiler_params=params(),
        cost_estimate=cost(2 * size * width, 4 * size, size),
        name="setup",
    )(latents, codes)

    def rows(columns):
        return pl.pallas_call(
            rows_kernel,
            grid=(BLOCKS,),
            in_specs=[columns_spec, tile_spec],
            out_specs=rows_spec,
            out_shape=rows_shape,
            scratch_shapes=[per_token],
            compiler_params=params(),
            cost_estimate=cost(2 * size, 4 * size),
            name="rows",
        )(columns, tile)

    def columns(parts):
        return pl.pallas_call(
            columns_kernel,
            grid=(BLOCKS,),
            in_specs=[rows_spec, tile_spec],
            out_specs=columns_spec,
            out_shape=columns_shape,
            scratch_shapes=[per_token],
            compiler_params=params(),
            cost_estimate=cost(2 * size, 4 * size),
            name="columns",
        )(parts, tile)

    def targets_part(half, parts, added=None):
        spec = pl.BlockSpec((block, width), lambda i, half: (i, 0))
        more, more_specs = ((), ()) if added is None else ((added,), (spec,))
        return pl.pallas_call(
            targets_kernel,
            grid_spec=pltpu.PrefetchScalarGridSpec(
                num_scalar_prefetch=1,
                grid=(X,),
                in_specs=[
                    rows_spec,
                    latents_spec,
                    pl.BlockSpec((token_count, block), lambda i, half: (0, half[0] * X + i)),
                    *more_specs,
                ],
                out_specs=spec,
                scratch_shapes=[per_token],
            ),
            out_shape=f32(X * block, width),
            compiler_params=params(),
            cost_estimate=cost(size * width, 4 * size),
            name="targets" if added is None else "targets_added",
        )(half, parts, latents, tile, *more)

    for sweep_index in range(ITERS):
        parts = exchange(part, ("h", "y"))
        sums = jnp.sum(exchange(columns(parts), ("c", "x")), axis=0)
        total = jnp.sum(spread(sums, "z", Z), axis=0)
        mine = total_tokens / total_codes / total
        col_scale = spread(mine, ("c", "x"), BLOCKS)
        if sweep_index < ITERS - 1:
            part = rows(col_scale)

    core = lax.axis_index("c").reshape(1)
    sent = targets_part(1 - core, parts)
    summed = targets_part(core, parts, lax.ppermute(sent, "c", [(0, 1), (1, 0)]))
    summed = jnp.sum(exchange(summed.reshape(X, block, width), "x"), axis=0)
    summed = jnp.sum(exchange(summed.reshape(Z, share, width), "z"), axis=0)
    own = lax.dynamic_slice(mine, (0, lax.axis_index("z") * share), (1, share))[0]
    targets = summed * (own * (total_codes / total_tokens))[:, None]

    group = token_count // Y
    packed = pl.pallas_call(
        final_kernel,
        grid=(BLOCKS,),
        in_specs=[rows_spec, columns_spec, codes_spec, tile_spec],
        out_specs=whole(Y, group + PAD, width),
        out_shape=f32(Y, group + PAD, width),
        scratch_shapes=[per_token, pltpu.VMEM((token_count, width), jnp.float32), per_token],
        compiler_params=params(),
        cost_estimate=cost(2 * size * width, 4 * size),
        name="final",
    )(parts, col_scale, codes, tile)
    packed = jnp.sum(exchange(packed, "y"), axis=0)
    packed = packed + lax.ppermute(packed, "h", [(0, 1), (1, 0)])
    mass = packed[group : group + 2].reshape(2 * width)[:token_count]
    rebuilt = spread(packed[:group], "y", Y).reshape(token_count, width) / mass[:, None]
    return (targets, rebuilt)


def solution(mesh):
    fine = Mesh(mesh.devices.reshape(Z, X, C, H, Y), AXES)
    return jax.shard_map(
        per_device,
        mesh=fine,
        in_specs=(P(("z", "x", "c"), None), P(("h", "y"), None)),
        out_specs=(P(("h", "y", "z", "x", "c"), None), P(("z", "x", "c"), None)),
        check_vma=False,
    )
```

```python
import functools

import jax
import jax.numpy as jnp
from jax import lax
from jax.experimental import pallas as pl
from jax.experimental.pallas import tpu as pltpu
from jax.sharding import Mesh, PartitionSpec as P

ITERS = 3
SHARP = 48.0
EPSILON = 1e-06

AXES = ("z", "x", "c", "h", "y")
Z, X, C, H, Y = 8, 4, 2, 2, 4
BLOCKS = C * X
LANES = 128
PAD = 8


def exchange(blocks, axes):
    return lax.all_to_all(blocks, axes, 0, 0, tiled=True)


def params(mib=8):
    return pltpu.CompilerParams(vmem_limit_bytes=mib << 20)


def column_of(row):
    return jnp.broadcast_to(row, (LANES, row.shape[1])).T


def row_of(partial):
    return jnp.sum(partial.T, axis=0, keepdims=True)


def fold(product):
    total = product[:, :LANES]
    for start in range(LANES, product.shape[1], LANES):
        total = total + product[:, start : start + LANES]
    return total


def widen(column, width):
    return jnp.concatenate([column] * (width // LANES), axis=1)


def place(b):
    return (b % X) * C + b // X


def setup_kernel(where_ref, latents_ref, codes_ref, tile_ref, rows_ref, scale_ref, total_ref):
    step = pl.program_id(0)
    latents = latents_ref[...]
    width = latents.shape[1]

    @pl.when(step == 0)
    def _():
        floats = latents.astype(jnp.float32)
        mean = jnp.sum(floats * floats, axis=1, keepdims=True) * (1.0 / width)
        scale_ref[...] = jnp.broadcast_to(lax.rsqrt(mean + EPSILON) * (SHARP / width), scale_ref.shape)
        total_ref[...] = jnp.zeros_like(total_ref)

    codes = codes_ref[...].reshape(-1, width)
    count = codes.shape[0]
    floats = codes.astype(jnp.float32)
    squares = floats * floats
    high = squares.astype(jnp.bfloat16)
    low = (squares - high.astype(jnp.float32)).astype(jnp.bfloat16)
    ones = jnp.ones((8, width), jnp.bfloat16)
    across = (((1,), (1,)), ((), ()))
    dot = functools.partial(lax.dot_general, dimension_numbers=across, preferred_element_type=jnp.float32)
    sums = dot(ones, high) + dot(ones, low)
    code_norm = lax.rsqrt(sums[:1] * (1.0 / width) + EPSILON)
    inner = dot(latents, codes)
    tile = jnp.exp(inner * widen(scale_ref[...], count) * code_norm)
    tile_ref[...] = tile
    total_ref[...] += fold(tile)

    @pl.when(step == pl.num_programs(0) - 1)
    def _():
        rows_ref[...] = jnp.broadcast_to(row_of(total_ref[...])[None], rows_ref.shape)


def rows_kernel(columns_ref, tile_ref, rows_ref, total_ref):
    step = pl.program_id(0)

    @pl.when(step == 0)
    def _():
        total_ref[...] = jnp.zeros_like(total_ref)

    total_ref[...] += fold(tile_ref[...] * columns_ref[...])

    @pl.when(step == pl.num_programs(0) - 1)
    def _():
        rows_ref[...] = jnp.broadcast_to(row_of(total_ref[...])[None], rows_ref.shape)


def row_scale_of(parts_ref):
    return column_of(1.0 / jnp.sum(parts_ref[...], axis=0))


def columns_kernel(parts_ref, tile_ref, columns_ref, scale_ref):
    @pl.when(pl.program_id(0) == 0)
    def _():
        scale_ref[...] = row_scale_of(parts_ref)

    tile = tile_ref[...]
    columns_ref[...] = jnp.sum(tile * widen(scale_ref[...], tile.shape[1]), axis=0, keepdims=True)


def targets_part(parts_ref, latents_ref, tile_ref, scale_ref):
    @pl.when(pl.program_id(0) == 0)
    def _():
        scale_ref[...] = row_scale_of(parts_ref)

    tile = tile_ref[...]
    weighted = (tile * widen(scale_ref[...], tile.shape[1])).astype(jnp.bfloat16)
    return lax.dot_general(
        latents_ref[...], weighted, (((0,), (0,)), ((), ())), preferred_element_type=jnp.float32
    )


def targets_sent_kernel(where_ref, parts_ref, latents_ref, tile_ref, after_ref, out_ref, scale_ref):
    del where_ref, after_ref
    out_ref[...] = targets_part(parts_ref, latents_ref, tile_ref, scale_ref)


def targets_kept_kernel(
    where_ref, parts_ref, latents_ref, tile_ref, after_ref, added_ref, one_ref, two_ref, own_one_ref, own_two_ref, scale_ref
):
    del where_ref, after_ref
    slot = pl.program_id(0)
    summed = targets_part(parts_ref, latents_ref, tile_ref, scale_ref) + added_ref[...]
    upper, lower = jnp.split(summed, 2, axis=0)

    def put(ref, index, value, when):
        @pl.when(slot == when)
        def _():
            ref[index] = value

    put(own_one_ref, 0, upper, 0)
    put(one_ref, 0, upper, 1)
    put(one_ref, 1, upper, 2)
    put(own_one_ref, 1, upper, 3)
    put(own_two_ref, 0, lower, 0)
    put(own_two_ref, 1, lower, 1)
    put(two_ref, 1, lower, 2)
    put(two_ref, 0, lower, 3)


def sum_kernel(parts_ref, *refs):
    out_ref = refs[-1]
    out_ref[...] = jnp.broadcast_to(jnp.sum(parts_ref[...], axis=0, keepdims=True), out_ref.shape)


def inverse_kernel(factor, parts_ref, *refs):
    out_ref = refs[-1]
    out_ref[...] = jnp.broadcast_to(factor / jnp.sum(parts_ref[...], axis=0, keepdims=True), out_ref.shape)


def add_kernel(kept_ref, came_ref, after_ref, out_ref):
    del after_ref
    out_ref[...] = kept_ref[...] + came_ref[...]


def join_kernel(kept_ref, came_ref, spread_ref, mass_ref):
    total = kept_ref[...] + came_ref[...]
    group = spread_ref.shape[1]
    spread_ref[...] = jnp.broadcast_to(total[None, :group], spread_ref.shape)
    mass_ref[...] = total[group:]


def turn_kernel(where_ref, own_one_ref, one_ref, more_one_ref, own_two_ref, two_ref, more_two_ref, after_ref, *refs):
    del after_ref
    send_ref, keep_ref, turned_ref = refs
    upper = own_one_ref[0] + one_ref[0] + more_one_ref[...]
    lower = own_two_ref[0] + two_ref[0] + more_two_ref[...]
    turned_ref[...] = jnp.concatenate([upper, lower], axis=0).T
    share = send_ref.shape[1]
    for i, slot in enumerate((0, 4, 2, 6)):
        for ref, s in ((keep_ref, slot), (send_ref, slot + 1)):
            start = pl.multiple_of((where_ref[2] ^ s) * share, share)
            ref[i] = turned_ref[pl.ds(start, share), :]


def final_kernel(parts_ref, columns_ref, codes_ref, tile_ref, out_ref, scale_ref, numer_ref, mass_ref):
    step = pl.program_id(0)

    @pl.when(step == 0)
    def _():
        scale_ref[...] = row_scale_of(parts_ref)
        numer_ref[...] = jnp.zeros_like(numer_ref)
        mass_ref[...] = jnp.zeros_like(mass_ref)

    tile = tile_ref[...]
    plan = (widen(scale_ref[...], tile.shape[1]) * tile * columns_ref[...]).astype(jnp.bfloat16)
    mass_ref[...] += fold(plan.astype(jnp.float32))
    codes = codes_ref[...].reshape(tile.shape[1], -1)
    numer_ref[...] += jnp.dot(plan, codes, preferred_element_type=jnp.float32)

    @pl.when(step == pl.num_programs(0) - 1)
    def _():
        tokens, width = numer_ref.shape
        group = tokens // Y
        mass = row_of(mass_ref[...])
        mass = jnp.concatenate([mass, jnp.zeros((1, 2 * width - tokens), jnp.float32)], axis=1)
        extra = jnp.concatenate(
            [mass[:, :width], mass[:, width:], jnp.zeros((PAD - 2, width), jnp.float32)], axis=0
        )
        for y in range(Y):
            out_ref[y, :group, :] = numer_ref[y * group : (y + 1) * group, :]
            out_ref[y, group:, :] = extra


def f32(*shape):
    return jax.ShapeDtypeStruct(shape, jnp.float32)


def whole(*shape):
    return pl.BlockSpec(shape, lambda *_: (0,) * len(shape))


def cost(flops, moved, exps=0):
    return pl.CostEstimate(flops=flops, bytes_accessed=moved, transcendentals=exps)


def per_device(latents, codebook):
    token_count, width = latents.shape
    code_count = codebook.shape[0]
    total_tokens = token_count * Z * X * C
    total_codes = code_count * H * Y
    share = code_count // (Z * X * C)
    block = code_count // BLOCKS
    size = token_count * code_count

    codes = codebook.reshape(Z, X * C, share, width)
    codes_spec = pl.BlockSpec((Z, None, share, width), lambda b: (0, place(b), 0, 0))
    latents_spec = whole(token_count, width)
    tile_spec = pl.BlockSpec((None, token_count, block), lambda b: (b, 0, 0))
    rows_spec = whole(H * Y, 1, token_count)
    columns_spec = pl.BlockSpec((None, 1, block), lambda b: (b, 0, 0))
    per_token = pltpu.VMEM((token_count, LANES), jnp.float32)
    rows_shape = f32(H * Y, 1, token_count)
    columns_shape = f32(BLOCKS, 1, block)

    core, x, z = (lax.axis_index(axis) for axis in ("c", "x", "z"))
    where = jnp.stack([core, x, z, 1 - core, z * share])

    tile, part = pl.pallas_call(
        setup_kernel,
        grid=(BLOCKS,),
        in_specs=[pl.BlockSpec(memory_space=pltpu.SMEM), latents_spec, codes_spec],
        out_specs=[tile_spec, rows_spec],
        out_shape=[f32(BLOCKS, token_count, block), rows_shape],
        scratch_shapes=[per_token, per_token],
        compiler_params=params(16),
        cost_estimate=cost(2 * size * width, 4 * size, size),
        name="setup",
    )(where, latents, codes)

    def rows(columns):
        return pl.pallas_call(
            rows_kernel,
            grid=(BLOCKS,),
            in_specs=[columns_spec, tile_spec],
            out_specs=rows_spec,
            out_shape=rows_shape,
            scratch_shapes=[per_token],
            compiler_params=params(),
            cost_estimate=cost(2 * size, 4 * size),
            name="rows",
        )(columns, tile)

    def columns(parts):
        return pl.pallas_call(
            columns_kernel,
            grid=(BLOCKS,),
            in_specs=[rows_spec, tile_spec],
            out_specs=columns_spec,
            out_shape=columns_shape,
            scratch_shapes=[per_token],
            compiler_params=params(),
            cost_estimate=cost(2 * size, 4 * size),
            name="columns",
        )(parts, tile)

    anywhere = pl.BlockSpec(memory_space=pl.ANY)

    def targets_spec(kept):
        spec = pl.BlockSpec((None, width, block), lambda i, where: (i, 0, 0))
        halves = whole(2, width // 2, block)
        return pltpu.PrefetchScalarGridSpec(
            num_scalar_prefetch=1,
            grid=(X,),
            in_specs=[
                rows_spec,
                latents_spec,
                pl.BlockSpec((None, token_count, block), lambda i, where: (where[0 if kept else 3] * X + (where[1] ^ i), 0, 0)),
                anywhere,
                *([spec] if kept else []),
            ],
            out_specs=[halves] * 4 if kept else spec,
            scratch_shapes=[per_token],
        )

    def targets_sent(where, parts, after):
        return pl.pallas_call(
            targets_sent_kernel,
            grid_spec=targets_spec(False),
            out_shape=f32(X, width, block),
            compiler_params=params(),
            cost_estimate=cost(size * width, 4 * size),
            name="targets_sent",
        )(where, parts, latents, tile, after)

    def targets_kept(where, parts, after, added):
        return pl.pallas_call(
            targets_kept_kernel,
            grid_spec=targets_spec(True),
            out_shape=[f32(2, width // 2, block)] * 4,
            compiler_params=params(16),
            cost_estimate=cost(size * width, 4 * size),
            name="targets_kept",
        )(where, parts, latents, tile, after, added)

    def small(kernel, name, count, parts, *after):
        return pl.pallas_call(
            kernel,
            in_specs=[pl.BlockSpec(memory_space=pltpu.VMEM)] + [anywhere] * len(after),
            out_specs=pl.BlockSpec(memory_space=pltpu.VMEM),
            out_shape=f32(count, 1, block),
            compiler_params=params(),
            cost_estimate=cost(parts.size, 4 * parts.size),
            name=name,
        )(parts, *after)

    inverse = functools.partial(inverse_kernel, total_tokens / total_codes)
    def swap(value, axis, count, bits):
        return lax.ppermute(value, axis, [(i, i ^ bits) for i in range(count)])

    def add(kept, came, after):
        return pl.pallas_call(
            add_kernel,
            in_specs=[pl.BlockSpec(memory_space=pltpu.VMEM)] * 2 + [anywhere],
            out_specs=pl.BlockSpec(memory_space=pltpu.VMEM),
            out_shape=f32(*kept.shape),
            compiler_params=params(),
            cost_estimate=cost(kept.size, 12 * kept.size),
            name="add",
        )(kept, came, after)

    for sweep_index in range(ITERS):
        last = sweep_index == ITERS - 1
        parts = exchange(part, ("h", "y"))
        column_sums = columns(parts)
        if last:
            sent = targets_sent(where, parts, column_sums)
        after = (sent,) if last else ()
        sums = small(sum_kernel, "sums", Z, exchange(column_sums, ("c", "x")), *after)
        if last:
            kept = targets_kept(where, parts, sums, swap(sent, "c", C, 1))
        after = (kept[0],) if last else ()
        mine = small(inverse, "inverse", BLOCKS, exchange(sums, "z"), *after)
        col_scale = exchange(mine, ("c", "x"))
        if not last:
            part = rows(col_scale)

    one, two, own_one, own_two = kept
    one, two = swap(one, "x", X, 1), swap(two, "x", X, 3)
    more_one = swap(own_one[1] + one[1], "x", X, 3)
    more_two = swap(own_two[1] + two[1], "x", X, 1)

    group = token_count // Y
    packed = pl.pallas_call(
        final_kernel,
        grid=(BLOCKS,),
        in_specs=[rows_spec, columns_spec, codes_spec, tile_spec],
        out_specs=whole(Y, group + PAD, width),
        out_shape=f32(Y, group + PAD, width),
        scratch_shapes=[per_token, pltpu.VMEM((token_count, width), jnp.float32), per_token],
        compiler_params=params(16),
        cost_estimate=cost(20 * size * width, 4 * size),
        name="final",
    )(parts, col_scale, codes, tile)
    packed = jnp.sum(exchange(packed, "y"), axis=0)
    vmem = pl.BlockSpec(memory_space=pltpu.VMEM)
    away, near = pl.pallas_call(
        turn_kernel,
        in_specs=[pl.BlockSpec(memory_space=pltpu.SMEM)] + [vmem] * 6 + [anywhere],
        out_specs=[vmem] * 2,
        out_shape=[f32(Z // 2, share, width)] * 2,
        scratch_shapes=[pltpu.VMEM((block, width), jnp.float32)],
        compiler_params=params(16),
        cost_estimate=cost(3 * block * width, 12 * block * width),
        name="turn",
    )(where, own_one, one, more_one, own_two, two, more_two, packed)
    numer, mass = pl.pallas_call(
        join_kernel,
        in_specs=[vmem] * 2,
        out_specs=[vmem] * 2,
        out_shape=[f32(Y, group, width), f32(PAD, width)],
        compiler_params=params(),
        cost_estimate=cost(20000 * token_count * width, 8 * token_count * width),
        name="join",
    )(packed, swap(packed, "h", H, 1))
    near = near + swap(away, "z", Z, 1)
    near = add(near[:2], swap(near[2:], "z", Z, 2), mass)
    summed = near[0] + swap(near[1], "z", Z, 4)
    own = lax.dynamic_slice(mine, (0, 0, where[4]), (1, 1, share)).reshape(share)
    targets = summed * (own * (total_codes / total_tokens))[:, None]
    mass = mass[:2].reshape(2 * width)[:token_count]
    rebuilt = exchange(numer, "y").reshape(token_count, width) / mass[:, None]
    return (targets, rebuilt)


def solution(mesh):
    fine = Mesh(mesh.devices.reshape(Z, X, C, H, Y), AXES)
    return jax.shard_map(
        per_device,
        mesh=fine,
        in_specs=(P(("z", "x", "c"), None), P(("h", "y"), None)),
        out_specs=(P(("h", "y", "z", "x", "c"), None), P(("z", "x", "c"), None)),
        check_vma=False,
    )
```

```python
import functools

import jax
import jax.numpy as jnp
from jax import lax
from jax.experimental import pallas as pl
from jax.experimental.pallas import tpu as pltpu
from jax.sharding import Mesh, PartitionSpec as P

ITERS = 3
SHARP = 48.0
EPSILON = 1e-06

AXES = ("z", "x", "c", "h", "y")
Z, X, C, H, Y = 8, 4, 2, 2, 4
BLOCKS = C * X
LANES = 128
PAD = 8


def exchange(blocks, axes):
    return lax.all_to_all(blocks, axes, 0, 0, tiled=True)


FETCHES = 55_500_000
FETCHES_BESIDE_TILE = 40_000_000


def params(limit=8 << 20):
    return pltpu.CompilerParams(vmem_limit_bytes=limit)


def column_of(row):
    return jnp.broadcast_to(row, (LANES, row.shape[1])).T


def row_of(partial):
    return jnp.sum(partial.T, axis=0, keepdims=True)


def fold(product):
    total = product[:, :LANES]
    for start in range(LANES, product.shape[1], LANES):
        total = total + product[:, start : start + LANES]
    return total


def widen(column, width):
    return jnp.concatenate([column] * (width // LANES), axis=1)


def place(b):
    return (b % X) * C + b // X


def fetch(pairs, sems):
    copies = [pltpu.make_async_copy(source, target, sems.at[i]) for i, (source, target) in enumerate(pairs)]
    for copy in copies:
        copy.start()
    return copies


def setup_kernel(where_ref, latents_ref, codes_ref, tile_ref, rows_ref, far_ref, tokens_ref, held_ref, sems):
    del where_ref
    pairs = [(codes_ref.at[:, place(b)], held_ref.at[b]) for b in range(BLOCKS)]
    *copies, first = fetch(pairs + [(latents_ref, tokens_ref)], sems)
    first.wait()
    saves = []
    latents = tokens_ref[...]
    width = latents.shape[1]
    floats = latents.astype(jnp.float32)
    mean = jnp.sum(floats * floats, axis=1, keepdims=True) * (1.0 / width)
    scale = jnp.broadcast_to(lax.rsqrt(mean + EPSILON) * (SHARP / width), (latents.shape[0], LANES))
    total = jnp.zeros(scale.shape, jnp.float32)
    across = (((1,), (1,)), ((), ()))
    for b in range(BLOCKS):
        copies[b].wait()
        codes = held_ref[b].reshape(-1, width)
        floats = codes.astype(jnp.float32)
        code_norm = lax.rsqrt(row_of(fold(floats * floats)) * (1.0 / width) + EPSILON)
        inner = lax.dot_general(latents, codes, across, preferred_element_type=jnp.float32)
        tile = jnp.exp(inner * widen(scale, codes.shape[0]) * code_norm)
        tile_ref[b] = tile
        saves.append(pltpu.make_async_copy(tile_ref.at[b], far_ref.at[b], sems.at[BLOCKS + 1 + b]))
        saves[b].start()
        total += fold(tile)
    rows_ref[...] = jnp.broadcast_to(row_of(total)[None], rows_ref.shape)
    for save in saves:
        save.wait()


def rows_kernel(columns_ref, tile_ref, rows_ref, total_ref):
    step = pl.program_id(0)

    @pl.when(step == 0)
    def _():
        total_ref[...] = jnp.zeros_like(total_ref)

    total_ref[...] += fold(tile_ref[...] * columns_ref[...])

    @pl.when(step == pl.num_programs(0) - 1)
    def _():
        rows_ref[...] = jnp.broadcast_to(row_of(total_ref[...])[None], rows_ref.shape)


def row_scale_of(parts_ref):
    return column_of(1.0 / jnp.sum(parts_ref[...], axis=0))


def columns_kernel(parts_ref, tile_ref, columns_ref, scale_ref):
    @pl.when(pl.program_id(0) == 0)
    def _():
        scale_ref[...] = row_scale_of(parts_ref)

    tile = tile_ref[...]
    columns_ref[...] = jnp.sum(tile * widen(scale_ref[...], tile.shape[1]), axis=0, keepdims=True)


def targets_part(tile, scale, latents):
    weighted = (tile * widen(scale, tile.shape[1])).astype(jnp.bfloat16)
    return lax.dot_general(latents, weighted, (((0,), (0,)), ((), ())), preferred_element_type=jnp.float32)


def targets_sent_kernel(where_ref, parts_ref, latents_ref, tile_ref, after_ref, out_ref, tiles_ref, sems):
    del after_ref
    pairs = [(tile_ref.at[where_ref[3] * X + (where_ref[1] ^ s)], tiles_ref.at[s]) for s in range(X)]
    copies = fetch(pairs, sems)
    scale = row_scale_of(parts_ref)
    latents = latents_ref[...]
    for s in range(X):
        copies[s].wait()
        out_ref[s] = targets_part(tiles_ref[s], scale, latents)


def targets_kept_kernel(
    where_ref, parts_ref, latents_ref, tile_ref, added_ref, after_ref,
    one_ref, two_ref, own_one_ref, own_two_ref, tiles_ref, more_ref, sems,
):
    del after_ref
    pairs = [(tile_ref.at[where_ref[0] * X + (where_ref[1] ^ s)], tiles_ref.at[s]) for s in range(X)]
    pairs += [(added_ref.at[s], more_ref.at[s]) for s in range(X)]
    copies = fetch([pairs[i] for s in range(X) for i in (s, s + X)], sems)
    scale = row_scale_of(parts_ref)
    latents = latents_ref[...]
    for s in range(X):
        copies[2 * s].wait()
        summed = targets_part(tiles_ref[s], scale, latents)
        copies[2 * s + 1].wait()
        summed += more_ref[s]
        upper, lower = jnp.split(summed, 2, axis=0)
        ref, index = ((own_one_ref, 0), (one_ref, 0), (one_ref, 1), (own_one_ref, 1))[s]
        ref[index] = upper
        ref, index = ((own_two_ref, 0), (own_two_ref, 1), (two_ref, 1), (two_ref, 0))[s]
        ref[index] = lower


def sum_kernel(parts_ref, *refs):
    out_ref = refs[-1]
    out_ref[...] = jnp.broadcast_to(jnp.sum(parts_ref[...], axis=0, keepdims=True), out_ref.shape)


def inverse_kernel(factor, parts_ref, *refs):
    out_ref = refs[-1]
    out_ref[...] = jnp.broadcast_to(factor / jnp.sum(parts_ref[...], axis=0, keepdims=True), out_ref.shape)


def add_kernel(kept_ref, came_ref, after_ref, out_ref):
    del after_ref
    out_ref[...] = kept_ref[...] + came_ref[...]


def join_kernel(kept_ref, came_ref, spread_ref, mass_ref):
    total = kept_ref[...] + came_ref[...]
    group = spread_ref.shape[1]
    spread_ref[...] = jnp.broadcast_to(total[None, :group], spread_ref.shape)
    mass_ref[...] = total[group:]


def turn_kernel(where_ref, own_one_ref, one_ref, more_one_ref, own_two_ref, two_ref, more_two_ref, after_ref, *refs):
    del after_ref
    send_ref, keep_ref, turned_ref = refs
    upper = own_one_ref[0] + one_ref[0] + more_one_ref[...]
    lower = own_two_ref[0] + two_ref[0] + more_two_ref[...]
    turned_ref[...] = jnp.concatenate([upper, lower], axis=0).T
    share = send_ref.shape[1]
    for i, slot in enumerate((0, 4, 2, 6)):
        for ref, s in ((keep_ref, slot), (send_ref, slot + 1)):
            start = pl.multiple_of((where_ref[2] ^ s) * share, share)
            ref[i] = turned_ref[pl.ds(start, share), :]


def final_kernel(
    parts_ref, columns_ref, codes_ref, tile_ref, out_ref, held_ref, tiles_ref, numer_ref, sems
):
    pairs = [
        pair
        for b in range(BLOCKS)
        for pair in ((tile_ref.at[b], tiles_ref.at[b]), (codes_ref.at[:, place(b)], held_ref.at[b]))
    ]
    copies = fetch(pairs, sems)
    tokens, width = numer_ref.shape
    scale = row_scale_of(parts_ref)
    total = jnp.zeros(scale.shape, jnp.float32)
    for b in range(BLOCKS):
        copies[2 * b].wait()
        tile = tiles_ref[b]
        plan = (widen(scale, tile.shape[1]) * tile * columns_ref[b]).astype(jnp.bfloat16)
        total += fold(plan.astype(jnp.float32))
        copies[2 * b + 1].wait()
        part = jnp.dot(plan, held_ref[b].reshape(-1, width), preferred_element_type=jnp.float32)
        numer_ref[...] = part if b == 0 else numer_ref[...] + part
    group = tokens // Y
    mass = row_of(total)
    mass = jnp.concatenate([mass, jnp.zeros((1, 2 * width - tokens), jnp.float32)], axis=1)
    extra = jnp.concatenate(
        [mass[:, :width], mass[:, width:], jnp.zeros((PAD - 2, width), jnp.float32)], axis=0
    )
    for y in range(Y):
        out_ref[y, :group, :] = numer_ref[y * group : (y + 1) * group, :]
        out_ref[y, group:, :] = extra


def f32(*shape):
    return jax.ShapeDtypeStruct(shape, jnp.float32)


def whole(*shape):
    return pl.BlockSpec(shape, lambda *_: (0,) * len(shape))


def cost(flops, moved, exps=0):
    return pl.CostEstimate(flops=flops, bytes_accessed=moved, transcendentals=exps)


def per_device(latents, codebook):
    token_count, width = latents.shape
    code_count = codebook.shape[0]
    total_tokens = token_count * Z * X * C
    total_codes = code_count * H * Y
    share = code_count // (Z * X * C)
    block = code_count // BLOCKS
    size = token_count * code_count

    codes = codebook.reshape(Z, X * C, share, width)
    tile_spec = pl.BlockSpec((None, token_count, block), lambda b: (b, 0, 0))
    rows_spec = whole(H * Y, 1, token_count)
    columns_spec = pl.BlockSpec((None, 1, block), lambda b: (b, 0, 0))
    vmem = pl.BlockSpec(memory_space=pltpu.VMEM)
    smem = pl.BlockSpec(memory_space=pltpu.SMEM)
    hbm = pl.BlockSpec(memory_space=pltpu.HBM)
    anywhere = pl.BlockSpec(memory_space=pl.ANY)
    per_token = pltpu.VMEM((token_count, LANES), jnp.float32)
    held = pltpu.VMEM((BLOCKS, Z, share, width), jnp.bfloat16)
    tiles = functools.partial(pltpu.VMEM, dtype=jnp.float32)
    rows_shape = f32(H * Y, 1, token_count)
    columns_shape = f32(BLOCKS, 1, block)

    core, x, z = (lax.axis_index(axis) for axis in ("c", "x", "z"))
    where = jnp.stack([core, x, z, 1 - core, z * share])

    tile, part, far = pl.pallas_call(
        setup_kernel,
        in_specs=[smem, hbm, hbm],
        out_specs=[vmem, vmem, hbm],
        out_shape=[f32(BLOCKS, token_count, block), rows_shape, f32(BLOCKS, token_count, block)],
        scratch_shapes=[
            pltpu.VMEM((token_count, width), jnp.bfloat16),
            held,
            pltpu.SemaphoreType.DMA((2 * BLOCKS + 1,)),
        ],
        compiler_params=params(FETCHES_BESIDE_TILE),
        cost_estimate=cost(2 * size * width, 4 * size, size),
        name="setup",
    )(where, latents, codes)

    def rows(columns):
        return pl.pallas_call(
            rows_kernel,
            grid=(BLOCKS,),
            in_specs=[columns_spec, tile_spec],
            out_specs=rows_spec,
            out_shape=rows_shape,
            scratch_shapes=[per_token],
            compiler_params=params(),
            cost_estimate=cost(2 * size, 4 * size),
            name="rows",
        )(columns, tile)

    def columns(parts):
        return pl.pallas_call(
            columns_kernel,
            grid=(BLOCKS,),
            in_specs=[rows_spec, tile_spec],
            out_specs=columns_spec,
            out_shape=columns_shape,
            scratch_shapes=[per_token],
            compiler_params=params(),
            cost_estimate=cost(2 * size, 4 * size),
            name="columns",
        )(parts, tile)

    def targets_sent(parts, after):
        return pl.pallas_call(
            targets_sent_kernel,
            in_specs=[smem, vmem, vmem, hbm, anywhere],
            out_specs=vmem,
            out_shape=f32(X, width, block),
            scratch_shapes=[tiles((X, token_count, block)), pltpu.SemaphoreType.DMA((X,))],
            compiler_params=params(FETCHES),
            cost_estimate=cost(size * width, 4 * size),
            name="targets_sent",
        )(where, parts, latents, far, after)

    def targets_kept(parts, added, after):
        return pl.pallas_call(
            targets_kept_kernel,
            in_specs=[smem, vmem, vmem, hbm, hbm, anywhere],
            out_specs=[vmem] * 4,
            out_shape=[f32(2, width // 2, block)] * 4,
            scratch_shapes=[
                tiles((X, token_count, block)),
                tiles((X, width, block)),
                pltpu.SemaphoreType.DMA((2 * X,)),
            ],
            compiler_params=params(FETCHES),
            cost_estimate=cost(size * width, 4 * size),
            name="targets_kept",
        )(where, parts, latents, far, added, after)

    def small(kernel, name, count, weight, parts, *after):
        return pl.pallas_call(
            kernel,
            in_specs=[vmem] + [anywhere] * len(after),
            out_specs=vmem,
            out_shape=f32(count, 1, block),
            compiler_params=params(),
            cost_estimate=cost(weight * parts.size, 4 * parts.size),
            name=name,
        )(parts, *after)

    inverse = functools.partial(inverse_kernel, total_tokens / total_codes)
    def swap(value, axis, count, bits):
        return lax.ppermute(value, axis, [(i, i ^ bits) for i in range(count)])

    def add(kept, came, after):
        return pl.pallas_call(
            add_kernel,
            in_specs=[vmem] * 2 + [anywhere],
            out_specs=vmem,
            out_shape=f32(*kept.shape),
            compiler_params=params(),
            cost_estimate=cost(kept.size, 12 * kept.size),
            name="add",
        )(kept, came, after)

    for sweep_index in range(ITERS):
        last = sweep_index == ITERS - 1
        parts = exchange(part, ("h", "y"))
        column_sums = columns(parts)
        if last:
            sent = targets_sent(parts, column_sums)
        sums = small(sum_kernel, "sums", Z, 20_000_000 if last else 1, exchange(column_sums, ("c", "x")))
        if last:
            kept = targets_kept(parts, swap(sent, "c", C, 1), sums)
        after = (kept[0],) if last else ()
        mine = small(inverse, "inverse", BLOCKS, 1, exchange(sums, "z"), *after)
        col_scale = exchange(mine, ("c", "x"))
        if not last:
            part = rows(col_scale)

    one, two, own_one, own_two = kept
    one, two = swap(one, "x", X, 1), swap(two, "x", X, 3)
    more_one = swap(own_one[1] + one[1], "x", X, 3)
    more_two = swap(own_two[1] + two[1], "x", X, 1)

    group = token_count // Y
    packed = pl.pallas_call(
        final_kernel,
        in_specs=[vmem, vmem, hbm, hbm],
        out_specs=vmem,
        out_shape=f32(Y, group + PAD, width),
        scratch_shapes=[
            held,
            tiles((BLOCKS, token_count, block)),
            tiles((token_count, width)),
            pltpu.SemaphoreType.DMA((2 * BLOCKS,)),
        ],
        compiler_params=params(FETCHES),
        cost_estimate=cost(13 * size * width, 4 * size),
        name="final",
    )(parts, col_scale, codes, far)
    packed = jnp.sum(exchange(packed, "y"), axis=0)
    away, near = pl.pallas_call(
        turn_kernel,
        in_specs=[smem] + [vmem] * 6 + [anywhere],
        out_specs=[vmem] * 2,
        out_shape=[f32(Z // 2, share, width)] * 2,
        scratch_shapes=[pltpu.VMEM((block, width), jnp.float32)],
        compiler_params=params(16 << 20),
        cost_estimate=cost(3 * block * width, 12 * block * width),
        name="turn",
    )(where, own_one, one, more_one, own_two, two, more_two, packed)
    numer, mass = pl.pallas_call(
        join_kernel,
        in_specs=[vmem] * 2,
        out_specs=[vmem] * 2,
        out_shape=[f32(Y, group, width), f32(PAD, width)],
        compiler_params=params(),
        cost_estimate=cost(20000 * token_count * width, 8 * token_count * width),
        name="join",
    )(packed, swap(packed, "h", H, 1))
    near = near + swap(away, "z", Z, 1)
    near = add(near[:2], swap(near[2:], "z", Z, 2), mass)
    summed = near[0] + swap(near[1], "z", Z, 4)
    own = lax.dynamic_slice(mine, (0, 0, where[4]), (1, 1, share)).reshape(share)
    targets = summed * (own * (total_codes / total_tokens))[:, None]
    mass = mass[:2].reshape(2 * width)[:token_count]
    rebuilt = exchange(numer, "y").reshape(token_count, width) / mass[:, None]
    return (targets, rebuilt)


def solution(mesh):
    fine = Mesh(mesh.devices.reshape(Z, X, C, H, Y), AXES)
    return jax.shard_map(
        per_device,
        mesh=fine,
        in_specs=(P(("z", "x", "c"), None), P(("h", "y"), None)),
        out_specs=(P(("h", "y", "z", "x", "c"), None), P(("z", "x", "c"), None)),
        check_vma=False,
    )
```

```python
import functools

import jax
import jax.numpy as jnp
from jax import lax
from jax.experimental import pallas as pl
from jax.experimental.pallas import tpu as pltpu
from jax.sharding import Mesh, PartitionSpec as P

ITERS = 3
SHARP = 48.0
EPSILON = 1e-06

AXES = ("z", "x", "c", "h", "y")
Z, X, C, H, Y = 8, 4, 2, 2, 4
BLOCKS = C * X
LANES = 128
PAD = 8


def exchange(blocks, axes):
    return lax.all_to_all(blocks, axes, 0, 0, tiled=True)


FETCHES = 55_500_000
FETCHES_BESIDE_TILE = 40_000_000


def params(limit=8 << 20):
    return pltpu.CompilerParams(vmem_limit_bytes=limit)


def column_of(row):
    return jnp.broadcast_to(row, (LANES, row.shape[1])).T


def row_of(partial):
    return jnp.sum(partial.T, axis=0, keepdims=True)


def fold(product):
    total = product[:, :LANES]
    for start in range(LANES, product.shape[1], LANES):
        total = total + product[:, start : start + LANES]
    return total


def widen(column, width):
    return jnp.concatenate([column] * (width // LANES), axis=1)


def place(b):
    return (b % X) * C + b // X


def fetch(pairs, sems):
    copies = [pltpu.make_async_copy(source, target, sems.at[i]) for i, (source, target) in enumerate(pairs)]
    for copy in copies:
        copy.start()
    return copies


def setup_kernel(where_ref, latents_ref, codes_ref, tile_ref, rows_ref, far_ref, tokens_ref, held_ref, sems):
    del where_ref
    pairs = [(codes_ref.at[:, place(b)], held_ref.at[b]) for b in range(BLOCKS)]
    *copies, first = fetch(pairs + [(latents_ref, tokens_ref)], sems)
    first.wait()
    saves = []
    latents = tokens_ref[...]
    width = latents.shape[1]
    floats = latents.astype(jnp.float32)
    mean = jnp.sum(floats * floats, axis=1, keepdims=True) * (1.0 / width)
    scale = jnp.broadcast_to(lax.rsqrt(mean + EPSILON) * (SHARP / width), (latents.shape[0], LANES))
    total = jnp.zeros(scale.shape, jnp.float32)
    across = (((1,), (1,)), ((), ()))
    for b in range(BLOCKS):
        copies[b].wait()
        codes = held_ref[b].reshape(-1, width)
        floats = codes.astype(jnp.float32)
        code_norm = lax.rsqrt(row_of(fold(floats * floats)) * (1.0 / width) + EPSILON)
        inner = lax.dot_general(latents, codes, across, preferred_element_type=jnp.float32)
        tile = jnp.exp(inner * widen(scale, codes.shape[0]) * code_norm)
        tile_ref[b] = tile
        saves.append(pltpu.make_async_copy(tile_ref.at[b], far_ref.at[b], sems.at[BLOCKS + 1 + b]))
        saves[b].start()
        total += fold(tile)
    rows_ref[...] = jnp.broadcast_to(row_of(total)[None], rows_ref.shape)
    for save in saves:
        save.wait()


def rows_kernel(columns_ref, tile_ref, rows_ref, total_ref):
    step = pl.program_id(0)

    @pl.when(step == 0)
    def _():
        total_ref[...] = jnp.zeros_like(total_ref)

    total_ref[...] += fold(tile_ref[...] * columns_ref[...])

    @pl.when(step == pl.num_programs(0) - 1)
    def _():
        rows_ref[...] = jnp.broadcast_to(row_of(total_ref[...])[None], rows_ref.shape)


def row_scale_of(parts_ref):
    return column_of(1.0 / jnp.sum(parts_ref[...], axis=0))


def columns_kernel(parts_ref, tile_ref, columns_ref, scale_ref):
    @pl.when(pl.program_id(0) == 0)
    def _():
        scale_ref[...] = row_scale_of(parts_ref)

    tile = tile_ref[...]
    sums = jnp.sum(tile * widen(scale_ref[...], tile.shape[1]), axis=0, keepdims=True)
    columns_ref[pl.program_id(0)] = sums


def targets_part(tile, scale, latents):
    weighted = (tile * widen(scale, tile.shape[1])).astype(jnp.bfloat16)
    return lax.dot_general(latents, weighted, (((0,), (0,)), ((), ())), preferred_element_type=jnp.float32)


def targets_sent_kernel(where_ref, parts_ref, latents_ref, tile_ref, after_ref, out_ref, tiles_ref, sems):
    del after_ref
    pairs = [(tile_ref.at[where_ref[3] * X + (where_ref[1] ^ s)], tiles_ref.at[s]) for s in range(X)]
    copies = fetch(pairs, sems)
    scale = row_scale_of(parts_ref)
    latents = latents_ref[...]
    for s in range(X):
        copies[s].wait()
        out_ref[s] = targets_part(tiles_ref[s], scale, latents)


def targets_kept_kernel(
    where_ref, parts_ref, latents_ref, tile_ref, added_ref, after_ref,
    one_ref, two_ref, own_one_ref, own_two_ref, tiles_ref, more_ref, sems,
):
    del after_ref
    pairs = [(tile_ref.at[where_ref[0] * X + (where_ref[1] ^ s)], tiles_ref.at[s]) for s in range(X)]
    pairs += [(added_ref.at[s], more_ref.at[s]) for s in range(X)]
    copies = fetch([pairs[i] for s in range(X) for i in (s, s + X)], sems)
    scale = row_scale_of(parts_ref)
    latents = latents_ref[...]
    for s in range(X):
        copies[2 * s].wait()
        summed = targets_part(tiles_ref[s], scale, latents)
        copies[2 * s + 1].wait()
        summed += more_ref[s]
        upper, lower = jnp.split(summed, 2, axis=0)
        ref, index = ((own_one_ref, 0), (one_ref, 0), (one_ref, 1), (own_one_ref, 1))[s]
        ref[index] = upper
        ref, index = ((own_two_ref, 0), (own_two_ref, 1), (two_ref, 1), (two_ref, 0))[s]
        ref[index] = lower


def sum_kernel(parts_ref, *refs):
    out_ref = refs[-1]
    out_ref[...] = jnp.broadcast_to(jnp.sum(parts_ref[...], axis=0, keepdims=True), out_ref.shape)


def inverse_kernel(factor, parts_ref, *refs):
    out_ref = refs[-1]
    out_ref[...] = jnp.broadcast_to(factor / jnp.sum(parts_ref[...], axis=0, keepdims=True), out_ref.shape)


def add_kernel(kept_ref, came_ref, after_ref, out_ref):
    del after_ref
    out_ref[...] = kept_ref[...] + came_ref[...]


def join_kernel(kept_ref, came_ref, after_ref, spread_ref, mass_ref):
    del after_ref
    total = kept_ref[...] + came_ref[...]
    group = spread_ref.shape[1]
    spread_ref[...] = jnp.broadcast_to(total[None, :group], spread_ref.shape)
    mass_ref[...] = total[group:]


def turn_kernel(where_ref, own_one_ref, one_ref, more_one_ref, own_two_ref, two_ref, more_two_ref, after_ref, *refs):
    del after_ref
    send_ref, keep_ref, turned_ref = refs
    upper = own_one_ref[0] + one_ref[0] + more_one_ref[...]
    lower = own_two_ref[0] + two_ref[0] + more_two_ref[...]
    turned_ref[...] = jnp.concatenate([upper, lower], axis=0).T
    share = send_ref.shape[1]
    for i, slot in enumerate((0, 4, 2, 6)):
        for ref, s in ((keep_ref, slot), (send_ref, slot + 1)):
            start = pl.multiple_of((where_ref[2] ^ s) * share, share)
            ref[i] = turned_ref[pl.ds(start, share), :]


def final_kernel(
    parts_ref, columns_ref, codes_ref, tile_ref, out_ref, held_ref, tiles_ref, numer_ref, sems
):
    pairs = [
        pair
        for b in range(BLOCKS)
        for pair in ((tile_ref.at[b], tiles_ref.at[b]), (codes_ref.at[:, place(b)], held_ref.at[b]))
    ]
    copies = fetch(pairs, sems)
    tokens, width = numer_ref.shape
    scale = row_scale_of(parts_ref)
    total = jnp.zeros(scale.shape, jnp.float32)
    for b in range(BLOCKS):
        copies[2 * b].wait()
        tile = tiles_ref[b]
        plan = (widen(scale, tile.shape[1]) * tile * columns_ref[b]).astype(jnp.bfloat16)
        total += fold(plan.astype(jnp.float32))
        copies[2 * b + 1].wait()
        part = jnp.dot(plan, held_ref[b].reshape(-1, width), preferred_element_type=jnp.float32)
        numer_ref[...] = part if b == 0 else numer_ref[...] + part
    group = tokens // Y
    mass = row_of(total)
    mass = jnp.concatenate([mass, jnp.zeros((1, 2 * width - tokens), jnp.float32)], axis=1)
    extra = jnp.concatenate(
        [mass[:, :width], mass[:, width:], jnp.zeros((PAD - 2, width), jnp.float32)], axis=0
    )
    for y in range(Y):
        out_ref[y, :group, :] = numer_ref[y * group : (y + 1) * group, :]
        out_ref[y, group:, :] = extra


def f32(*shape):
    return jax.ShapeDtypeStruct(shape, jnp.float32)


def whole(*shape):
    return pl.BlockSpec(shape, lambda *_: (0,) * len(shape))


def cost(flops, moved, exps=0):
    return pl.CostEstimate(flops=flops, bytes_accessed=moved, transcendentals=exps)


def per_device(latents, codebook):
    token_count, width = latents.shape
    code_count = codebook.shape[0]
    total_tokens = token_count * Z * X * C
    total_codes = code_count * H * Y
    share = code_count // (Z * X * C)
    block = code_count // BLOCKS
    size = token_count * code_count

    codes = codebook.reshape(Z, X * C, share, width)
    tile_spec = pl.BlockSpec((None, token_count, block), lambda b: (b, 0, 0))
    rows_spec = whole(H * Y, 1, token_count)
    columns_spec = pl.BlockSpec((None, 1, block), lambda b: (b, 0, 0))
    vmem = pl.BlockSpec(memory_space=pltpu.VMEM)
    smem = pl.BlockSpec(memory_space=pltpu.SMEM)
    hbm = pl.BlockSpec(memory_space=pltpu.HBM)
    anywhere = pl.BlockSpec(memory_space=pl.ANY)
    per_token = pltpu.VMEM((token_count, LANES), jnp.float32)
    held = pltpu.VMEM((BLOCKS, Z, share, width), jnp.bfloat16)
    tiles = functools.partial(pltpu.VMEM, dtype=jnp.float32)
    rows_shape = f32(H * Y, 1, token_count)
    columns_shape = f32(BLOCKS, 1, block)

    core, x, z = (lax.axis_index(axis) for axis in ("c", "x", "z"))
    where = jnp.stack([core, x, z, 1 - core, z * share])

    tile, part, far = pl.pallas_call(
        setup_kernel,
        in_specs=[smem, hbm, hbm],
        out_specs=[vmem, vmem, hbm],
        out_shape=[f32(BLOCKS, token_count, block), rows_shape, f32(BLOCKS, token_count, block)],
        scratch_shapes=[
            pltpu.VMEM((token_count, width), jnp.bfloat16),
            held,
            pltpu.SemaphoreType.DMA((2 * BLOCKS + 1,)),
        ],
        compiler_params=params(FETCHES_BESIDE_TILE),
        cost_estimate=cost(2 * size * width, 4 * size, size),
        name="setup",
    )(where, latents, codes)

    def rows(columns):
        return pl.pallas_call(
            rows_kernel,
            grid=(BLOCKS,),
            in_specs=[columns_spec, tile_spec],
            out_specs=rows_spec,
            out_shape=rows_shape,
            scratch_shapes=[per_token],
            compiler_params=params(),
            cost_estimate=cost(2 * size, 4 * size),
            name="rows",
        )(columns, tile)

    def columns(parts):
        return pl.pallas_call(
            columns_kernel,
            grid=(BLOCKS,),
            in_specs=[rows_spec, tile_spec],
            out_specs=whole(BLOCKS, 1, block),
            out_shape=columns_shape,
            scratch_shapes=[per_token],
            compiler_params=params(),
            cost_estimate=cost(2 * size, 4 * size),
            name="columns",
        )(parts, tile)

    def targets_sent(parts, after):
        return pl.pallas_call(
            targets_sent_kernel,
            in_specs=[smem, vmem, vmem, hbm, anywhere],
            out_specs=vmem,
            out_shape=f32(X, width, block),
            scratch_shapes=[tiles((X, token_count, block)), pltpu.SemaphoreType.DMA((X,))],
            compiler_params=params(FETCHES),
            cost_estimate=cost(size * width, 4 * size),
            name="targets_sent",
        )(where, parts, latents, far, after)

    def targets_kept(parts, added, after):
        return pl.pallas_call(
            targets_kept_kernel,
            in_specs=[smem, vmem, vmem, hbm, hbm, anywhere],
            out_specs=[vmem] * 4,
            out_shape=[f32(2, width // 2, block)] * 4,
            scratch_shapes=[
                tiles((X, token_count, block)),
                tiles((X, width, block)),
                pltpu.SemaphoreType.DMA((2 * X,)),
            ],
            compiler_params=params(FETCHES),
            cost_estimate=cost(size * width, 4 * size),
            name="targets_kept",
        )(where, parts, latents, far, added, after)

    def small(kernel, name, count, weight, parts, *after):
        return pl.pallas_call(
            kernel,
            in_specs=[vmem] + [anywhere] * len(after),
            out_specs=vmem,
            out_shape=f32(count, 1, block),
            compiler_params=params(),
            cost_estimate=cost(weight * parts.size, 4 * parts.size),
            name=name,
        )(parts, *after)

    inverse = functools.partial(inverse_kernel, total_tokens / total_codes)
    def swap(value, axis, count, bits):
        return lax.ppermute(value, axis, [(i, i ^ bits) for i in range(count)])

    def add(kept, came, after):
        return pl.pallas_call(
            add_kernel,
            in_specs=[vmem] * 2 + [anywhere],
            out_specs=vmem,
            out_shape=f32(*kept.shape),
            compiler_params=params(),
            cost_estimate=cost(kept.size, 12 * kept.size),
            name="add",
        )(kept, came, after)

    for sweep_index in range(ITERS):
        last = sweep_index == ITERS - 1
        parts = exchange(part, ("h", "y"))
        column_sums = columns(parts)
        if last:
            sent = targets_sent(parts, column_sums)
        sums = small(sum_kernel, "sums", Z, 20_000_000 if last else 1, exchange(column_sums, ("c", "x")))
        if last:
            kept = targets_kept(parts, swap(sent, "c", C, 1), sums)
        after = (kept[0],) if last else ()
        mine = small(inverse, "inverse", BLOCKS, 1, exchange(sums, "z"), *after)
        col_scale = exchange(mine, ("c", "x"))
        if not last:
            part = rows(col_scale)

    one, two, own_one, own_two = kept
    one, two = swap(one, "x", X, 1), swap(two, "x", X, 3)
    more_one = swap(own_one[1] + one[1], "x", X, 3)
    more_two = swap(own_two[1] + two[1], "x", X, 1)

    group = token_count // Y
    packed = pl.pallas_call(
        final_kernel,
        in_specs=[vmem, vmem, hbm, hbm],
        out_specs=vmem,
        out_shape=f32(Y, group + PAD, width),
        scratch_shapes=[
            held,
            tiles((BLOCKS, token_count, block)),
            tiles((token_count, width)),
            pltpu.SemaphoreType.DMA((2 * BLOCKS,)),
        ],
        compiler_params=params(FETCHES),
        cost_estimate=cost(12 * size * width, 4 * size),
        name="final",
    )(parts, col_scale, codes, far)
    packed = jnp.sum(exchange(packed, "y"), axis=0)
    away, near = pl.pallas_call(
        turn_kernel,
        in_specs=[smem] + [vmem] * 6 + [anywhere],
        out_specs=[vmem] * 2,
        out_shape=[f32(Z // 2, share, width)] * 2,
        scratch_shapes=[pltpu.VMEM((block, width), jnp.float32)],
        compiler_params=params(16 << 20),
        cost_estimate=cost(3 * block * width, 12 * block * width),
        name="turn",
    )(where, own_one, one, more_one, own_two, two, more_two, packed)
    near = near + swap(away, "z", Z, 1)
    numer, mass = pl.pallas_call(
        join_kernel,
        in_specs=[vmem] * 2 + [anywhere],
        out_specs=[vmem] * 2,
        out_shape=[f32(Y, group, width), f32(PAD, width)],
        compiler_params=params(),
        cost_estimate=cost(20000 * token_count * width, 8 * token_count * width),
        name="join",
    )(packed, swap(packed, "h", H, 1), near)
    near = add(near[:2], swap(near[2:], "z", Z, 2), mass)
    summed = near[0] + swap(near[1], "z", Z, 4)
    own = lax.dynamic_slice(mine, (0, 0, where[4]), (1, 1, share)).reshape(share)
    targets = summed * (own * (total_codes / total_tokens))[:, None]
    mass = mass[:2].reshape(2 * width)[:token_count]
    rebuilt = exchange(numer, "y").reshape(token_count, width) / mass[:, None]
    return (targets, rebuilt)


def solution(mesh):
    fine = Mesh(mesh.devices.reshape(Z, X, C, H, Y), AXES)
    return jax.shard_map(
        per_device,
        mesh=fine,
        in_specs=(P(("z", "x", "c"), None), P(("h", "y"), None)),
        out_specs=(P(("h", "y", "z", "x", "c"), None), P(("z", "x", "c"), None)),
        check_vma=False,
    )
```

```python
import functools

import jax
import jax.numpy as jnp
from jax import lax
from jax.experimental import pallas as pl
from jax.experimental.pallas import tpu as pltpu
from jax.sharding import Mesh, PartitionSpec as P

ITERS = 3
SHARP = 48.0
EPSILON = 1e-06

AXES = ("z", "x", "c", "h", "y")
Z, X, C, H, Y = 8, 4, 2, 2, 4
BLOCKS = C * X
LANES = 128
PAD = 8


def exchange(blocks, axes):
    return lax.all_to_all(blocks, axes, 0, 0, tiled=True)


FETCHES = 55_500_000
FETCHES_BESIDE_TILE = 40_000_000


def params(limit=8 << 20):
    return pltpu.CompilerParams(vmem_limit_bytes=limit)


def column_of(row):
    return jnp.broadcast_to(row, (LANES, row.shape[1])).T


def row_of(partial):
    return jnp.sum(partial.T, axis=0, keepdims=True)


def fold(product):
    total = product[:, :LANES]
    for start in range(LANES, product.shape[1], LANES):
        total = total + product[:, start : start + LANES]
    return total


def widen(column, width):
    return jnp.concatenate([column] * (width // LANES), axis=1)


def place(b):
    return (b % X) * C + b // X


AHEAD = 3


def fetch(steps, sems):
    copies, count = [], 0
    for pairs in steps:
        copies.append([pltpu.make_async_copy(*pair, sems.at[count + i]) for i, pair in enumerate(pairs)])
        count += len(pairs)

    def start(step):
        for copy in copies[step]:
            copy.start()

    def wait(step):
        if step + AHEAD < len(copies):
            start(step + AHEAD)
        for copy in copies[step]:
            copy.wait()

    for step in range(min(AHEAD, len(copies))):
        start(step)
    return wait


def setup_kernel(where_ref, latents_ref, codes_ref, tile_ref, rows_ref, far_ref, tokens_ref, held_ref, sems):
    del where_ref
    steps = [[(latents_ref, tokens_ref)]]
    wait = fetch(steps + [[(codes_ref.at[:, place(b)], held_ref.at[b])] for b in range(BLOCKS)], sems)
    wait(0)
    saves = []
    latents = tokens_ref[...]
    width = latents.shape[1]
    floats = latents.astype(jnp.float32)
    mean = jnp.sum(floats * floats, axis=1, keepdims=True) * (1.0 / width)
    scale = jnp.broadcast_to(lax.rsqrt(mean + EPSILON) * (SHARP / width), (latents.shape[0], LANES))
    total = jnp.zeros(scale.shape, jnp.float32)
    across = (((1,), (1,)), ((), ()))
    for b in range(BLOCKS):
        wait(1 + b)
        codes = held_ref[b].reshape(-1, width)
        floats = codes.astype(jnp.float32)
        code_norm = lax.rsqrt(row_of(fold(floats * floats)) * (1.0 / width) + EPSILON)
        inner = lax.dot_general(latents, codes, across, preferred_element_type=jnp.float32)
        tile = jnp.exp(inner * widen(scale, codes.shape[0]) * code_norm)
        tile_ref[b] = tile
        saves.append(pltpu.make_async_copy(tile_ref.at[b], far_ref.at[b], sems.at[BLOCKS + 1 + b]))
        saves[b].start()
        total += fold(tile)
    rows_ref[...] = jnp.broadcast_to(row_of(total)[None], rows_ref.shape)
    for save in saves:
        save.wait()


def rows_kernel(columns_ref, tile_ref, rows_ref, total_ref):
    step = pl.program_id(0)

    @pl.when(step == 0)
    def _():
        total_ref[...] = jnp.zeros_like(total_ref)

    total_ref[...] += fold(tile_ref[...] * columns_ref[...])

    @pl.when(step == pl.num_programs(0) - 1)
    def _():
        rows_ref[...] = jnp.broadcast_to(row_of(total_ref[...])[None], rows_ref.shape)


def row_scale_of(parts_ref):
    return column_of(1.0 / jnp.sum(parts_ref[...], axis=0))


def columns_kernel(parts_ref, tile_ref, columns_ref, scale_ref):
    @pl.when(pl.program_id(0) == 0)
    def _():
        scale_ref[...] = row_scale_of(parts_ref)

    tile = tile_ref[...]
    sums = jnp.sum(tile * widen(scale_ref[...], tile.shape[1]), axis=0, keepdims=True)
    columns_ref[pl.program_id(0)] = sums


def targets_part(tile, scale, latents):
    weighted = (tile * widen(scale, tile.shape[1])).astype(jnp.bfloat16)
    return lax.dot_general(latents, weighted, (((0,), (0,)), ((), ())), preferred_element_type=jnp.float32)


def targets_sent_kernel(where_ref, parts_ref, latents_ref, tile_ref, after_ref, out_ref, tiles_ref, sems):
    del after_ref
    wait = fetch([[(tile_ref.at[where_ref[3] * X + (where_ref[1] ^ s)], tiles_ref.at[s])] for s in range(X)], sems)
    scale = row_scale_of(parts_ref)
    latents = latents_ref[...]
    for s in range(X):
        wait(s)
        out_ref[s] = targets_part(tiles_ref[s], scale, latents)


def targets_kept_kernel(
    where_ref, parts_ref, latents_ref, tile_ref, added_ref, after_ref, own_ref, one_ref, two_ref, three_ref, tiles_ref, more_ref, sems
):
    del after_ref
    slots = (2, 1, 3, 0)
    steps = [
        [(tile_ref.at[where_ref[0] * X + (where_ref[1] ^ s)], tiles_ref.at[s]), (added_ref.at[s], more_ref.at[s])]
        for s in slots
    ]
    wait = fetch(steps, sems)
    scale = row_scale_of(parts_ref)
    latents = latents_ref[...]
    for step, s in enumerate(slots):
        wait(step)
        (own_ref, one_ref, two_ref, three_ref)[s][...] = targets_part(tiles_ref[s], scale, latents) + more_ref[s]


def sum_kernel(parts_ref, *refs):
    out_ref = refs[-1]
    out_ref[...] = jnp.broadcast_to(jnp.sum(parts_ref[...], axis=0, keepdims=True), out_ref.shape)


def inverse_kernel(factor, parts_ref, *refs):
    out_ref = refs[-1]
    out_ref[...] = jnp.broadcast_to(factor / jnp.sum(parts_ref[...], axis=0, keepdims=True), out_ref.shape)


def add_kernel(kept_ref, came_ref, after_ref, out_ref):
    del after_ref
    out_ref[...] = kept_ref[...] + came_ref[...]


def join_kernel(kept_ref, came_ref, after_ref, spread_ref, mass_ref):
    del after_ref
    total = kept_ref[...] + came_ref[...]
    group = spread_ref.shape[1]
    spread_ref[...] = jnp.broadcast_to(total[None, :group], spread_ref.shape)
    mass_ref[...] = total[group:]


def turn_kernel(where_ref, own_ref, one_ref, two_ref, three_ref, after_ref, send_ref, keep_ref, turned_ref):
    del after_ref
    turned_ref[...] = (own_ref[...] + one_ref[...] + two_ref[...] + three_ref[...]).T
    share = send_ref.shape[1]
    for i, slot in enumerate((0, 4, 2, 6)):
        for ref, s in ((keep_ref, slot), (send_ref, slot + 1)):
            start = pl.multiple_of((where_ref[2] ^ s) * share, share)
            ref[i] = turned_ref[pl.ds(start, share), :]


def final_kernel(
    parts_ref, columns_ref, codes_ref, tile_ref, out_ref, held_ref, tiles_ref, numer_ref, sems
):
    steps = [
        [(tile_ref.at[b], tiles_ref.at[b]), (codes_ref.at[:, place(b)], held_ref.at[b])] for b in range(BLOCKS)
    ]
    wait = fetch(steps, sems)
    tokens, width = numer_ref.shape
    scale = row_scale_of(parts_ref)
    total = jnp.zeros(scale.shape, jnp.float32)
    for b in range(BLOCKS):
        wait(b)
        tile = tiles_ref[b]
        plan = (widen(scale, tile.shape[1]) * tile * columns_ref[b]).astype(jnp.bfloat16)
        total += fold(plan.astype(jnp.float32))
        part = jnp.dot(plan, held_ref[b].reshape(-1, width), preferred_element_type=jnp.float32)
        numer_ref[...] = part if b == 0 else numer_ref[...] + part
    group = tokens // Y
    mass = row_of(total)
    mass = jnp.concatenate([mass, jnp.zeros((1, 2 * width - tokens), jnp.float32)], axis=1)
    extra = jnp.concatenate(
        [mass[:, :width], mass[:, width:], jnp.zeros((PAD - 2, width), jnp.float32)], axis=0
    )
    for y in range(Y):
        out_ref[y, :group, :] = numer_ref[y * group : (y + 1) * group, :]
        out_ref[y, group:, :] = extra


def f32(*shape):
    return jax.ShapeDtypeStruct(shape, jnp.float32)


def whole(*shape):
    return pl.BlockSpec(shape, lambda *_: (0,) * len(shape))


def cost(flops, moved, exps=0):
    return pl.CostEstimate(flops=flops, bytes_accessed=moved, transcendentals=exps)


def per_device(latents, codebook):
    token_count, width = latents.shape
    code_count = codebook.shape[0]
    total_tokens = token_count * Z * X * C
    total_codes = code_count * H * Y
    share = code_count // (Z * X * C)
    block = code_count // BLOCKS
    size = token_count * code_count

    codes = codebook.reshape(Z, X * C, share, width)
    tile_spec = pl.BlockSpec((None, token_count, block), lambda b: (b, 0, 0))
    rows_spec = whole(H * Y, 1, token_count)
    columns_spec = pl.BlockSpec((None, 1, block), lambda b: (b, 0, 0))
    vmem = pl.BlockSpec(memory_space=pltpu.VMEM)
    smem = pl.BlockSpec(memory_space=pltpu.SMEM)
    hbm = pl.BlockSpec(memory_space=pltpu.HBM)
    anywhere = pl.BlockSpec(memory_space=pl.ANY)
    per_token = pltpu.VMEM((token_count, LANES), jnp.float32)
    held = pltpu.VMEM((BLOCKS, Z, share, width), jnp.bfloat16)
    tiles = functools.partial(pltpu.VMEM, dtype=jnp.float32)
    rows_shape = f32(H * Y, 1, token_count)
    columns_shape = f32(BLOCKS, 1, block)

    core, x, z = (lax.axis_index(axis) for axis in ("c", "x", "z"))
    where = jnp.stack([core, x, z, 1 - core, z * share])

    tile, part, far = pl.pallas_call(
        setup_kernel,
        in_specs=[smem, hbm, hbm],
        out_specs=[vmem, vmem, hbm],
        out_shape=[f32(BLOCKS, token_count, block), rows_shape, f32(BLOCKS, token_count, block)],
        scratch_shapes=[
            pltpu.VMEM((token_count, width), jnp.bfloat16),
            held,
            pltpu.SemaphoreType.DMA((2 * BLOCKS + 1,)),
        ],
        compiler_params=params(FETCHES_BESIDE_TILE),
        cost_estimate=cost(2 * size * width, 4 * size, size),
        name="setup",
    )(where, latents, codes)

    def rows(columns):
        return pl.pallas_call(
            rows_kernel,
            grid=(BLOCKS,),
            in_specs=[columns_spec, tile_spec],
            out_specs=rows_spec,
            out_shape=rows_shape,
            scratch_shapes=[per_token],
            compiler_params=params(),
            cost_estimate=cost(2 * size, 4 * size),
            name="rows",
        )(columns, tile)

    def columns(parts):
        return pl.pallas_call(
            columns_kernel,
            grid=(BLOCKS,),
            in_specs=[rows_spec, tile_spec],
            out_specs=whole(BLOCKS, 1, block),
            out_shape=columns_shape,
            scratch_shapes=[per_token],
            compiler_params=params(),
            cost_estimate=cost(2 * size, 4 * size),
            name="columns",
        )(parts, tile)

    def targets_sent(parts, after):
        return pl.pallas_call(
            targets_sent_kernel,
            in_specs=[smem, vmem, vmem, hbm, anywhere],
            out_specs=vmem,
            out_shape=f32(X, width, block),
            scratch_shapes=[tiles((X, token_count, block)), pltpu.SemaphoreType.DMA((X,))],
            compiler_params=params(FETCHES),
            cost_estimate=cost(size * width, 4 * size),
            name="targets_sent",
        )(where, parts, latents, far, after)

    def targets_kept(parts, added, after):
        return pl.pallas_call(
            targets_kept_kernel,
            in_specs=[smem, vmem, vmem, hbm, hbm, anywhere],
            out_specs=[vmem] * 4,
            out_shape=[f32(width, block)] * 4,
            scratch_shapes=[
                tiles((X, token_count, block)),
                tiles((X, width, block)),
                pltpu.SemaphoreType.DMA((2 * X,)),
            ],
            compiler_params=params(FETCHES),
            cost_estimate=cost(size * width, 4 * size),
            name="targets_kept",
        )(where, parts, latents, far, added, after)

    def small(kernel, name, count, weight, parts, *after):
        return pl.pallas_call(
            kernel,
            in_specs=[vmem] + [anywhere] * len(after),
            out_specs=vmem,
            out_shape=f32(count, 1, block),
            compiler_params=params(),
            cost_estimate=cost(weight * parts.size, 4 * parts.size),
            name=name,
        )(parts, *after)

    inverse = functools.partial(inverse_kernel, total_tokens / total_codes)
    def swap(value, axis, count, bits):
        return lax.ppermute(value, axis, [(i, i ^ bits) for i in range(count)])

    def add(kept, came, after):
        return pl.pallas_call(
            add_kernel,
            in_specs=[vmem] * 2 + [anywhere],
            out_specs=vmem,
            out_shape=f32(*kept.shape),
            compiler_params=params(),
            cost_estimate=cost(kept.size, 12 * kept.size),
            name="add",
        )(kept, came, after)

    for sweep_index in range(ITERS):
        last = sweep_index == ITERS - 1
        parts = exchange(part, ("h", "y"))
        column_sums = columns(parts)
        if last:
            sent = targets_sent(parts, column_sums)
        sums = small(sum_kernel, "sums", Z, 20_000_000 if last else 1, exchange(column_sums, ("c", "x")))
        if last:
            kept = targets_kept(parts, swap(sent, "c", C, 1), sums)
        after = (kept[0],) if last else ()
        mine = small(inverse, "inverse", BLOCKS, 1, exchange(sums, "z"), *after)
        col_scale = exchange(mine, ("c", "x"))
        if not last:
            part = rows(col_scale)

    own, *others = kept
    others = [swap(other, "x", X, s) for s, other in enumerate(others, 1)]

    group = token_count // Y
    packed = pl.pallas_call(
        final_kernel,
        in_specs=[vmem, vmem, hbm, hbm],
        out_specs=vmem,
        out_shape=f32(Y, group + PAD, width),
        scratch_shapes=[
            held,
            tiles((BLOCKS, token_count, block)),
            tiles((token_count, width)),
            pltpu.SemaphoreType.DMA((2 * BLOCKS,)),
        ],
        compiler_params=params(FETCHES),
        cost_estimate=cost(5 * size * width, 4 * size),
        name="final",
    )(parts, col_scale, codes, far)
    packed = jnp.sum(exchange(packed, "y"), axis=0)
    away, near = pl.pallas_call(
        turn_kernel,
        in_specs=[smem] + [vmem] * 4 + [anywhere],
        out_specs=[vmem] * 2,
        out_shape=[f32(Z // 2, share, width)] * 2,
        scratch_shapes=[pltpu.VMEM((block, width), jnp.float32)],
        compiler_params=params(16 << 20),
        cost_estimate=cost(3 * block * width, 12 * block * width),
        name="turn",
    )(where, own, *others, packed)
    near = near + swap(away, "z", Z, 1)
    numer, mass = pl.pallas_call(
        join_kernel,
        in_specs=[vmem] * 2 + [anywhere],
        out_specs=[vmem] * 2,
        out_shape=[f32(Y, group, width), f32(PAD, width)],
        compiler_params=params(),
        cost_estimate=cost(20000 * token_count * width, 8 * token_count * width),
        name="join",
    )(packed, swap(packed, "h", H, 1), near)
    near = add(near[:2], swap(near[2:], "z", Z, 2), mass)
    summed = near[0] + swap(near[1], "z", Z, 4)
    scale = lax.dynamic_slice(mine, (0, 0, where[4]), (1, 1, share)).reshape(share)
    targets = summed * (scale * (total_codes / total_tokens))[:, None]
    mass = mass[:2].reshape(2 * width)[:token_count]
    rebuilt = exchange(numer, "y").reshape(token_count, width) / mass[:, None]
    return (targets, rebuilt)


def solution(mesh):
    fine = Mesh(mesh.devices.reshape(Z, X, C, H, Y), AXES)
    return jax.shard_map(
        per_device,
        mesh=fine,
        in_specs=(P(("z", "x", "c"), None), P(("h", "y"), None)),
        out_specs=(P(("h", "y", "z", "x", "c"), None), P(("z", "x", "c"), None)),
        check_vma=False,
    )
```

```python
import functools

import jax
import jax.numpy as jnp
from jax import lax
from jax.experimental import pallas as pl
from jax.experimental.pallas import tpu as pltpu
from jax.sharding import Mesh, PartitionSpec as P

ITERS = 3
SHARP = 48.0
EPSILON = 1e-06

AXES = ("z", "x", "c", "h", "y")
Z, X, C, H, Y = 8, 4, 2, 2, 4
BLOCKS = C * X
LANES = 128
PAD = 8


def exchange(blocks, axes):
    return lax.all_to_all(blocks, axes, 0, 0, tiled=True)


FETCHES = 55_500_000
FETCHES_BESIDE_TILE = 40_000_000


def params(limit=8 << 20):
    return pltpu.CompilerParams(vmem_limit_bytes=limit)


def column_of(row):
    return jnp.broadcast_to(row, (LANES, row.shape[1])).T


def row_of(partial):
    return jnp.sum(partial.T, axis=0, keepdims=True)


def fold(product):
    total = product[:, :LANES]
    for start in range(LANES, product.shape[1], LANES):
        total = total + product[:, start : start + LANES]
    return total


def widen(column, width):
    return jnp.concatenate([column] * (width // LANES), axis=1)


def place(b):
    return (b % X) * C + b // X


AHEAD = 3


def fetch(steps, sems):
    copies, count = [], 0
    for pairs in steps:
        copies.append([pltpu.make_async_copy(*pair, sems.at[count + i]) for i, pair in enumerate(pairs)])
        count += len(pairs)

    def start(step):
        for copy in copies[step]:
            copy.start()

    def wait(step):
        if step + AHEAD < len(copies):
            start(step + AHEAD)
        for copy in copies[step]:
            copy.wait()

    for step in range(min(AHEAD, len(copies))):
        start(step)
    return wait


def setup_kernel(where_ref, latents_ref, codes_ref, tile_ref, rows_ref, far_ref, tokens_ref, held_ref, sems):
    del where_ref
    steps = [[(latents_ref, tokens_ref)]]
    wait = fetch(steps + [[(codes_ref.at[:, place(b)], held_ref.at[b])] for b in range(BLOCKS)], sems)
    wait(0)
    saves = []
    latents = tokens_ref[...]
    width = latents.shape[1]
    floats = latents.astype(jnp.float32)
    mean = jnp.sum(floats * floats, axis=1, keepdims=True) * (1.0 / width)
    scale = jnp.broadcast_to(lax.rsqrt(mean + EPSILON) * (SHARP / width), (latents.shape[0], LANES))
    total = jnp.zeros(scale.shape, jnp.float32)
    across = (((1,), (1,)), ((), ()))
    for b in range(BLOCKS):
        wait(1 + b)
        codes = held_ref[b].reshape(-1, width)
        floats = codes.astype(jnp.float32)
        code_norm = lax.rsqrt(row_of(fold(floats * floats)) * (1.0 / width) + EPSILON)
        inner = lax.dot_general(latents, codes, across, preferred_element_type=jnp.float32)
        tile = jnp.exp(inner * widen(scale, codes.shape[0]) * code_norm)
        tile_ref[b] = tile
        saves.append(pltpu.make_async_copy(tile_ref.at[b], far_ref.at[b], sems.at[BLOCKS + 1 + b]))
        saves[b].start()
        total += fold(tile)
    rows_ref[...] = jnp.broadcast_to(row_of(total)[None], rows_ref.shape)
    for save in saves:
        save.wait()


def rows_kernel(columns_ref, tile_ref, rows_ref, total_ref):
    step = pl.program_id(0)

    @pl.when(step == 0)
    def _():
        total_ref[...] = jnp.zeros_like(total_ref)

    total_ref[...] += fold(tile_ref[...] * columns_ref[...])

    @pl.when(step == pl.num_programs(0) - 1)
    def _():
        rows_ref[...] = jnp.broadcast_to(row_of(total_ref[...])[None], rows_ref.shape)


def row_scale_of(parts_ref):
    return column_of(1.0 / jnp.sum(parts_ref[...], axis=0))


def columns_kernel(parts_ref, tile_ref, columns_ref, scale_ref):
    @pl.when(pl.program_id(0) == 0)
    def _():
        scale_ref[...] = row_scale_of(parts_ref)

    tile = tile_ref[...]
    sums = jnp.sum(tile * widen(scale_ref[...], tile.shape[1]), axis=0, keepdims=True)
    columns_ref[pl.program_id(0)] = sums


def targets_part(tile, scale, latents):
    weighted = (tile * widen(scale, tile.shape[1])).astype(jnp.bfloat16)
    return lax.dot_general(latents, weighted, (((0,), (0,)), ((), ())), preferred_element_type=jnp.float32)


def targets_sent_kernel(where_ref, parts_ref, latents_ref, tile_ref, after_ref, out_ref, tiles_ref, sems):
    del after_ref
    wait = fetch([[(tile_ref.at[where_ref[3] * X + (where_ref[1] ^ s)], tiles_ref.at[s])] for s in range(X)], sems)
    scale = row_scale_of(parts_ref)
    latents = latents_ref[...]
    for s in range(X):
        wait(s)
        out_ref[s] = targets_part(tiles_ref[s], scale, latents)


def targets_kept_kernel(
    where_ref, parts_ref, latents_ref, tile_ref, added_ref, after_ref,
    one_ref, two_ref, own_one_ref, own_two_ref, tiles_ref, more_ref, sems,
):
    del after_ref
    steps = [
        [(tile_ref.at[where_ref[0] * X + (where_ref[1] ^ s)], tiles_ref.at[s]), (added_ref.at[s], more_ref.at[s])]
        for s in range(X)
    ]
    wait = fetch(steps, sems)
    scale = row_scale_of(parts_ref)
    latents = latents_ref[...]
    for s in range(X):
        wait(s)
        summed = targets_part(tiles_ref[s], scale, latents) + more_ref[s]
        upper, lower = jnp.split(summed, 2, axis=0)
        ref, index = ((own_one_ref, 0), (one_ref, 0), (one_ref, 1), (own_one_ref, 1))[s]
        ref[index] = upper
        ref, index = ((own_two_ref, 0), (own_two_ref, 1), (two_ref, 1), (two_ref, 0))[s]
        ref[index] = lower


def sum_kernel(parts_ref, *refs):
    out_ref = refs[-1]
    out_ref[...] = jnp.broadcast_to(jnp.sum(parts_ref[...], axis=0, keepdims=True), out_ref.shape)


def inverse_kernel(factor, parts_ref, *refs):
    out_ref = refs[-1]
    out_ref[...] = jnp.broadcast_to(factor / jnp.sum(parts_ref[...], axis=0, keepdims=True), out_ref.shape)


def add_kernel(kept_ref, came_ref, after_ref, out_ref):
    del after_ref
    out_ref[...] = kept_ref[...] + came_ref[...]


def join_kernel(kept_ref, came_ref, after_ref, spread_ref, mass_ref):
    del after_ref
    total = kept_ref[...] + came_ref[...]
    group = spread_ref.shape[1]
    spread_ref[...] = jnp.broadcast_to(total[None, :group], spread_ref.shape)
    mass_ref[...] = total[group:]


def turn_kernel(where_ref, own_one_ref, one_ref, more_one_ref, own_two_ref, two_ref, more_two_ref, after_ref, *refs):
    del after_ref
    send_ref, keep_ref, turned_ref = refs
    upper = own_one_ref[0] + one_ref[0] + more_one_ref[...]
    lower = own_two_ref[0] + two_ref[0] + more_two_ref[...]
    turned_ref[...] = jnp.concatenate([upper, lower], axis=0).T
    share = send_ref.shape[1]
    for i, slot in enumerate((0, 4, 2, 6)):
        for ref, s in ((keep_ref, slot), (send_ref, slot + 1)):
            start = pl.multiple_of((where_ref[2] ^ s) * share, share)
            ref[i] = turned_ref[pl.ds(start, share), :]


def final_kernel(
    parts_ref, columns_ref, codes_ref, tile_ref, out_ref, held_ref, tiles_ref, numer_ref, sems
):
    steps = [
        [(tile_ref.at[b], tiles_ref.at[b]), (codes_ref.at[:, place(b)], held_ref.at[b])] for b in range(BLOCKS)
    ]
    wait = fetch(steps, sems)
    tokens, width = numer_ref.shape
    scale = row_scale_of(parts_ref)
    total = jnp.zeros(scale.shape, jnp.float32)
    for b in range(BLOCKS):
        wait(b)
        tile = tiles_ref[b]
        plan = (widen(scale, tile.shape[1]) * tile * columns_ref[b]).astype(jnp.bfloat16)
        total += fold(plan.astype(jnp.float32))
        part = jnp.dot(plan, held_ref[b].reshape(-1, width), preferred_element_type=jnp.float32)
        numer_ref[...] = part if b == 0 else numer_ref[...] + part
    group = tokens // Y
    mass = row_of(total)
    mass = jnp.concatenate([mass, jnp.zeros((1, 2 * width - tokens), jnp.float32)], axis=1)
    extra = jnp.concatenate(
        [mass[:, :width], mass[:, width:], jnp.zeros((PAD - 2, width), jnp.float32)], axis=0
    )
    for y in range(Y):
        out_ref[y, :group, :] = numer_ref[y * group : (y + 1) * group, :]
        out_ref[y, group:, :] = extra


def f32(*shape):
    return jax.ShapeDtypeStruct(shape, jnp.float32)


def whole(*shape):
    return pl.BlockSpec(shape, lambda *_: (0,) * len(shape))


def cost(flops, moved, exps=0):
    return pl.CostEstimate(flops=flops, bytes_accessed=moved, transcendentals=exps)


def per_device(latents, codebook):
    token_count, width = latents.shape
    code_count = codebook.shape[0]
    total_tokens = token_count * Z * X * C
    total_codes = code_count * H * Y
    share = code_count // (Z * X * C)
    block = code_count // BLOCKS
    size = token_count * code_count

    codes = codebook.reshape(Z, X * C, share, width)
    tile_spec = pl.BlockSpec((None, token_count, block), lambda b: (b, 0, 0))
    rows_spec = whole(H * Y, 1, token_count)
    columns_spec = pl.BlockSpec((None, 1, block), lambda b: (b, 0, 0))
    vmem = pl.BlockSpec(memory_space=pltpu.VMEM)
    smem = pl.BlockSpec(memory_space=pltpu.SMEM)
    hbm = pl.BlockSpec(memory_space=pltpu.HBM)
    anywhere = pl.BlockSpec(memory_space=pl.ANY)
    per_token = pltpu.VMEM((token_count, LANES), jnp.float32)
    held = pltpu.VMEM((BLOCKS, Z, share, width), jnp.bfloat16)
    tiles = functools.partial(pltpu.VMEM, dtype=jnp.float32)
    rows_shape = f32(H * Y, 1, token_count)
    columns_shape = f32(BLOCKS, 1, block)

    core, x, z = (lax.axis_index(axis) for axis in ("c", "x", "z"))
    where = jnp.stack([core, x, z, 1 - core, z * share])

    tile, part, far = pl.pallas_call(
        setup_kernel,
        in_specs=[smem, hbm, hbm],
        out_specs=[vmem, vmem, hbm],
        out_shape=[f32(BLOCKS, token_count, block), rows_shape, f32(BLOCKS, token_count, block)],
        scratch_shapes=[
            pltpu.VMEM((token_count, width), jnp.bfloat16),
            held,
            pltpu.SemaphoreType.DMA((2 * BLOCKS + 1,)),
        ],
        compiler_params=params(FETCHES_BESIDE_TILE),
        cost_estimate=cost(2 * size * width, 4 * size, size),
        name="setup",
    )(where, latents, codes)

    def rows(columns):
        return pl.pallas_call(
            rows_kernel,
            grid=(BLOCKS,),
            in_specs=[columns_spec, tile_spec],
            out_specs=rows_spec,
            out_shape=rows_shape,
            scratch_shapes=[per_token],
            compiler_params=params(),
            cost_estimate=cost(2 * size, 4 * size),
            name="rows",
        )(columns, tile)

    def columns(parts):
        return pl.pallas_call(
            columns_kernel,
            grid=(BLOCKS,),
            in_specs=[rows_spec, tile_spec],
            out_specs=whole(BLOCKS, 1, block),
            out_shape=columns_shape,
            scratch_shapes=[per_token],
            compiler_params=params(),
            cost_estimate=cost(2 * size, 4 * size),
            name="columns",
        )(parts, tile)

    def targets_sent(parts, after):
        return pl.pallas_call(
            targets_sent_kernel,
            in_specs=[smem, vmem, vmem, hbm, anywhere],
            out_specs=vmem,
            out_shape=f32(X, width, block),
            scratch_shapes=[tiles((X, token_count, block)), pltpu.SemaphoreType.DMA((X,))],
            compiler_params=params(FETCHES),
            cost_estimate=cost(size * width, 4 * size),
            name="targets_sent",
        )(where, parts, latents, far, after)

    def targets_kept(parts, added, after):
        return pl.pallas_call(
            targets_kept_kernel,
            in_specs=[smem, vmem, vmem, hbm, hbm, anywhere],
            out_specs=[vmem] * 4,
            out_shape=[f32(2, width // 2, block)] * 4,
            scratch_shapes=[
                tiles((X, token_count, block)),
                tiles((X, width, block)),
                pltpu.SemaphoreType.DMA((2 * X,)),
            ],
            compiler_params=params(FETCHES),
            cost_estimate=cost(size * width, 4 * size),
            name="targets_kept",
        )(where, parts, latents, far, added, after)

    def small(kernel, name, count, weight, parts, *after):
        return pl.pallas_call(
            kernel,
            in_specs=[vmem] + [anywhere] * len(after),
            out_specs=vmem,
            out_shape=f32(count, 1, block),
            compiler_params=params(),
            cost_estimate=cost(weight * parts.size, 4 * parts.size),
            name=name,
        )(parts, *after)

    inverse = functools.partial(inverse_kernel, total_tokens / total_codes)
    def swap(value, axis, count, bits):
        return lax.ppermute(value, axis, [(i, i ^ bits) for i in range(count)])

    def add(kept, came, after):
        return pl.pallas_call(
            add_kernel,
            in_specs=[vmem] * 2 + [anywhere],
            out_specs=vmem,
            out_shape=f32(*kept.shape),
            compiler_params=params(),
            cost_estimate=cost(kept.size, 12 * kept.size),
            name="add",
        )(kept, came, after)

    for sweep_index in range(ITERS):
        last = sweep_index == ITERS - 1
        parts = exchange(part, ("h", "y"))
        column_sums = columns(parts)
        if last:
            sent = targets_sent(parts, column_sums)
        sums = small(sum_kernel, "sums", Z, 20_000_000 if last else 1, exchange(column_sums, ("c", "x")))
        if last:
            kept = targets_kept(parts, swap(sent, "c", C, 1), sums)
        after = (kept[0],) if last else ()
        mine = small(inverse, "inverse", BLOCKS, 1, exchange(sums, "z"), *after)
        col_scale = exchange(mine, ("c", "x"))
        if not last:
            part = rows(col_scale)

    one, two, own_one, own_two = kept
    one, two = swap(one, "x", X, 1), swap(two, "x", X, 3)
    more_one = swap(own_one[1] + one[1], "x", X, 3)
    more_two = swap(own_two[1] + two[1], "x", X, 1)

    group = token_count // Y
    packed = pl.pallas_call(
        final_kernel,
        in_specs=[vmem, vmem, hbm, hbm],
        out_specs=vmem,
        out_shape=f32(Y, group + PAD, width),
        scratch_shapes=[
            held,
            tiles((BLOCKS, token_count, block)),
            tiles((token_count, width)),
            pltpu.SemaphoreType.DMA((2 * BLOCKS,)),
        ],
        compiler_params=params(FETCHES),
        cost_estimate=cost(12 * size * width, 4 * size),
        name="final",
    )(parts, col_scale, codes, far)
    packed = jnp.sum(exchange(packed, "y"), axis=0)
    away, near = pl.pallas_call(
        turn_kernel,
        in_specs=[smem] + [vmem] * 6 + [anywhere],
        out_specs=[vmem] * 2,
        out_shape=[f32(Z // 2, share, width)] * 2,
        scratch_shapes=[pltpu.VMEM((block, width), jnp.float32)],
        compiler_params=params(16 << 20),
        cost_estimate=cost(3 * block * width, 12 * block * width),
        name="turn",
    )(where, own_one, one, more_one, own_two, two, more_two, packed)
    near = near + swap(away, "z", Z, 1)
    numer, mass = pl.pallas_call(
        join_kernel,
        in_specs=[vmem] * 2 + [anywhere],
        out_specs=[vmem] * 2,
        out_shape=[f32(Y, group, width), f32(PAD, width)],
        compiler_params=params(),
        cost_estimate=cost(20000 * token_count * width, 8 * token_count * width),
        name="join",
    )(packed, swap(packed, "h", H, 1), near)
    near = add(near[:2], swap(near[2:], "z", Z, 2), mass)
    summed = near[0] + swap(near[1], "z", Z, 4)
    own = lax.dynamic_slice(mine, (0, 0, where[4]), (1, 1, share)).reshape(share)
    targets = summed * (own * (total_codes / total_tokens))[:, None]
    mass = mass[:2].reshape(2 * width)[:token_count]
    rebuilt = exchange(numer, "y").reshape(token_count, width) / mass[:, None]
    return (targets, rebuilt)


def solution(mesh):
    fine = Mesh(mesh.devices.reshape(Z, X, C, H, Y), AXES)
    return jax.shard_map(
        per_device,
        mesh=fine,
        in_specs=(P(("z", "x", "c"), None), P(("h", "y"), None)),
        out_specs=(P(("h", "y", "z", "x", "c"), None), P(("z", "x", "c"), None)),
        check_vma=False,
    )
```

```python
import functools

import jax
import jax.numpy as jnp
from jax import lax
from jax.experimental import pallas as pl
from jax.experimental.pallas import tpu as pltpu
from jax.sharding import Mesh, PartitionSpec as P

ITERS = 3
SHARP = 48.0
EPSILON = 1e-06

AXES = ("z", "x", "c", "h", "y")
Z, X, C, H, Y = 8, 4, 2, 2, 4
BLOCKS = C * X
LANES = 128
PAD = 8


def exchange(blocks, axes):
    return lax.all_to_all(blocks, axes, 0, 0, tiled=True)


FETCHES = 55_500_000
FETCHES_BESIDE_TILE = 40_000_000


def params(limit=8 << 20):
    return pltpu.CompilerParams(vmem_limit_bytes=limit)


def column_of(row):
    return jnp.broadcast_to(row, (LANES, row.shape[1])).T


def row_of(partial):
    return jnp.sum(partial.T, axis=0, keepdims=True)


def fold(product):
    total = product[:, :LANES]
    for start in range(LANES, product.shape[1], LANES):
        total = total + product[:, start : start + LANES]
    return total


def widen(column, width):
    return jnp.concatenate([column] * (width // LANES), axis=1)


def place(b):
    return (b % X) * C + b // X


AHEAD = 3


def fetch(steps, sems):
    copies, count = [], 0
    for pairs in steps:
        copies.append([pltpu.make_async_copy(*pair, sems.at[count + i]) for i, pair in enumerate(pairs)])
        count += len(pairs)

    def start(step):
        for copy in copies[step]:
            copy.start()

    def wait(step):
        if step + AHEAD < len(copies):
            start(step + AHEAD)
        for copy in copies[step]:
            copy.wait()

    for step in range(min(AHEAD, len(copies))):
        start(step)
    return wait


def setup_kernel(where_ref, latents_ref, codes_ref, tile_ref, rows_ref, far_ref, tokens_ref, held_ref, sems):
    del where_ref
    steps = [[(latents_ref, tokens_ref)]]
    wait = fetch(steps + [[(codes_ref.at[:, place(b)], held_ref.at[b])] for b in range(BLOCKS)], sems)
    wait(0)
    saves = []
    latents = tokens_ref[...]
    width = latents.shape[1]
    floats = latents.astype(jnp.float32)
    mean = jnp.sum(floats * floats, axis=1, keepdims=True) * (1.0 / width)
    scale = jnp.broadcast_to(lax.rsqrt(mean + EPSILON) * (SHARP / width), (latents.shape[0], LANES))
    total = jnp.zeros(scale.shape, jnp.float32)
    across = (((1,), (1,)), ((), ()))
    for b in range(BLOCKS):
        wait(1 + b)
        codes = held_ref[b].reshape(-1, width)
        floats = codes.astype(jnp.float32)
        code_norm = lax.rsqrt(row_of(fold(floats * floats)) * (1.0 / width) + EPSILON)
        inner = lax.dot_general(latents, codes, across, preferred_element_type=jnp.float32)
        tile = jnp.exp(inner * widen(scale, codes.shape[0]) * code_norm)
        tile_ref[b] = tile
        saves.append(pltpu.make_async_copy(tile_ref.at[b], far_ref.at[b], sems.at[BLOCKS + 1 + b]))
        saves[b].start()
        total += fold(tile)
    rows_ref[...] = jnp.broadcast_to(row_of(total)[None], rows_ref.shape)
    for save in saves:
        save.wait()


def rows_kernel(columns_ref, tile_ref, rows_ref, total_ref):
    step = pl.program_id(0)

    @pl.when(step == 0)
    def _():
        total_ref[...] = jnp.zeros_like(total_ref)

    total_ref[...] += fold(tile_ref[...] * columns_ref[...])

    @pl.when(step == pl.num_programs(0) - 1)
    def _():
        rows_ref[...] = jnp.broadcast_to(row_of(total_ref[...])[None], rows_ref.shape)


def row_scale_of(parts_ref):
    return column_of(1.0 / jnp.sum(parts_ref[...], axis=0))


def columns_kernel(parts_ref, tile_ref, columns_ref, scale_ref):
    @pl.when(pl.program_id(0) == 0)
    def _():
        scale_ref[...] = row_scale_of(parts_ref)

    tile = tile_ref[...]
    sums = jnp.sum(tile * widen(scale_ref[...], tile.shape[1]), axis=0, keepdims=True)
    columns_ref[pl.program_id(0)] = sums


def targets_part(tile, scale, latents):
    weighted = (tile * widen(scale, tile.shape[1])).astype(jnp.bfloat16)
    return lax.dot_general(latents, weighted, (((0,), (0,)), ((), ())), preferred_element_type=jnp.float32)


def targets_sent_kernel(where_ref, parts_ref, latents_ref, tile_ref, after_ref, out_ref, tiles_ref, sems):
    del after_ref
    wait = fetch([[(tile_ref.at[where_ref[3] * X + (where_ref[1] ^ s)], tiles_ref.at[s])] for s in range(X)], sems)
    scale = row_scale_of(parts_ref)
    latents = latents_ref[...]
    for s in range(X):
        wait(s)
        out_ref[s] = targets_part(tiles_ref[s], scale, latents)


def targets_kept_kernel(
    where_ref, parts_ref, latents_ref, tile_ref, added_ref, after_ref,
    one_ref, two_ref, own_one_ref, own_two_ref, tiles_ref, more_ref, sems,
):
    del after_ref
    steps = [
        [(tile_ref.at[where_ref[0] * X + (where_ref[1] ^ s)], tiles_ref.at[s]), (added_ref.at[s], more_ref.at[s])]
        for s in range(X)
    ]
    wait = fetch(steps, sems)
    scale = row_scale_of(parts_ref)
    latents = latents_ref[...]
    for s in range(X):
        wait(s)
        summed = targets_part(tiles_ref[s], scale, latents) + more_ref[s]
        upper, lower = jnp.split(summed, 2, axis=0)
        ref, index = ((own_one_ref, 0), (one_ref, 0), (one_ref, 1), (own_one_ref, 1))[s]
        ref[index] = upper
        ref, index = ((own_two_ref, 0), (own_two_ref, 1), (two_ref, 1), (two_ref, 0))[s]
        ref[index] = lower


def sum_kernel(parts_ref, *refs):
    out_ref = refs[-1]
    out_ref[...] = jnp.broadcast_to(jnp.sum(parts_ref[...], axis=0, keepdims=True), out_ref.shape)


def gather_kernel(parts_ref, after_ref, out_ref):
    del after_ref
    out_ref[...] = jnp.sum(parts_ref[...], axis=0)


def inverse_kernel(factor, parts_ref, *refs):
    out_ref = refs[-1]
    out_ref[...] = jnp.broadcast_to(factor / jnp.sum(parts_ref[...], axis=0, keepdims=True), out_ref.shape)


def add_kernel(kept_ref, came_ref, after_ref, out_ref):
    del after_ref
    out_ref[...] = kept_ref[...] + came_ref[...]


def join_kernel(kept_ref, came_ref, after_ref, spread_ref, mass_ref):
    del after_ref
    total = kept_ref[...] + came_ref[...]
    group = spread_ref.shape[1]
    spread_ref[...] = jnp.broadcast_to(total[None, :group], spread_ref.shape)
    mass_ref[...] = total[group:]


def turn_kernel(where_ref, own_one_ref, one_ref, more_one_ref, own_two_ref, two_ref, more_two_ref, *refs):
    send_ref, keep_ref, turned_ref = refs
    upper = own_one_ref[0] + one_ref[0] + more_one_ref[...]
    lower = own_two_ref[0] + two_ref[0] + more_two_ref[...]
    turned_ref[...] = jnp.concatenate([upper, lower], axis=0).T
    share = send_ref.shape[1]
    for i, slot in enumerate((0, 4, 2, 6)):
        for ref, s in ((keep_ref, slot), (send_ref, slot + 1)):
            start = pl.multiple_of((where_ref[2] ^ s) * share, share)
            ref[i] = turned_ref[pl.ds(start, share), :]


def final_kernel(
    parts_ref, columns_ref, codes_ref, tile_ref, more_one_ref, more_two_ref,
    out_ref, held_ref, tiles_ref, numer_ref, sems,
):
    del more_one_ref, more_two_ref
    steps = [
        [(tile_ref.at[b], tiles_ref.at[b]), (codes_ref.at[:, place(b)], held_ref.at[b])] for b in range(BLOCKS)
    ]
    wait = fetch(steps, sems)
    tokens, width = numer_ref.shape
    scale = row_scale_of(parts_ref)
    total = jnp.zeros(scale.shape, jnp.float32)
    for b in range(BLOCKS):
        wait(b)
        tile = tiles_ref[b]
        plan = (widen(scale, tile.shape[1]) * tile * columns_ref[b]).astype(jnp.bfloat16)
        total += fold(plan.astype(jnp.float32))
        part = jnp.dot(plan, held_ref[b].reshape(-1, width), preferred_element_type=jnp.float32)
        numer_ref[...] = part if b == 0 else numer_ref[...] + part
    group = tokens // Y
    mass = row_of(total)
    mass = jnp.concatenate([mass, jnp.zeros((1, 2 * width - tokens), jnp.float32)], axis=1)
    extra = jnp.concatenate(
        [mass[:, :width], mass[:, width:], jnp.zeros((PAD - 2, width), jnp.float32)], axis=0
    )
    for y in range(Y):
        out_ref[y, :group, :] = numer_ref[y * group : (y + 1) * group, :]
        out_ref[y, group:, :] = extra


def f32(*shape):
    return jax.ShapeDtypeStruct(shape, jnp.float32)


def whole(*shape):
    return pl.BlockSpec(shape, lambda *_: (0,) * len(shape))


def cost(flops, moved, exps=0):
    return pl.CostEstimate(flops=flops, bytes_accessed=moved, transcendentals=exps)


def per_device(latents, codebook):
    token_count, width = latents.shape
    code_count = codebook.shape[0]
    total_tokens = token_count * Z * X * C
    total_codes = code_count * H * Y
    share = code_count // (Z * X * C)
    block = code_count // BLOCKS
    size = token_count * code_count

    codes = codebook.reshape(Z, X * C, share, width)
    tile_spec = pl.BlockSpec((None, token_count, block), lambda b: (b, 0, 0))
    rows_spec = whole(H * Y, 1, token_count)
    columns_spec = pl.BlockSpec((None, 1, block), lambda b: (b, 0, 0))
    vmem = pl.BlockSpec(memory_space=pltpu.VMEM)
    smem = pl.BlockSpec(memory_space=pltpu.SMEM)
    hbm = pl.BlockSpec(memory_space=pltpu.HBM)
    anywhere = pl.BlockSpec(memory_space=pl.ANY)
    per_token = pltpu.VMEM((token_count, LANES), jnp.float32)
    held = pltpu.VMEM((BLOCKS, Z, share, width), jnp.bfloat16)
    tiles = functools.partial(pltpu.VMEM, dtype=jnp.float32)
    rows_shape = f32(H * Y, 1, token_count)
    columns_shape = f32(BLOCKS, 1, block)

    core, x, z = (lax.axis_index(axis) for axis in ("c", "x", "z"))
    where = jnp.stack([core, x, z, 1 - core, z * share])

    tile, part, far = pl.pallas_call(
        setup_kernel,
        in_specs=[smem, hbm, hbm],
        out_specs=[vmem, vmem, hbm],
        out_shape=[f32(BLOCKS, token_count, block), rows_shape, f32(BLOCKS, token_count, block)],
        scratch_shapes=[
            pltpu.VMEM((token_count, width), jnp.bfloat16),
            held,
            pltpu.SemaphoreType.DMA((2 * BLOCKS + 1,)),
        ],
        compiler_params=params(FETCHES_BESIDE_TILE),
        cost_estimate=cost(2 * size * width, 4 * size, size),
        name="setup",
    )(where, latents, codes)

    def rows(columns):
        return pl.pallas_call(
            rows_kernel,
            grid=(BLOCKS,),
            in_specs=[columns_spec, tile_spec],
            out_specs=rows_spec,
            out_shape=rows_shape,
            scratch_shapes=[per_token],
            compiler_params=params(),
            cost_estimate=cost(2 * size, 4 * size),
            name="rows",
        )(columns, tile)

    def columns(parts):
        return pl.pallas_call(
            columns_kernel,
            grid=(BLOCKS,),
            in_specs=[rows_spec, tile_spec],
            out_specs=whole(BLOCKS, 1, block),
            out_shape=columns_shape,
            scratch_shapes=[per_token],
            compiler_params=params(),
            cost_estimate=cost(2 * size, 4 * size),
            name="columns",
        )(parts, tile)

    def targets_sent(parts, after):
        return pl.pallas_call(
            targets_sent_kernel,
            in_specs=[smem, vmem, vmem, hbm, anywhere],
            out_specs=vmem,
            out_shape=f32(X, width, block),
            scratch_shapes=[tiles((X, token_count, block)), pltpu.SemaphoreType.DMA((X,))],
            compiler_params=params(FETCHES),
            cost_estimate=cost(size * width, 4 * size),
            name="targets_sent",
        )(where, parts, latents, far, after)

    def targets_kept(parts, added, after):
        return pl.pallas_call(
            targets_kept_kernel,
            in_specs=[smem, vmem, vmem, hbm, hbm, anywhere],
            out_specs=[vmem] * 4,
            out_shape=[f32(2, width // 2, block)] * 4,
            scratch_shapes=[
                tiles((X, token_count, block)),
                tiles((X, width, block)),
                pltpu.SemaphoreType.DMA((2 * X,)),
            ],
            compiler_params=params(FETCHES),
            cost_estimate=cost(size * width, 4 * size),
            name="targets_kept",
        )(where, parts, latents, far, added, after)

    def small(kernel, name, count, weight, parts, *after):
        return pl.pallas_call(
            kernel,
            in_specs=[vmem] + [anywhere] * len(after),
            out_specs=vmem,
            out_shape=f32(count, 1, block),
            compiler_params=params(),
            cost_estimate=cost(weight * parts.size, 4 * parts.size),
            name=name,
        )(parts, *after)

    inverse = functools.partial(inverse_kernel, total_tokens / total_codes)
    def swap(value, axis, count, bits):
        return lax.ppermute(value, axis, [(i, i ^ bits) for i in range(count)])

    def add(kept, came, after):
        return pl.pallas_call(
            add_kernel,
            in_specs=[vmem] * 2 + [anywhere],
            out_specs=vmem,
            out_shape=f32(*kept.shape),
            compiler_params=params(),
            cost_estimate=cost(kept.size, 12 * kept.size),
            name="add",
        )(kept, came, after)

    for sweep_index in range(ITERS):
        last = sweep_index == ITERS - 1
        parts = exchange(part, ("h", "y"))
        column_sums = columns(parts)
        if last:
            sent = targets_sent(parts, column_sums)
        sums = small(sum_kernel, "sums", Z, 20_000_000 if last else 1, exchange(column_sums, ("c", "x")))
        if last:
            kept = targets_kept(parts, swap(sent, "c", C, 1), sums)
        after = (kept[0],) if last else ()
        mine = small(inverse, "inverse", BLOCKS, 2_000_000 if last else 1, exchange(sums, "z"), *after)
        col_scale = exchange(mine, ("c", "x"))
        if not last:
            part = rows(col_scale)

    one, two, own_one, own_two = kept
    one, two = swap(one, "x", X, 1), swap(two, "x", X, 3)
    more_one, more_two = own_one[1] + one[1], own_two[1] + two[1]

    group = token_count // Y
    packed = pl.pallas_call(
        final_kernel,
        in_specs=[vmem, vmem, hbm, hbm, anywhere, anywhere],
        out_specs=vmem,
        out_shape=f32(Y, group + PAD, width),
        scratch_shapes=[
            held,
            tiles((BLOCKS, token_count, block)),
            tiles((token_count, width)),
            pltpu.SemaphoreType.DMA((2 * BLOCKS,)),
        ],
        compiler_params=params(FETCHES),
        cost_estimate=cost(12 * size * width, 4 * size),
        name="final",
    )(parts, col_scale, codes, far, more_one, more_two)
    more_one, more_two = swap(more_one, "x", X, 3), swap(more_two, "x", X, 1)
    away, near = pl.pallas_call(
        turn_kernel,
        in_specs=[smem] + [vmem] * 6,
        out_specs=[vmem] * 2,
        out_shape=[f32(Z // 2, share, width)] * 2,
        scratch_shapes=[pltpu.VMEM((block, width), jnp.float32)],
        compiler_params=params(16 << 20),
        cost_estimate=cost(3 * block * width, 12 * block * width),
        name="turn",
    )(where, own_one, one, more_one, own_two, two, more_two)
    packed = pl.pallas_call(
        gather_kernel,
        in_specs=[vmem, anywhere],
        out_specs=vmem,
        out_shape=f32(group + PAD, width),
        compiler_params=params(),
        cost_estimate=cost(packed.size, 4 * packed.size),
        name="gathered",
    )(exchange(packed, "y"), away)
    near = near + swap(away, "z", Z, 1)
    numer, mass = pl.pallas_call(
        join_kernel,
        in_specs=[vmem] * 2 + [anywhere],
        out_specs=[vmem] * 2,
        out_shape=[f32(Y, group, width), f32(PAD, width)],
        compiler_params=params(),
        cost_estimate=cost(20000 * token_count * width, 8 * token_count * width),
        name="join",
    )(packed, swap(packed, "h", H, 1), near)
    near = add(near[:2], swap(near[2:], "z", Z, 2), mass)
    summed = near[0] + swap(near[1], "z", Z, 4)
    own = lax.dynamic_slice(mine, (0, 0, where[4]), (1, 1, share)).reshape(share)
    targets = summed * (own * (total_codes / total_tokens))[:, None]
    mass = mass[:2].reshape(2 * width)[:token_count]
    rebuilt = exchange(numer, "y").reshape(token_count, width) / mass[:, None]
    return (targets, rebuilt)


def solution(mesh):
    fine = Mesh(mesh.devices.reshape(Z, X, C, H, Y), AXES)
    return jax.shard_map(
        per_device,
        mesh=fine,
        in_specs=(P(("z", "x", "c"), None), P(("h", "y"), None)),
        out_specs=(P(("h", "y", "z", "x", "c"), None), P(("z", "x", "c"), None)),
        check_vma=False,
    )
```

```python
import functools

import jax
import jax.numpy as jnp
from jax import lax
from jax.experimental import pallas as pl
from jax.experimental.pallas import tpu as pltpu
from jax.sharding import Mesh, PartitionSpec as P

ITERS = 3
SHARP = 48.0
EPSILON = 1e-06

AXES = ("z", "x", "c", "h", "y")
Z, X, C, H, Y = 8, 4, 2, 2, 4
BLOCKS = C * X
LANES = 128
PAD = 8


def exchange(blocks, axes):
    return lax.all_to_all(blocks, axes, 0, 0, tiled=True)


FETCHES = 55_500_000
FETCHES_BESIDE_TILE = 40_000_000
FETCHES_BESIDE_SUMS = 53_000_000


def params(limit=8 << 20):
    return pltpu.CompilerParams(vmem_limit_bytes=limit)


def column_of(row):
    return jnp.broadcast_to(row, (LANES, row.shape[1])).T


def row_of(partial):
    return jnp.sum(partial.T, axis=0, keepdims=True)


def fold(product):
    total = product[:, :LANES]
    for start in range(LANES, product.shape[1], LANES):
        total = total + product[:, start : start + LANES]
    return total


def widen(column, width):
    return jnp.concatenate([column] * (width // LANES), axis=1)


def place(b):
    return (b % X) * C + b // X


AHEAD = 3


def fetch(steps, sems):
    copies, count = [], 0
    for pairs in steps:
        copies.append([pltpu.make_async_copy(*pair, sems.at[count + i]) for i, pair in enumerate(pairs)])
        count += len(pairs)

    def start(step):
        for copy in copies[step]:
            copy.start()

    def wait(step):
        if step + AHEAD < len(copies):
            start(step + AHEAD)
        for copy in copies[step]:
            copy.wait()

    for step in range(min(AHEAD, len(copies))):
        start(step)
    return wait


def setup_kernel(where_ref, latents_ref, codes_ref, tile_ref, rows_ref, far_ref, tokens_ref, held_ref, sems):
    del where_ref
    steps = [[(latents_ref, tokens_ref)]]
    wait = fetch(steps + [[(codes_ref.at[:, place(b)], held_ref.at[b])] for b in range(BLOCKS)], sems)
    wait(0)
    saves = []
    latents = tokens_ref[...]
    width = latents.shape[1]
    floats = latents.astype(jnp.float32)
    mean = jnp.sum(floats * floats, axis=1, keepdims=True) * (1.0 / width)
    scale = jnp.broadcast_to(lax.rsqrt(mean + EPSILON) * (SHARP / width), (latents.shape[0], LANES))
    total = jnp.zeros(scale.shape, jnp.float32)
    across = (((1,), (1,)), ((), ()))
    for b in range(BLOCKS):
        wait(1 + b)
        codes = held_ref[b].reshape(-1, width)
        floats = codes.astype(jnp.float32)
        code_norm = lax.rsqrt(row_of(fold(floats * floats)) * (1.0 / width) + EPSILON)
        inner = lax.dot_general(latents, codes, across, preferred_element_type=jnp.float32)
        tile = jnp.exp(inner * widen(scale, codes.shape[0]) * code_norm)
        tile_ref[b] = tile
        saves.append(pltpu.make_async_copy(tile_ref.at[b], far_ref.at[b], sems.at[BLOCKS + 1 + b]))
        saves[b].start()
        total += fold(tile)
    rows_ref[...] = jnp.broadcast_to(row_of(total)[None], rows_ref.shape)
    for save in saves:
        save.wait()


def rows_kernel(columns_ref, tile_ref, rows_ref, total_ref):
    step = pl.program_id(0)

    @pl.when(step == 0)
    def _():
        total_ref[...] = jnp.zeros_like(total_ref)

    total_ref[...] += fold(tile_ref[...] * columns_ref[...])

    @pl.when(step == pl.num_programs(0) - 1)
    def _():
        rows_ref[...] = jnp.broadcast_to(row_of(total_ref[...])[None], rows_ref.shape)


def row_scale_of(parts_ref):
    return column_of(1.0 / jnp.sum(parts_ref[...], axis=0))


def columns_kernel(parts_ref, tile_ref, columns_ref, scale_ref):
    @pl.when(pl.program_id(0) == 0)
    def _():
        scale_ref[...] = row_scale_of(parts_ref)

    tile = tile_ref[...]
    sums = jnp.sum(tile * widen(scale_ref[...], tile.shape[1]), axis=0, keepdims=True)
    columns_ref[pl.program_id(0)] = sums


def targets_part(tile, scale, latents):
    weighted = (tile * widen(scale, tile.shape[1])).astype(jnp.bfloat16)
    return lax.dot_general(latents, weighted, (((0,), (0,)), ((), ())), preferred_element_type=jnp.float32)


def leave(pieces, sems, first):
    copies = [pltpu.make_async_copy(*piece, sems.at[first + i]) for i, piece in enumerate(pieces)]
    for copy in copies:
        copy.start()
    return copies


def targets_sent_kernel(where_ref, parts_ref, latents_ref, tile_ref, after_ref, out_ref, tiles_ref, done_ref, sems):
    del after_ref
    wait = fetch([[(tile_ref.at[where_ref[3] * X + (where_ref[1] ^ s)], tiles_ref.at[s])] for s in range(X)], sems)
    scale = row_scale_of(parts_ref)
    latents = latents_ref[...]
    copies = []
    for s in range(X):
        wait(s)
        done_ref[s] = targets_part(tiles_ref[s], scale, latents)
        copies += leave([(done_ref.at[s], out_ref.at[s])], sems, X + s)
    for copy in copies:
        copy.wait()


def targets_kept_kernel(
    where_ref, parts_ref, latents_ref, tile_ref, added_ref, after_ref,
    one_ref, two_ref, own_one_ref, own_two_ref, tiles_ref, more_ref, done_ref, sems,
):
    del after_ref
    steps = [
        [(tile_ref.at[where_ref[0] * X + (where_ref[1] ^ s)], tiles_ref.at[s]), (added_ref.at[s], more_ref.at[s])]
        for s in range(X)
    ]
    wait = fetch(steps, sems)
    scale = row_scale_of(parts_ref)
    latents = latents_ref[...]
    half = latents.shape[1] // 2
    uppers = (own_one_ref.at[0], one_ref.at[0], one_ref.at[1], own_one_ref.at[1])
    lowers = (own_two_ref.at[0], own_two_ref.at[1], two_ref.at[1], two_ref.at[0])
    copies = []
    for s in range(X):
        wait(s)
        done_ref[s] = targets_part(tiles_ref[s], scale, latents) + more_ref[s]
        pieces = [(done_ref.at[s, :half], uppers[s]), (done_ref.at[s, half:], lowers[s])]
        copies += leave(pieces, sems, 2 * X + 2 * s)
    for copy in copies:
        copy.wait()


def sum_kernel(parts_ref, *refs):
    out_ref = refs[-1]
    out_ref[...] = jnp.broadcast_to(jnp.sum(parts_ref[...], axis=0, keepdims=True), out_ref.shape)


def gather_kernel(parts_ref, after_ref, out_ref):
    del after_ref
    out_ref[...] = jnp.sum(parts_ref[...], axis=0)


def inverse_kernel(factor, parts_ref, *refs):
    out_ref = refs[-1]
    out_ref[...] = jnp.broadcast_to(factor / jnp.sum(parts_ref[...], axis=0, keepdims=True), out_ref.shape)


def join_kernel(kept_ref, came_ref, after_ref, spread_ref, mass_ref):
    del after_ref
    total = kept_ref[...] + came_ref[...]
    group = spread_ref.shape[1]
    spread_ref[...] = jnp.broadcast_to(total[None, :group], spread_ref.shape)
    mass_ref[...] = total[group:]


def turn_kernel(where_ref, own_one_ref, one_ref, more_one_ref, own_two_ref, two_ref, more_two_ref, *refs):
    send_ref, keep_ref, turned_ref = refs
    upper = own_one_ref[0] + one_ref[0] + more_one_ref[...]
    lower = own_two_ref[0] + two_ref[0] + more_two_ref[...]
    turned_ref[...] = jnp.concatenate([upper, lower], axis=0).T
    share = send_ref.shape[1]
    for i, slot in enumerate((0, 4, 2, 6)):
        for ref, s in ((keep_ref, slot), (send_ref, slot + 1)):
            start = pl.multiple_of((where_ref[2] ^ s) * share, share)
            ref[i] = turned_ref[pl.ds(start, share), :]


def final_kernel(
    parts_ref, columns_ref, codes_ref, tile_ref, more_one_ref, more_two_ref,
    out_ref, held_ref, tiles_ref, numer_ref, sems,
):
    del more_one_ref, more_two_ref
    steps = [
        [(tile_ref.at[b], tiles_ref.at[b]), (codes_ref.at[:, place(b)], held_ref.at[b])] for b in range(BLOCKS)
    ]
    wait = fetch(steps, sems)
    tokens, width = numer_ref.shape
    scale = row_scale_of(parts_ref)
    total = jnp.zeros(scale.shape, jnp.float32)
    for b in range(BLOCKS):
        wait(b)
        tile = tiles_ref[b]
        plan = (widen(scale, tile.shape[1]) * tile * columns_ref[b]).astype(jnp.bfloat16)
        total += fold(plan.astype(jnp.float32))
        part = jnp.dot(plan, held_ref[b].reshape(-1, width), preferred_element_type=jnp.float32)
        numer_ref[...] = part if b == 0 else numer_ref[...] + part
    group = tokens // Y
    mass = row_of(total)
    mass = jnp.concatenate([mass, jnp.zeros((1, 2 * width - tokens), jnp.float32)], axis=1)
    extra = jnp.concatenate(
        [mass[:, :width], mass[:, width:], jnp.zeros((PAD - 2, width), jnp.float32)], axis=0
    )
    for y in range(Y):
        out_ref[y, :group, :] = numer_ref[y * group : (y + 1) * group, :]
        out_ref[y, group:, :] = extra


def f32(*shape):
    return jax.ShapeDtypeStruct(shape, jnp.float32)


def whole(*shape):
    return pl.BlockSpec(shape, lambda *_: (0,) * len(shape))


def cost(flops, moved, exps=0):
    return pl.CostEstimate(flops=flops, bytes_accessed=moved, transcendentals=exps)


def per_device(latents, codebook):
    token_count, width = latents.shape
    code_count = codebook.shape[0]
    total_tokens = token_count * Z * X * C
    total_codes = code_count * H * Y
    share = code_count // (Z * X * C)
    block = code_count // BLOCKS
    size = token_count * code_count

    codes = codebook.reshape(Z, X * C, share, width)
    tile_spec = pl.BlockSpec((None, token_count, block), lambda b: (b, 0, 0))
    rows_spec = whole(H * Y, 1, token_count)
    columns_spec = pl.BlockSpec((None, 1, block), lambda b: (b, 0, 0))
    vmem = pl.BlockSpec(memory_space=pltpu.VMEM)
    smem = pl.BlockSpec(memory_space=pltpu.SMEM)
    hbm = pl.BlockSpec(memory_space=pltpu.HBM)
    anywhere = pl.BlockSpec(memory_space=pl.ANY)
    per_token = pltpu.VMEM((token_count, LANES), jnp.float32)
    held = pltpu.VMEM((BLOCKS, Z, share, width), jnp.bfloat16)
    tiles = functools.partial(pltpu.VMEM, dtype=jnp.float32)
    rows_shape = f32(H * Y, 1, token_count)
    columns_shape = f32(BLOCKS, 1, block)

    core, x, z = (lax.axis_index(axis) for axis in ("c", "x", "z"))
    where = jnp.stack([core, x, z, 1 - core, z * share])

    tile, part, far = pl.pallas_call(
        setup_kernel,
        in_specs=[smem, hbm, hbm],
        out_specs=[vmem, vmem, hbm],
        out_shape=[f32(BLOCKS, token_count, block), rows_shape, f32(BLOCKS, token_count, block)],
        scratch_shapes=[
            pltpu.VMEM((token_count, width), jnp.bfloat16),
            held,
            pltpu.SemaphoreType.DMA((2 * BLOCKS + 1,)),
        ],
        compiler_params=params(FETCHES_BESIDE_TILE),
        cost_estimate=cost(2 * size * width, 4 * size, size),
        name="setup",
    )(where, latents, codes)

    def rows(columns):
        return pl.pallas_call(
            rows_kernel,
            grid=(BLOCKS,),
            in_specs=[columns_spec, tile_spec],
            out_specs=rows_spec,
            out_shape=rows_shape,
            scratch_shapes=[per_token],
            compiler_params=params(),
            cost_estimate=cost(2 * size, 4 * size),
            name="rows",
        )(columns, tile)

    def columns(parts):
        return pl.pallas_call(
            columns_kernel,
            grid=(BLOCKS,),
            in_specs=[rows_spec, tile_spec],
            out_specs=whole(BLOCKS, 1, block),
            out_shape=columns_shape,
            scratch_shapes=[per_token],
            compiler_params=params(),
            cost_estimate=cost(2 * size, 4 * size),
            name="columns",
        )(parts, tile)

    def targets_sent(parts, after):
        return pl.pallas_call(
            targets_sent_kernel,
            in_specs=[smem, vmem, vmem, hbm, anywhere],
            out_specs=hbm,
            out_shape=f32(X, width, block),
            scratch_shapes=[
                tiles((X, token_count, block)),
                tiles((X, width, block)),
                pltpu.SemaphoreType.DMA((2 * X,)),
            ],
            compiler_params=params(FETCHES),
            cost_estimate=cost(size * width, 4 * size),
            name="targets_sent",
        )(where, parts, latents, far, after)

    def targets_kept(parts, added, after):
        return pl.pallas_call(
            targets_kept_kernel,
            in_specs=[smem, vmem, vmem, hbm, anywhere, anywhere],
            out_specs=[hbm] * 4,
            out_shape=[f32(2, width // 2, block)] * 4,
            scratch_shapes=[
                tiles((X, token_count, block)),
                tiles((X, width, block)),
                tiles((X, width, block)),
                pltpu.SemaphoreType.DMA((4 * X,)),
            ],
            compiler_params=params(FETCHES_BESIDE_SUMS),
            cost_estimate=cost(size * width, 4 * size),
            name="targets_kept",
        )(where, parts, latents, far, added, after)

    def small(kernel, name, count, weight, parts, *after):
        return pl.pallas_call(
            kernel,
            in_specs=[vmem] + [anywhere] * len(after),
            out_specs=vmem,
            out_shape=f32(count, 1, block),
            compiler_params=params(),
            cost_estimate=cost(weight * parts.size, 4 * parts.size),
            name=name,
        )(parts, *after)

    inverse = functools.partial(inverse_kernel, total_tokens / total_codes)
    def swap(value, axis, count, bits):
        return lax.ppermute(value, axis, [(i, i ^ bits) for i in range(count)])

    for sweep_index in range(ITERS):
        last = sweep_index == ITERS - 1
        parts = exchange(part, ("h", "y"))
        column_sums = columns(parts)
        if last:
            sent = targets_sent(parts, column_sums)
        sums = small(sum_kernel, "sums", Z, 20_000_000 if last else 1, exchange(column_sums, ("c", "x")))
        if last:
            kept = targets_kept(parts, swap(sent, "c", C, 1), sums)
        after = (kept[0],) if last else ()
        mine = small(inverse, "inverse", BLOCKS, 2_000_000 if last else 1, exchange(sums, "z"), *after)
        col_scale = exchange(mine, ("c", "x"))
        if not last:
            part = rows(col_scale)

    one, two, own_one, own_two = kept
    one, two = swap(one, "x", X, 1), swap(two, "x", X, 3)
    more_one, more_two = own_one[1] + one[1], own_two[1] + two[1]

    group = token_count // Y
    packed = pl.pallas_call(
        final_kernel,
        in_specs=[vmem, vmem, hbm, hbm, anywhere, anywhere],
        out_specs=vmem,
        out_shape=f32(Y, group + PAD, width),
        scratch_shapes=[
            held,
            tiles((BLOCKS, token_count, block)),
            tiles((token_count, width)),
            pltpu.SemaphoreType.DMA((2 * BLOCKS,)),
        ],
        compiler_params=params(FETCHES),
        cost_estimate=cost(12 * size * width, 4 * size),
        name="final",
    )(parts, col_scale, codes, far, more_one, more_two)
    more_one, more_two = swap(more_one, "x", X, 3), swap(more_two, "x", X, 1)
    away, near = pl.pallas_call(
        turn_kernel,
        in_specs=[smem] + [vmem] * 6,
        out_specs=[vmem] * 2,
        out_shape=[f32(Z // 2, share, width)] * 2,
        scratch_shapes=[pltpu.VMEM((block, width), jnp.float32)],
        compiler_params=params(16 << 20),
        cost_estimate=cost(3 * block * width, 12 * block * width),
        name="turn",
    )(where, own_one, one, more_one, own_two, two, more_two)
    packed = pl.pallas_call(
        gather_kernel,
        in_specs=[vmem, anywhere],
        out_specs=vmem,
        out_shape=f32(group + PAD, width),
        compiler_params=params(),
        cost_estimate=cost(packed.size, 4 * packed.size),
        name="gathered",
    )(exchange(packed, "y"), away)
    near = near + swap(away, "z", Z, 1)
    numer, mass = pl.pallas_call(
        join_kernel,
        in_specs=[vmem] * 2 + [anywhere],
        out_specs=[vmem] * 2,
        out_shape=[f32(Y, group, width), f32(PAD, width)],
        compiler_params=params(),
        cost_estimate=cost(20000 * token_count * width, 8 * token_count * width),
        name="join",
    )(packed, swap(packed, "h", H, 1), near)
    near = near[:2] + swap(near[2:], "z", Z, 2)
    summed = near[0] + swap(near[1], "z", Z, 4)
    own = lax.dynamic_slice(mine, (0, 0, where[4]), (1, 1, share)).reshape(share)
    targets = summed * (own * (total_codes / total_tokens))[:, None]
    mass = mass[:2].reshape(2 * width)[:token_count]
    rebuilt = exchange(numer, "y").reshape(token_count, width) / mass[:, None]
    return (targets, rebuilt)


def solution(mesh):
    fine = Mesh(mesh.devices.reshape(Z, X, C, H, Y), AXES)
    return jax.shard_map(
        per_device,
        mesh=fine,
        in_specs=(P(("z", "x", "c"), None), P(("h", "y"), None)),
        out_specs=(P(("h", "y", "z", "x", "c"), None), P(("z", "x", "c"), None)),
        check_vma=False,
    )
```

```python
import functools

import jax
import jax.numpy as jnp
from jax import lax
from jax.experimental import pallas as pl
from jax.experimental.pallas import tpu as pltpu
from jax.sharding import Mesh, PartitionSpec as P

ITERS = 3
SHARP = 48.0
EPSILON = 1e-06

AXES = ("z", "x", "c", "h", "y")
Z, X, C, H, Y = 8, 4, 2, 2, 4
BLOCKS = C * X
LANES = 128
PAD = 8


def exchange(blocks, axes):
    return lax.all_to_all(blocks, axes, 0, 0, tiled=True)


FETCHES = 55_500_000
FETCHES_BESIDE_SUMS = 53_000_000


def params(limit=8 << 20):
    return pltpu.CompilerParams(vmem_limit_bytes=limit)


def column_of(row):
    return jnp.broadcast_to(row, (LANES, row.shape[1])).T


def row_of(partial):
    return jnp.sum(partial.T, axis=0, keepdims=True)


def fold(product):
    total = product[:, :LANES]
    for start in range(LANES, product.shape[1], LANES):
        total = total + product[:, start : start + LANES]
    return total


def widen(column, width):
    return jnp.concatenate([column] * (width // LANES), axis=1)


def place(b):
    return (b % X) * C + b // X


AHEAD = 3


def fetch(steps, sems):
    copies, count = [], 0
    for pairs in steps:
        copies.append([pltpu.make_async_copy(*pair, sems.at[count + i]) for i, pair in enumerate(pairs)])
        count += len(pairs)

    def start(step):
        for copy in copies[step]:
            copy.start()

    def wait(step):
        if step + AHEAD < len(copies):
            start(step + AHEAD)
        for copy in copies[step]:
            copy.wait()

    for step in range(min(AHEAD, len(copies))):
        start(step)
    return wait


def setup_kernel(where_ref, latents_ref, codes_ref, tile_ref, rows_ref):
    del where_ref
    latents = latents_ref[...]
    width = latents.shape[1]
    floats = latents.astype(jnp.float32)
    mean = jnp.sum(floats * floats, axis=1, keepdims=True) * (1.0 / width)
    scale = jnp.broadcast_to(lax.rsqrt(mean + EPSILON) * (SHARP / width), (latents.shape[0], LANES))
    total = jnp.zeros(scale.shape, jnp.float32)
    across = (((1,), (1,)), ((), ()))
    for b in range(BLOCKS):
        codes = codes_ref[:, place(b)].reshape(-1, width)
        floats = codes.astype(jnp.float32)
        code_norm = lax.rsqrt(row_of(fold(floats * floats)) * (1.0 / width) + EPSILON)
        inner = lax.dot_general(latents, codes, across, preferred_element_type=jnp.float32)
        tile = jnp.exp(inner * widen(scale, codes.shape[0]) * code_norm)
        tile_ref[b] = tile
        total += fold(tile)
    rows_ref[...] = jnp.broadcast_to(row_of(total)[None], rows_ref.shape)


def rows_kernel(columns_ref, tile_ref, rows_ref, total_ref):
    step = pl.program_id(0)

    @pl.when(step == 0)
    def _():
        total_ref[...] = jnp.zeros_like(total_ref)

    total_ref[...] += fold(tile_ref[...] * columns_ref[...])

    @pl.when(step == pl.num_programs(0) - 1)
    def _():
        rows_ref[...] = jnp.broadcast_to(row_of(total_ref[...])[None], rows_ref.shape)


def row_scale_of(parts_ref):
    return column_of(1.0 / jnp.sum(parts_ref[...], axis=0))


def columns_kernel(parts_ref, tile_ref, columns_ref, scale_ref):
    @pl.when(pl.program_id(0) == 0)
    def _():
        scale_ref[...] = row_scale_of(parts_ref)

    tile = tile_ref[...]
    sums = jnp.sum(tile * widen(scale_ref[...], tile.shape[1]), axis=0, keepdims=True)
    columns_ref[pl.program_id(0)] = sums


def targets_part(tile, scale, latents):
    weighted = (tile * widen(scale, tile.shape[1])).astype(jnp.bfloat16)
    return lax.dot_general(latents, weighted, (((0,), (0,)), ((), ())), preferred_element_type=jnp.float32)


def leave(pieces, sems, first):
    copies = [pltpu.make_async_copy(*piece, sems.at[first + i]) for i, piece in enumerate(pieces)]
    for copy in copies:
        copy.start()
    return copies


def targets_sent_kernel(where_ref, parts_ref, latents_ref, tile_ref, after_ref, out_ref, tiles_ref, done_ref, sems):
    del after_ref
    wait = fetch([[(tile_ref.at[where_ref[3] * X + (where_ref[1] ^ s)], tiles_ref.at[s])] for s in range(X)], sems)
    scale = row_scale_of(parts_ref)
    latents = latents_ref[...]
    copies = []
    for s in range(X):
        wait(s)
        done_ref[s] = targets_part(tiles_ref[s], scale, latents)
        copies += leave([(done_ref.at[s], out_ref.at[s])], sems, X + s)
    for copy in copies:
        copy.wait()


def targets_kept_kernel(
    where_ref, parts_ref, latents_ref, tile_ref, added_ref, after_ref,
    one_ref, two_ref, own_one_ref, own_two_ref, tiles_ref, more_ref, done_ref, sems,
):
    del after_ref
    steps = [
        [(tile_ref.at[where_ref[0] * X + (where_ref[1] ^ s)], tiles_ref.at[s]), (added_ref.at[s], more_ref.at[s])]
        for s in range(X)
    ]
    wait = fetch(steps, sems)
    scale = row_scale_of(parts_ref)
    latents = latents_ref[...]
    half = latents.shape[1] // 2
    uppers = (own_one_ref.at[0], one_ref.at[0], one_ref.at[1], own_one_ref.at[1])
    lowers = (own_two_ref.at[0], own_two_ref.at[1], two_ref.at[1], two_ref.at[0])
    copies = []
    for s in range(X):
        wait(s)
        done_ref[s] = targets_part(tiles_ref[s], scale, latents) + more_ref[s]
        pieces = [(done_ref.at[s, :half], uppers[s]), (done_ref.at[s, half:], lowers[s])]
        copies += leave(pieces, sems, 2 * X + 2 * s)
    for copy in copies:
        copy.wait()


def sum_kernel(parts_ref, *refs):
    out_ref = refs[-1]
    out_ref[...] = jnp.broadcast_to(jnp.sum(parts_ref[...], axis=0, keepdims=True), out_ref.shape)


def gather_kernel(parts_ref, after_ref, out_ref):
    del after_ref
    out_ref[...] = jnp.sum(parts_ref[...], axis=0)


def inverse_kernel(factor, parts_ref, *refs):
    out_ref = refs[-1]
    out_ref[...] = jnp.broadcast_to(factor / jnp.sum(parts_ref[...], axis=0, keepdims=True), out_ref.shape)


def join_kernel(kept_ref, came_ref, after_ref, spread_ref, mass_ref):
    del after_ref
    total = kept_ref[...] + came_ref[...]
    group = spread_ref.shape[1]
    spread_ref[...] = jnp.broadcast_to(total[None, :group], spread_ref.shape)
    mass_ref[...] = total[group:]


def turn_kernel(where_ref, own_one_ref, one_ref, more_one_ref, own_two_ref, two_ref, more_two_ref, *refs):
    send_ref, keep_ref, turned_ref = refs
    upper = own_one_ref[0] + one_ref[0] + more_one_ref[...]
    lower = own_two_ref[0] + two_ref[0] + more_two_ref[...]
    turned_ref[...] = jnp.concatenate([upper, lower], axis=0).T
    share = send_ref.shape[1]
    for i, slot in enumerate((0, 4, 2, 6)):
        for ref, s in ((keep_ref, slot), (send_ref, slot + 1)):
            start = pl.multiple_of((where_ref[2] ^ s) * share, share)
            ref[i] = turned_ref[pl.ds(start, share), :]


def final_kernel(
    parts_ref, columns_ref, codes_ref, tile_ref, more_one_ref, more_two_ref,
    out_ref, held_ref, tiles_ref, numer_ref, sems,
):
    del more_one_ref, more_two_ref
    steps = [
        [(tile_ref.at[b], tiles_ref.at[b]), (codes_ref.at[:, place(b)], held_ref.at[b])] for b in range(BLOCKS)
    ]
    wait = fetch(steps, sems)
    tokens, width = numer_ref.shape
    scale = row_scale_of(parts_ref)
    total = jnp.zeros(scale.shape, jnp.float32)
    for b in range(BLOCKS):
        wait(b)
        tile = tiles_ref[b]
        plan = (widen(scale, tile.shape[1]) * tile * columns_ref[b]).astype(jnp.bfloat16)
        total += fold(plan.astype(jnp.float32))
        part = jnp.dot(plan, held_ref[b].reshape(-1, width), preferred_element_type=jnp.float32)
        numer_ref[...] = part if b == 0 else numer_ref[...] + part
    group = tokens // Y
    mass = row_of(total)
    mass = jnp.concatenate([mass, jnp.zeros((1, 2 * width - tokens), jnp.float32)], axis=1)
    extra = jnp.concatenate(
        [mass[:, :width], mass[:, width:], jnp.zeros((PAD - 2, width), jnp.float32)], axis=0
    )
    for y in range(Y):
        out_ref[y, :group, :] = numer_ref[y * group : (y + 1) * group, :]
        out_ref[y, group:, :] = extra


def f32(*shape):
    return jax.ShapeDtypeStruct(shape, jnp.float32)


def whole(*shape):
    return pl.BlockSpec(shape, lambda *_: (0,) * len(shape))


def cost(flops, moved, exps=0):
    return pl.CostEstimate(flops=flops, bytes_accessed=moved, transcendentals=exps)


def per_device(latents, codebook):
    token_count, width = latents.shape
    code_count = codebook.shape[0]
    total_tokens = token_count * Z * X * C
    total_codes = code_count * H * Y
    share = code_count // (Z * X * C)
    block = code_count // BLOCKS
    size = token_count * code_count

    codes = codebook.reshape(Z, X * C, share, width)
    tile_spec = pl.BlockSpec((None, token_count, block), lambda b: (b, 0, 0))
    rows_spec = whole(H * Y, 1, token_count)
    columns_spec = pl.BlockSpec((None, 1, block), lambda b: (b, 0, 0))
    vmem = pl.BlockSpec(memory_space=pltpu.VMEM)
    smem = pl.BlockSpec(memory_space=pltpu.SMEM)
    hbm = pl.BlockSpec(memory_space=pltpu.HBM)
    anywhere = pl.BlockSpec(memory_space=pl.ANY)
    per_token = pltpu.VMEM((token_count, LANES), jnp.float32)
    held = pltpu.VMEM((BLOCKS, Z, share, width), jnp.bfloat16)
    tiles = functools.partial(pltpu.VMEM, dtype=jnp.float32)
    rows_shape = f32(H * Y, 1, token_count)
    columns_shape = f32(BLOCKS, 1, block)

    core, x, z = (lax.axis_index(axis) for axis in ("c", "x", "z"))
    where = jnp.stack([core, x, z, 1 - core, z * share])

    tile, part = pl.pallas_call(
        setup_kernel,
        in_specs=[smem, vmem, vmem],
        out_specs=[vmem, vmem],
        out_shape=[f32(BLOCKS, token_count, block), rows_shape],
        compiler_params=params(40_000_000),
        cost_estimate=cost(2 * size * width, 4 * size, size),
        name="setup",
    )(where, latents, codes)

    def rows(columns):
        return pl.pallas_call(
            rows_kernel,
            grid=(BLOCKS,),
            in_specs=[columns_spec, tile_spec],
            out_specs=rows_spec,
            out_shape=rows_shape,
            scratch_shapes=[per_token],
            compiler_params=params(),
            cost_estimate=cost(2 * size, 4 * size),
            name="rows",
        )(columns, tile)

    def columns(parts):
        return pl.pallas_call(
            columns_kernel,
            grid=(BLOCKS,),
            in_specs=[rows_spec, tile_spec],
            out_specs=whole(BLOCKS, 1, block),
            out_shape=columns_shape,
            scratch_shapes=[per_token],
            compiler_params=params(),
            cost_estimate=cost(2 * size, 4 * size),
            name="columns",
        )(parts, tile)

    def targets_sent(parts, after):
        return pl.pallas_call(
            targets_sent_kernel,
            in_specs=[smem, vmem, vmem, hbm, anywhere],
            out_specs=hbm,
            out_shape=f32(X, width, block),
            scratch_shapes=[
                tiles((X, token_count, block)),
                tiles((X, width, block)),
                pltpu.SemaphoreType.DMA((2 * X,)),
            ],
            compiler_params=params(FETCHES),
            cost_estimate=cost(size * width, 4 * size),
            name="targets_sent",
        )(where, parts, latents, tile, after)

    def targets_kept(parts, added, after):
        return pl.pallas_call(
            targets_kept_kernel,
            in_specs=[smem, vmem, vmem, hbm, anywhere, anywhere],
            out_specs=[hbm] * 4,
            out_shape=[f32(2, width // 2, block)] * 4,
            scratch_shapes=[
                tiles((X, token_count, block)),
                tiles((X, width, block)),
                tiles((X, width, block)),
                pltpu.SemaphoreType.DMA((4 * X,)),
            ],
            compiler_params=params(FETCHES_BESIDE_SUMS),
            cost_estimate=cost(size * width, 4 * size),
            name="targets_kept",
        )(where, parts, latents, tile, added, after)

    def small(kernel, name, count, weight, parts, *after):
        return pl.pallas_call(
            kernel,
            in_specs=[vmem] + [anywhere] * len(after),
            out_specs=vmem,
            out_shape=f32(count, 1, block),
            compiler_params=params(),
            cost_estimate=cost(weight * parts.size, 4 * parts.size),
            name=name,
        )(parts, *after)

    inverse = functools.partial(inverse_kernel, total_tokens / total_codes)
    def swap(value, axis, count, bits):
        return lax.ppermute(value, axis, [(i, i ^ bits) for i in range(count)])

    for sweep_index in range(ITERS):
        last = sweep_index == ITERS - 1
        parts = exchange(part, ("h", "y"))
        column_sums = columns(parts)
        if last:
            sent = targets_sent(parts, column_sums)
        sums = small(sum_kernel, "sums", Z, 20_000_000 if last else 1, exchange(column_sums, ("c", "x")))
        if last:
            kept = targets_kept(parts, swap(sent, "c", C, 1), sums)
        after = (kept[0],) if last else ()
        mine = small(inverse, "inverse", BLOCKS, 2_000_000 if last else 1, exchange(sums, "z"), *after)
        col_scale = exchange(mine, ("c", "x"))
        if not last:
            part = rows(col_scale)

    one, two, own_one, own_two = kept
    one, two = swap(one, "x", X, 1), swap(two, "x", X, 3)
    more_one, more_two = own_one[1] + one[1], own_two[1] + two[1]

    group = token_count // Y
    packed = pl.pallas_call(
        final_kernel,
        in_specs=[vmem, vmem, hbm, hbm, anywhere, anywhere],
        out_specs=vmem,
        out_shape=f32(Y, group + PAD, width),
        scratch_shapes=[
            held,
            tiles((BLOCKS, token_count, block)),
            tiles((token_count, width)),
            pltpu.SemaphoreType.DMA((2 * BLOCKS,)),
        ],
        compiler_params=params(FETCHES),
        cost_estimate=cost(12 * size * width, 4 * size),
        name="final",
    )(parts, col_scale, codes, tile, more_one, more_two)
    more_one, more_two = swap(more_one, "x", X, 3), swap(more_two, "x", X, 1)
    away, near = pl.pallas_call(
        turn_kernel,
        in_specs=[smem] + [vmem] * 6,
        out_specs=[vmem] * 2,
        out_shape=[f32(Z // 2, share, width)] * 2,
        scratch_shapes=[pltpu.VMEM((block, width), jnp.float32)],
        compiler_params=params(16 << 20),
        cost_estimate=cost(3 * block * width, 12 * block * width),
        name="turn",
    )(where, own_one, one, more_one, own_two, two, more_two)
    packed = pl.pallas_call(
        gather_kernel,
        in_specs=[vmem, anywhere],
        out_specs=vmem,
        out_shape=f32(group + PAD, width),
        compiler_params=params(),
        cost_estimate=cost(packed.size, 4 * packed.size),
        name="gathered",
    )(exchange(packed, "y"), away)
    near = near + swap(away, "z", Z, 1)
    numer, mass = pl.pallas_call(
        join_kernel,
        in_specs=[vmem] * 2 + [anywhere],
        out_specs=[vmem] * 2,
        out_shape=[f32(Y, group, width), f32(PAD, width)],
        compiler_params=params(),
        cost_estimate=cost(20000 * token_count * width, 8 * token_count * width),
        name="join",
    )(packed, swap(packed, "h", H, 1), near)
    near = near[:2] + swap(near[2:], "z", Z, 2)
    summed = near[0] + swap(near[1], "z", Z, 4)
    own = lax.dynamic_slice(mine, (0, 0, where[4]), (1, 1, share)).reshape(share)
    targets = summed * (own * (total_codes / total_tokens))[:, None]
    mass = mass[:2].reshape(2 * width)[:token_count]
    rebuilt = exchange(numer, "y").reshape(token_count, width) / mass[:, None]
    return (targets, rebuilt)


def solution(mesh):
    fine = Mesh(mesh.devices.reshape(Z, X, C, H, Y), AXES)
    return jax.shard_map(
        per_device,
        mesh=fine,
        in_specs=(P(("z", "x", "c"), None), P(("h", "y"), None)),
        out_specs=(P(("h", "y", "z", "x", "c"), None), P(("z", "x", "c"), None)),
        check_vma=False,
    )
```

```python
import functools

import jax
import jax.numpy as jnp
from jax import lax
from jax.experimental import pallas as pl
from jax.experimental.pallas import tpu as pltpu
from jax.sharding import Mesh, PartitionSpec as P

ITERS = 3
SHARP = 48.0
EPSILON = 1e-06

AXES = ("z", "x", "c", "h", "y")
Z, X, C, H, Y = 8, 4, 2, 2, 4
BLOCKS = C * X
LANES = 128
PAD = 8


def exchange(blocks, axes):
    return lax.all_to_all(blocks, axes, 0, 0, tiled=True)


FETCHES = 55_500_000
FETCHES_BESIDE_SUMS = 53_000_000


def params(limit=8 << 20):
    return pltpu.CompilerParams(vmem_limit_bytes=limit)


def column_of(row):
    return jnp.broadcast_to(row, (LANES, row.shape[1])).T


def row_of(partial):
    return jnp.sum(partial.T, axis=0, keepdims=True)


def fold(product):
    total = product[:, :LANES]
    for start in range(LANES, product.shape[1], LANES):
        total = total + product[:, start : start + LANES]
    return total


def widen(column, width):
    return jnp.concatenate([column] * (width // LANES), axis=1)


def place(b):
    return (b % X) * C + b // X


AHEAD = 3


def fetch(steps, sems):
    copies, count = [], 0
    for pairs in steps:
        copies.append([pltpu.make_async_copy(*pair, sems.at[count + i]) for i, pair in enumerate(pairs)])
        count += len(pairs)

    def start(step):
        for copy in copies[step]:
            copy.start()

    def wait(step):
        if step + AHEAD < len(copies):
            start(step + AHEAD)
        for copy in copies[step]:
            copy.wait()

    for step in range(min(AHEAD, len(copies))):
        start(step)
    return wait


def setup_kernel(where_ref, latents_ref, codes_ref, tile_ref, rows_ref):
    del where_ref
    latents = latents_ref[...]
    width = latents.shape[1]
    floats = latents.astype(jnp.float32)
    mean = jnp.sum(floats * floats, axis=1, keepdims=True) * (1.0 / width)
    scale = jnp.broadcast_to(lax.rsqrt(mean + EPSILON) * (SHARP / width), (latents.shape[0], LANES))
    total = jnp.zeros(scale.shape, jnp.float32)
    across = (((1,), (1,)), ((), ()))
    for b in range(BLOCKS):
        codes = codes_ref[:, place(b)].reshape(-1, width)
        floats = codes.astype(jnp.float32)
        code_norm = lax.rsqrt(row_of(fold(floats * floats)) * (1.0 / width) + EPSILON)
        inner = lax.dot_general(latents, codes, across, preferred_element_type=jnp.float32)
        tile = jnp.exp(inner * widen(scale, codes.shape[0]) * code_norm)
        tile_ref[b] = tile
        total += fold(tile)
    rows_ref[...] = jnp.broadcast_to(row_of(total)[None], rows_ref.shape)


def rows_kernel(columns_ref, tile_ref, rows_ref, total_ref):
    step = pl.program_id(0)

    @pl.when(step == 0)
    def _():
        total_ref[...] = jnp.zeros_like(total_ref)

    total_ref[...] += fold(tile_ref[...] * columns_ref[...])

    @pl.when(step == pl.num_programs(0) - 1)
    def _():
        rows_ref[...] = jnp.broadcast_to(row_of(total_ref[...])[None], rows_ref.shape)


def row_scale_of(parts_ref):
    return column_of(1.0 / jnp.sum(parts_ref[...], axis=0))


def columns_kernel(parts_ref, tile_ref, columns_ref, scale_ref):
    @pl.when(pl.program_id(0) == 0)
    def _():
        scale_ref[...] = row_scale_of(parts_ref)

    tile = tile_ref[...]
    sums = jnp.sum(tile * widen(scale_ref[...], tile.shape[1]), axis=0, keepdims=True)
    columns_ref[pl.program_id(0)] = sums


def targets_part(tile, scale, latents):
    weighted = (tile * widen(scale, tile.shape[1])).astype(jnp.bfloat16)
    return lax.dot_general(latents, weighted, (((0,), (0,)), ((), ())), preferred_element_type=jnp.float32)


def leave(pieces, sems, first):
    copies = [pltpu.make_async_copy(*piece, sems.at[first + i]) for i, piece in enumerate(pieces)]
    for copy in copies:
        copy.start()
    return copies


def targets_sent_kernel(where_ref, parts_ref, latents_ref, tile_ref, after_ref, out_ref, tiles_ref, done_ref, sems):
    del after_ref
    wait = fetch([[(tile_ref.at[where_ref[3] * X + (where_ref[1] ^ s)], tiles_ref.at[s])] for s in range(X)], sems)
    scale = row_scale_of(parts_ref)
    latents = latents_ref[...]
    copies = []
    for s in range(X):
        wait(s)
        done_ref[s] = targets_part(tiles_ref[s], scale, latents)
        copies += leave([(done_ref.at[s], out_ref.at[s])], sems, X + s)
    for copy in copies:
        copy.wait()


def targets_kept_kernel(
    where_ref, parts_ref, latents_ref, tile_ref, added_ref, after_ref,
    own_ref, one_ref, two_ref, three_ref, tiles_ref, more_ref, done_ref, sems,
):
    del after_ref
    slots = (1, 3, 2, 0)
    steps = [
        [(tile_ref.at[where_ref[0] * X + (where_ref[1] ^ s)], tiles_ref.at[s]), (added_ref.at[s], more_ref.at[s])]
        for s in slots
    ]
    wait = fetch(steps, sems)
    scale = row_scale_of(parts_ref)
    latents = latents_ref[...]
    outs = (own_ref, one_ref, two_ref, three_ref)
    copies = []
    for step, s in enumerate(slots):
        wait(step)
        done_ref[s] = targets_part(tiles_ref[s], scale, latents) + more_ref[s]
        copies += leave([(done_ref.at[s], outs[s])], sems, 2 * X + s)
    for copy in copies:
        copy.wait()


def sum_kernel(parts_ref, *refs):
    out_ref = refs[-1]
    out_ref[...] = jnp.broadcast_to(jnp.sum(parts_ref[...], axis=0, keepdims=True), out_ref.shape)


def gather_kernel(parts_ref, after_ref, out_ref):
    del after_ref
    out_ref[...] = jnp.sum(parts_ref[...], axis=0)


def inverse_kernel(factor, parts_ref, *refs):
    out_ref = refs[-1]
    out_ref[...] = jnp.broadcast_to(factor / jnp.sum(parts_ref[...], axis=0, keepdims=True), out_ref.shape)


def join_kernel(kept_ref, came_ref, after_ref, spread_ref, mass_ref):
    del after_ref
    total = kept_ref[...] + came_ref[...]
    group = spread_ref.shape[1]
    spread_ref[...] = jnp.broadcast_to(total[None, :group], spread_ref.shape)
    mass_ref[...] = total[group:]


def near_kernel(own_ref, one_ref, three_ref, out_ref):
    out_ref[...] = own_ref[...] + one_ref[...] + three_ref[...]


def turn_kernel(where_ref, near_ref, two_ref, send_ref, keep_ref, turned_ref):
    turned_ref[...] = (near_ref[...] + two_ref[...]).T
    share = send_ref.shape[1]
    for i, slot in enumerate((0, 4, 2, 6)):
        for ref, s in ((keep_ref, slot), (send_ref, slot + 1)):
            start = pl.multiple_of((where_ref[2] ^ s) * share, share)
            ref[i] = turned_ref[pl.ds(start, share), :]


def final_kernel(
    parts_ref, columns_ref, codes_ref, tile_ref, out_ref, held_ref, tiles_ref, numer_ref, sems
):
    steps = [
        [(tile_ref.at[b], tiles_ref.at[b]), (codes_ref.at[:, place(b)], held_ref.at[b])] for b in range(BLOCKS)
    ]
    wait = fetch(steps, sems)
    tokens, width = numer_ref.shape
    scale = row_scale_of(parts_ref)
    total = jnp.zeros(scale.shape, jnp.float32)
    for b in range(BLOCKS):
        wait(b)
        tile = tiles_ref[b]
        plan = (widen(scale, tile.shape[1]) * tile * columns_ref[b]).astype(jnp.bfloat16)
        total += fold(plan.astype(jnp.float32))
        part = jnp.dot(plan, held_ref[b].reshape(-1, width), preferred_element_type=jnp.float32)
        numer_ref[...] = part if b == 0 else numer_ref[...] + part
    group = tokens // Y
    mass = row_of(total)
    mass = jnp.concatenate([mass, jnp.zeros((1, 2 * width - tokens), jnp.float32)], axis=1)
    extra = jnp.concatenate(
        [mass[:, :width], mass[:, width:], jnp.zeros((PAD - 2, width), jnp.float32)], axis=0
    )
    for y in range(Y):
        out_ref[y, :group, :] = numer_ref[y * group : (y + 1) * group, :]
        out_ref[y, group:, :] = extra


def f32(*shape):
    return jax.ShapeDtypeStruct(shape, jnp.float32)


def whole(*shape):
    return pl.BlockSpec(shape, lambda *_: (0,) * len(shape))


def cost(flops, moved, exps=0):
    return pl.CostEstimate(flops=flops, bytes_accessed=moved, transcendentals=exps)


def per_device(latents, codebook):
    token_count, width = latents.shape
    code_count = codebook.shape[0]
    total_tokens = token_count * Z * X * C
    total_codes = code_count * H * Y
    share = code_count // (Z * X * C)
    block = code_count // BLOCKS
    size = token_count * code_count

    codes = codebook.reshape(Z, X * C, share, width)
    tile_spec = pl.BlockSpec((None, token_count, block), lambda b: (b, 0, 0))
    rows_spec = whole(H * Y, 1, token_count)
    columns_spec = pl.BlockSpec((None, 1, block), lambda b: (b, 0, 0))
    vmem = pl.BlockSpec(memory_space=pltpu.VMEM)
    smem = pl.BlockSpec(memory_space=pltpu.SMEM)
    hbm = pl.BlockSpec(memory_space=pltpu.HBM)
    anywhere = pl.BlockSpec(memory_space=pl.ANY)
    per_token = pltpu.VMEM((token_count, LANES), jnp.float32)
    held = pltpu.VMEM((BLOCKS, Z, share, width), jnp.bfloat16)
    tiles = functools.partial(pltpu.VMEM, dtype=jnp.float32)
    rows_shape = f32(H * Y, 1, token_count)
    columns_shape = f32(BLOCKS, 1, block)

    core, x, z = (lax.axis_index(axis) for axis in ("c", "x", "z"))
    where = jnp.stack([core, x, z, 1 - core, z * share])

    tile, part = pl.pallas_call(
        setup_kernel,
        in_specs=[smem, vmem, vmem],
        out_specs=[vmem, vmem],
        out_shape=[f32(BLOCKS, token_count, block), rows_shape],
        compiler_params=params(40_000_000),
        cost_estimate=cost(2 * size * width, 4 * size, size),
        name="setup",
    )(where, latents, codes)

    def rows(columns):
        return pl.pallas_call(
            rows_kernel,
            grid=(BLOCKS,),
            in_specs=[columns_spec, tile_spec],
            out_specs=rows_spec,
            out_shape=rows_shape,
            scratch_shapes=[per_token],
            compiler_params=params(),
            cost_estimate=cost(2 * size, 4 * size),
            name="rows",
        )(columns, tile)

    def columns(parts):
        return pl.pallas_call(
            columns_kernel,
            grid=(BLOCKS,),
            in_specs=[rows_spec, tile_spec],
            out_specs=whole(BLOCKS, 1, block),
            out_shape=columns_shape,
            scratch_shapes=[per_token],
            compiler_params=params(),
            cost_estimate=cost(2 * size, 4 * size),
            name="columns",
        )(parts, tile)

    def targets_sent(parts, after):
        return pl.pallas_call(
            targets_sent_kernel,
            in_specs=[smem, vmem, vmem, hbm, anywhere],
            out_specs=hbm,
            out_shape=f32(X, width, block),
            scratch_shapes=[
                tiles((X, token_count, block)),
                tiles((X, width, block)),
                pltpu.SemaphoreType.DMA((2 * X,)),
            ],
            compiler_params=params(FETCHES),
            cost_estimate=cost(size * width, 4 * size),
            name="targets_sent",
        )(where, parts, latents, tile, after)

    def targets_kept(parts, added, after):
        return pl.pallas_call(
            targets_kept_kernel,
            in_specs=[smem, vmem, vmem, hbm, anywhere, anywhere],
            out_specs=[hbm] * 4,
            out_shape=[f32(width, block)] * 4,
            scratch_shapes=[
                tiles((X, token_count, block)),
                tiles((X, width, block)),
                tiles((X, width, block)),
                pltpu.SemaphoreType.DMA((3 * X,)),
            ],
            compiler_params=params(FETCHES_BESIDE_SUMS),
            cost_estimate=cost(size * width, 4 * size),
            name="targets_kept",
        )(where, parts, latents, tile, added, after)

    def small(kernel, name, count, weight, parts, *after):
        return pl.pallas_call(
            kernel,
            in_specs=[vmem] + [anywhere] * len(after),
            out_specs=vmem,
            out_shape=f32(count, 1, block),
            compiler_params=params(),
            cost_estimate=cost(weight * parts.size, 4 * parts.size),
            name=name,
        )(parts, *after)

    inverse = functools.partial(inverse_kernel, total_tokens / total_codes)
    def swap(value, axis, count, bits):
        return lax.ppermute(value, axis, [(i, i ^ bits) for i in range(count)])

    for sweep_index in range(ITERS):
        last = sweep_index == ITERS - 1
        parts = exchange(part, ("h", "y"))
        column_sums = columns(parts)
        if last:
            sent = targets_sent(parts, column_sums)
        sums = small(sum_kernel, "sums", Z, 20_000_000 if last else 1, exchange(column_sums, ("c", "x")))
        if last:
            kept = targets_kept(parts, swap(sent, "c", C, 1), sums)
        after = (kept[0],) if last else ()
        mine = small(inverse, "inverse", BLOCKS, 2_000_000 if last else 1, exchange(sums, "z"), *after)
        col_scale = exchange(mine, ("c", "x"))
        if not last:
            part = rows(col_scale)

    own, *others = kept
    one, two, three = (swap(other, "x", X, s) for s, other in enumerate(others, 1))

    group = token_count // Y
    packed = pl.pallas_call(
        final_kernel,
        in_specs=[vmem, vmem, hbm, hbm],
        out_specs=vmem,
        out_shape=f32(Y, group + PAD, width),
        scratch_shapes=[
            held,
            tiles((BLOCKS, token_count, block)),
            tiles((token_count, width)),
            pltpu.SemaphoreType.DMA((2 * BLOCKS,)),
        ],
        compiler_params=params(FETCHES),
        cost_estimate=cost(12 * size * width, 4 * size),
        name="final",
    )(parts, col_scale, codes, tile)
    chips = pl.pallas_call(
        near_kernel,
        in_specs=[vmem] * 3,
        out_specs=vmem,
        out_shape=f32(width, block),
        compiler_params=params(),
        cost_estimate=cost(80_000 * width * block, 12 * width * block),
        name="chips",
    )(own, one, three)
    away, near = pl.pallas_call(
        turn_kernel,
        in_specs=[smem] + [vmem] * 2,
        out_specs=[vmem] * 2,
        out_shape=[f32(Z // 2, share, width)] * 2,
        scratch_shapes=[pltpu.VMEM((block, width), jnp.float32)],
        compiler_params=params(16 << 20),
        cost_estimate=cost(3 * block * width, 12 * block * width),
        name="turn",
    )(where, chips, two)
    packed = pl.pallas_call(
        gather_kernel,
        in_specs=[vmem, anywhere],
        out_specs=vmem,
        out_shape=f32(group + PAD, width),
        compiler_params=params(),
        cost_estimate=cost(packed.size, 4 * packed.size),
        name="gathered",
    )(exchange(packed, "y"), away)
    near = near + swap(away, "z", Z, 1)
    numer, mass = pl.pallas_call(
        join_kernel,
        in_specs=[vmem] * 2 + [anywhere],
        out_specs=[vmem] * 2,
        out_shape=[f32(Y, group, width), f32(PAD, width)],
        compiler_params=params(),
        cost_estimate=cost(20000 * token_count * width, 8 * token_count * width),
        name="join",
    )(packed, swap(packed, "h", H, 1), near)
    near = near[:2] + swap(near[2:], "z", Z, 2)
    summed = near[0] + swap(near[1], "z", Z, 4)
    scale = lax.dynamic_slice(mine, (0, 0, where[4]), (1, 1, share)).reshape(share)
    targets = summed * (scale * (total_codes / total_tokens))[:, None]
    mass = mass[:2].reshape(2 * width)[:token_count]
    rebuilt = exchange(numer, "y").reshape(token_count, width) / mass[:, None]
    return (targets, rebuilt)


def solution(mesh):
    fine = Mesh(mesh.devices.reshape(Z, X, C, H, Y), AXES)
    return jax.shard_map(
        per_device,
        mesh=fine,
        in_specs=(P(("z", "x", "c"), None), P(("h", "y"), None)),
        out_specs=(P(("h", "y", "z", "x", "c"), None), P(("z", "x", "c"), None)),
        check_vma=False,
    )
```

```python
import functools

import jax
import jax.numpy as jnp
from jax import lax
from jax.experimental import pallas as pl
from jax.experimental.pallas import tpu as pltpu
from jax.sharding import Mesh, PartitionSpec as P

ITERS = 3
SHARP = 48.0
EPSILON = 1e-06

AXES = ("z", "x", "c", "h", "y")
Z, X, C, H, Y = 8, 4, 2, 2, 4
BLOCKS = C * X
LANES = 128
PAD = 8


def exchange(blocks, axes):
    return lax.all_to_all(blocks, axes, 0, 0, tiled=True)


FETCHES = 55_500_000
FETCHES_BESIDE_SUMS = 53_000_000


def params(limit=8 << 20):
    return pltpu.CompilerParams(vmem_limit_bytes=limit)


def column_of(row):
    return jnp.broadcast_to(row, (LANES, row.shape[1])).T


def row_of(partial):
    return jnp.sum(partial.T, axis=0, keepdims=True)


def fold(product):
    total = product[:, :LANES]
    for start in range(LANES, product.shape[1], LANES):
        total = total + product[:, start : start + LANES]
    return total


def widen(column, width):
    return jnp.concatenate([column] * (width // LANES), axis=1)


def place(b):
    return (b % X) * C + b // X


AHEAD = 3


def fetch(steps, sems):
    copies, count = [], 0
    for pairs in steps:
        copies.append([pltpu.make_async_copy(*pair, sems.at[count + i]) for i, pair in enumerate(pairs)])
        count += len(pairs)

    def start(step):
        for copy in copies[step]:
            copy.start()

    def wait(step):
        if step + AHEAD < len(copies):
            start(step + AHEAD)
        for copy in copies[step]:
            copy.wait()

    for step in range(min(AHEAD, len(copies))):
        start(step)
    return wait


def setup_kernel(where_ref, latents_ref, codes_ref, tile_ref, rows_ref):
    del where_ref
    latents = latents_ref[...]
    width = latents.shape[1]
    floats = latents.astype(jnp.float32)
    mean = jnp.sum(floats * floats, axis=1, keepdims=True) * (1.0 / width)
    scale = jnp.broadcast_to(lax.rsqrt(mean + EPSILON) * (SHARP / width), (latents.shape[0], LANES))
    total = jnp.zeros(scale.shape, jnp.float32)
    across = (((1,), (1,)), ((), ()))
    for b in range(BLOCKS):
        codes = codes_ref[:, place(b)].reshape(-1, width)
        floats = codes.astype(jnp.float32)
        code_norm = lax.rsqrt(row_of(fold(floats * floats)) * (1.0 / width) + EPSILON)
        inner = lax.dot_general(latents, codes, across, preferred_element_type=jnp.float32)
        tile = jnp.exp(inner * widen(scale, codes.shape[0]) * code_norm)
        tile_ref[b] = tile
        total += fold(tile)
    rows_ref[...] = jnp.broadcast_to(row_of(total)[None], rows_ref.shape)


def rows_kernel(columns_ref, tile_ref, rows_ref):
    total = fold(tile_ref[0] * columns_ref[0])
    for b in range(1, BLOCKS):
        total += fold(tile_ref[b] * columns_ref[b])
    rows_ref[...] = jnp.broadcast_to(row_of(total)[None], rows_ref.shape)


def row_scale_of(parts_ref):
    return column_of(1.0 / jnp.sum(parts_ref[...], axis=0))


def columns_kernel(parts_ref, tile_ref, columns_ref):
    scale = row_scale_of(parts_ref)
    for b in range(BLOCKS):
        tile = tile_ref[b]
        columns_ref[b] = jnp.sum(tile * widen(scale, tile.shape[1]), axis=0, keepdims=True)


def targets_part(tile, scale, latents):
    weighted = (tile * widen(scale, tile.shape[1])).astype(jnp.bfloat16)
    return lax.dot_general(latents, weighted, (((0,), (0,)), ((), ())), preferred_element_type=jnp.float32)


def leave(pieces, sems, first):
    copies = [pltpu.make_async_copy(*piece, sems.at[first + i]) for i, piece in enumerate(pieces)]
    for copy in copies:
        copy.start()
    return copies


def targets_sent_kernel(where_ref, parts_ref, latents_ref, tile_ref, after_ref, out_ref, tiles_ref, done_ref, sems):
    del after_ref
    wait = fetch([[(tile_ref.at[where_ref[3] * X + (where_ref[1] ^ s)], tiles_ref.at[s])] for s in range(X)], sems)
    scale = row_scale_of(parts_ref)
    latents = latents_ref[...]
    copies = []
    for s in range(X):
        wait(s)
        done_ref[s] = targets_part(tiles_ref[s], scale, latents)
        copies += leave([(done_ref.at[s], out_ref.at[s])], sems, X + s)
    for copy in copies:
        copy.wait()


def targets_kept_kernel(
    where_ref, parts_ref, latents_ref, tile_ref, added_ref, after_ref,
    one_ref, two_ref, own_one_ref, own_two_ref, tiles_ref, more_ref, done_ref, sems,
):
    del after_ref
    steps = [
        [(tile_ref.at[where_ref[0] * X + (where_ref[1] ^ s)], tiles_ref.at[s]), (added_ref.at[s], more_ref.at[s])]
        for s in range(X)
    ]
    wait = fetch(steps, sems)
    scale = row_scale_of(parts_ref)
    latents = latents_ref[...]
    half = latents.shape[1] // 2
    uppers = (own_one_ref.at[0], one_ref.at[0], one_ref.at[1], own_one_ref.at[1])
    lowers = (own_two_ref.at[0], own_two_ref.at[1], two_ref.at[1], two_ref.at[0])
    copies = []
    for s in range(X):
        wait(s)
        done_ref[s] = targets_part(tiles_ref[s], scale, latents) + more_ref[s]
        pieces = [(done_ref.at[s, :half], uppers[s]), (done_ref.at[s, half:], lowers[s])]
        copies += leave(pieces, sems, 2 * X + 2 * s)
    for copy in copies:
        copy.wait()


def sum_kernel(parts_ref, *refs):
    out_ref = refs[-1]
    out_ref[...] = jnp.broadcast_to(jnp.sum(parts_ref[...], axis=0, keepdims=True), out_ref.shape)


def gather_kernel(parts_ref, after_ref, out_ref):
    del after_ref
    out_ref[...] = jnp.sum(parts_ref[...], axis=0)


def inverse_kernel(factor, parts_ref, *refs):
    out_ref = refs[-1]
    out_ref[...] = jnp.broadcast_to(factor / jnp.sum(parts_ref[...], axis=0, keepdims=True), out_ref.shape)


def join_kernel(kept_ref, came_ref, after_ref, spread_ref, mass_ref):
    del after_ref
    total = kept_ref[...] + came_ref[...]
    group = spread_ref.shape[1]
    spread_ref[...] = jnp.broadcast_to(total[None, :group], spread_ref.shape)
    mass_ref[...] = total[group:]


def turn_kernel(where_ref, own_one_ref, one_ref, more_one_ref, own_two_ref, two_ref, more_two_ref, *refs):
    send_ref, keep_ref, turned_ref = refs
    upper = own_one_ref[0] + one_ref[0] + more_one_ref[...]
    lower = own_two_ref[0] + two_ref[0] + more_two_ref[...]
    turned_ref[...] = jnp.concatenate([upper, lower], axis=0).T
    share = send_ref.shape[1]
    for i, slot in enumerate((0, 4, 2, 6)):
        for ref, s in ((keep_ref, slot), (send_ref, slot + 1)):
            start = pl.multiple_of((where_ref[2] ^ s) * share, share)
            ref[i] = turned_ref[pl.ds(start, share), :]


def final_kernel(
    parts_ref, columns_ref, codes_ref, tile_ref, more_one_ref, more_two_ref,
    out_ref, held_ref, tiles_ref, numer_ref, sems,
):
    del more_one_ref, more_two_ref
    steps = [
        [(tile_ref.at[b], tiles_ref.at[b]), (codes_ref.at[:, place(b)], held_ref.at[b])] for b in range(BLOCKS)
    ]
    wait = fetch(steps, sems)
    tokens, width = numer_ref.shape
    scale = row_scale_of(parts_ref)
    total = jnp.zeros(scale.shape, jnp.float32)
    for b in range(BLOCKS):
        wait(b)
        tile = tiles_ref[b]
        plan = (widen(scale, tile.shape[1]) * tile * columns_ref[b]).astype(jnp.bfloat16)
        total += fold(plan.astype(jnp.float32))
        part = jnp.dot(plan, held_ref[b].reshape(-1, width), preferred_element_type=jnp.float32)
        numer_ref[...] = part if b == 0 else numer_ref[...] + part
    group = tokens // Y
    mass = row_of(total)
    mass = jnp.concatenate([mass, jnp.zeros((1, 2 * width - tokens), jnp.float32)], axis=1)
    extra = jnp.concatenate(
        [mass[:, :width], mass[:, width:], jnp.zeros((PAD - 2, width), jnp.float32)], axis=0
    )
    for y in range(Y):
        out_ref[y, :group, :] = numer_ref[y * group : (y + 1) * group, :]
        out_ref[y, group:, :] = extra


def f32(*shape):
    return jax.ShapeDtypeStruct(shape, jnp.float32)


def cost(flops, moved, exps=0):
    return pl.CostEstimate(flops=flops, bytes_accessed=moved, transcendentals=exps)


def per_device(latents, codebook):
    token_count, width = latents.shape
    code_count = codebook.shape[0]
    total_tokens = token_count * Z * X * C
    total_codes = code_count * H * Y
    share = code_count // (Z * X * C)
    block = code_count // BLOCKS
    size = token_count * code_count

    codes = codebook.reshape(Z, X * C, share, width)
    vmem = pl.BlockSpec(memory_space=pltpu.VMEM)
    smem = pl.BlockSpec(memory_space=pltpu.SMEM)
    hbm = pl.BlockSpec(memory_space=pltpu.HBM)
    anywhere = pl.BlockSpec(memory_space=pl.ANY)
    held = pltpu.VMEM((BLOCKS, Z, share, width), jnp.bfloat16)
    tiles = functools.partial(pltpu.VMEM, dtype=jnp.float32)
    rows_shape = f32(H * Y, 1, token_count)
    columns_shape = f32(BLOCKS, 1, block)

    core, x, z = (lax.axis_index(axis) for axis in ("c", "x", "z"))
    where = jnp.stack([core, x, z, 1 - core, z * share])

    tile, part = pl.pallas_call(
        setup_kernel,
        in_specs=[smem, vmem, vmem],
        out_specs=[vmem, vmem],
        out_shape=[f32(BLOCKS, token_count, block), rows_shape],
        compiler_params=params(40_000_000),
        cost_estimate=cost(2 * size * width, 4 * size, size),
        name="setup",
    )(where, latents, codes)

    def sweep(kernel, name, given, shape):
        return pl.pallas_call(
            kernel,
            in_specs=[vmem, vmem],
            out_specs=vmem,
            out_shape=shape,
            compiler_params=params(),
            cost_estimate=cost(2 * size, 4 * size),
            name=name,
        )(given, tile)

    def rows(columns):
        return sweep(rows_kernel, "rows", columns, rows_shape)

    def columns(parts):
        return sweep(columns_kernel, "columns", parts, columns_shape)

    def targets_sent(parts, after):
        return pl.pallas_call(
            targets_sent_kernel,
            in_specs=[smem, vmem, vmem, hbm, anywhere],
            out_specs=hbm,
            out_shape=f32(X, width, block),
            scratch_shapes=[
                tiles((X, token_count, block)),
                tiles((X, width, block)),
                pltpu.SemaphoreType.DMA((2 * X,)),
            ],
            compiler_params=params(FETCHES),
            cost_estimate=cost(size * width, 4 * size),
            name="targets_sent",
        )(where, parts, latents, tile, after)

    def targets_kept(parts, added, after):
        return pl.pallas_call(
            targets_kept_kernel,
            in_specs=[smem, vmem, vmem, hbm, anywhere, anywhere],
            out_specs=[hbm] * 4,
            out_shape=[f32(2, width // 2, block)] * 4,
            scratch_shapes=[
                tiles((X, token_count, block)),
                tiles((X, width, block)),
                tiles((X, width, block)),
                pltpu.SemaphoreType.DMA((4 * X,)),
            ],
            compiler_params=params(FETCHES_BESIDE_SUMS),
            cost_estimate=cost(size * width, 4 * size),
            name="targets_kept",
        )(where, parts, latents, tile, added, after)

    def small(kernel, name, count, weight, parts, *after):
        return pl.pallas_call(
            kernel,
            in_specs=[vmem] + [anywhere] * len(after),
            out_specs=vmem,
            out_shape=f32(count, 1, block),
            compiler_params=params(),
            cost_estimate=cost(weight * parts.size, 4 * parts.size),
            name=name,
        )(parts, *after)

    inverse = functools.partial(inverse_kernel, total_tokens / total_codes)
    def swap(value, axis, count, bits):
        return lax.ppermute(value, axis, [(i, i ^ bits) for i in range(count)])

    for sweep_index in range(ITERS):
        last = sweep_index == ITERS - 1
        parts = exchange(part, ("h", "y"))
        column_sums = columns(parts)
        if last:
            sent = targets_sent(parts, column_sums)
        sums = small(sum_kernel, "sums", Z, 20_000_000 if last else 1, exchange(column_sums, ("c", "x")))
        if last:
            kept = targets_kept(parts, swap(sent, "c", C, 1), sums)
        after = (kept[0],) if last else ()
        mine = small(inverse, "inverse", BLOCKS, 2_000_000 if last else 1, exchange(sums, "z"), *after)
        col_scale = exchange(mine, ("c", "x"))
        if not last:
            part = rows(col_scale)

    one, two, own_one, own_two = kept
    one, two = swap(one, "x", X, 1), swap(two, "x", X, 3)
    more_one, more_two = own_one[1] + one[1], own_two[1] + two[1]

    group = token_count // Y
    packed = pl.pallas_call(
        final_kernel,
        in_specs=[vmem, vmem, hbm, hbm, anywhere, anywhere],
        out_specs=vmem,
        out_shape=f32(Y, group + PAD, width),
        scratch_shapes=[
            held,
            tiles((BLOCKS, token_count, block)),
            tiles((token_count, width)),
            pltpu.SemaphoreType.DMA((2 * BLOCKS,)),
        ],
        compiler_params=params(FETCHES),
        cost_estimate=cost(12 * size * width, 4 * size),
        name="final",
    )(parts, col_scale, codes, tile, more_one, more_two)
    more_one, more_two = swap(more_one, "x", X, 3), swap(more_two, "x", X, 1)
    away, near = pl.pallas_call(
        turn_kernel,
        in_specs=[smem] + [vmem] * 6,
        out_specs=[vmem] * 2,
        out_shape=[f32(Z // 2, share, width)] * 2,
        scratch_shapes=[pltpu.VMEM((block, width), jnp.float32)],
        compiler_params=params(16 << 20),
        cost_estimate=cost(3 * block * width, 12 * block * width),
        name="turn",
    )(where, own_one, one, more_one, own_two, two, more_two)
    packed = pl.pallas_call(
        gather_kernel,
        in_specs=[vmem, anywhere],
        out_specs=vmem,
        out_shape=f32(group + PAD, width),
        compiler_params=params(),
        cost_estimate=cost(packed.size, 4 * packed.size),
        name="gathered",
    )(exchange(packed, "y"), away)
    near = near + swap(away, "z", Z, 1)
    numer, mass = pl.pallas_call(
        join_kernel,
        in_specs=[vmem] * 2 + [anywhere],
        out_specs=[vmem] * 2,
        out_shape=[f32(Y, group, width), f32(PAD, width)],
        compiler_params=params(),
        cost_estimate=cost(20000 * token_count * width, 8 * token_count * width),
        name="join",
    )(packed, swap(packed, "h", H, 1), near)
    near = near[:2] + swap(near[2:], "z", Z, 2)
    summed = near[0] + swap(near[1], "z", Z, 4)
    own = lax.dynamic_slice(mine, (0, 0, where[4]), (1, 1, share)).reshape(share)
    targets = summed * (own * (total_codes / total_tokens))[:, None]
    mass = mass[:2].reshape(2 * width)[:token_count]
    rebuilt = exchange(numer, "y").reshape(token_count, width) / mass[:, None]
    return (targets, rebuilt)


def solution(mesh):
    fine = Mesh(mesh.devices.reshape(Z, X, C, H, Y), AXES)
    return jax.shard_map(
        per_device,
        mesh=fine,
        in_specs=(P(("z", "x", "c"), None), P(("h", "y"), None)),
        out_specs=(P(("h", "y", "z", "x", "c"), None), P(("z", "x", "c"), None)),
        check_vma=False,
    )
```

```python
import functools

import jax
import jax.numpy as jnp
from jax import lax
from jax.experimental import pallas as pl
from jax.experimental.pallas import tpu as pltpu
from jax.sharding import Mesh, PartitionSpec as P

ITERS = 3
SHARP = 48.0
EPSILON = 1e-06

AXES = ("z", "x", "c", "h", "y")
Z, X, C, H, Y = 8, 4, 2, 2, 4
BLOCKS = C * X
LANES = 128
PAD = 8


def exchange(blocks, axes):
    return lax.all_to_all(blocks, axes, 0, 0, tiled=True)


FETCHES = 55_500_000
FETCHES_BESIDE_SUMS = 53_000_000


def params(limit=8 << 20):
    return pltpu.CompilerParams(vmem_limit_bytes=limit)


def column_of(row):
    return jnp.broadcast_to(row, (LANES, row.shape[1])).T


def row_of(partial):
    return jnp.sum(partial.T, axis=0, keepdims=True)


def fold(product):
    total = product[:, :LANES]
    for start in range(LANES, product.shape[1], LANES):
        total = total + product[:, start : start + LANES]
    return total


def widen(column, width):
    return jnp.concatenate([column] * (width // LANES), axis=1)


def place(b):
    return (b % X) * C + b // X


AHEAD = 3


def fetch(steps, sems):
    copies, count = [], 0
    for pairs in steps:
        copies.append([pltpu.make_async_copy(*pair, sems.at[count + i]) for i, pair in enumerate(pairs)])
        count += len(pairs)

    def start(step):
        for copy in copies[step]:
            copy.start()

    def wait(step):
        if step + AHEAD < len(copies):
            start(step + AHEAD)
        for copy in copies[step]:
            copy.wait()

    for step in range(min(AHEAD, len(copies))):
        start(step)
    return wait


def setup_kernel(where_ref, latents_ref, codes_ref, tile_ref, rows_ref):
    del where_ref
    latents = latents_ref[...]
    width = latents.shape[1]
    floats = latents.astype(jnp.float32)
    mean = jnp.sum(floats * floats, axis=1, keepdims=True) * (1.0 / width)
    scale = jnp.broadcast_to(lax.rsqrt(mean + EPSILON) * (SHARP / width), (latents.shape[0], LANES))
    total = jnp.zeros(scale.shape, jnp.float32)
    across = (((1,), (1,)), ((), ()))
    for b in range(BLOCKS):
        codes = codes_ref[:, place(b)].reshape(-1, width)
        floats = codes.astype(jnp.float32)
        code_norm = lax.rsqrt(row_of(fold(floats * floats)) * (1.0 / width) + EPSILON)
        inner = lax.dot_general(latents, codes, across, preferred_element_type=jnp.float32)
        tile = jnp.exp(inner * widen(scale, codes.shape[0]) * code_norm)
        tile_ref[b] = tile
        total += fold(tile)
    rows_ref[...] = jnp.broadcast_to(row_of(total)[None], rows_ref.shape)


def rows_kernel(columns_ref, tile_ref, rows_ref):
    total = fold(tile_ref[0] * columns_ref[0])
    for b in range(1, BLOCKS):
        total += fold(tile_ref[b] * columns_ref[b])
    rows_ref[...] = jnp.broadcast_to(row_of(total)[None], rows_ref.shape)


def row_scale_of(parts_ref):
    return column_of(1.0 / jnp.sum(parts_ref[...], axis=0))


def columns_kernel(parts_ref, tile_ref, columns_ref):
    scale = row_scale_of(parts_ref)
    for b in range(BLOCKS):
        tile = tile_ref[b]
        columns_ref[b] = jnp.sum(tile * widen(scale, tile.shape[1]), axis=0, keepdims=True)


def targets_part(tile, scale, latents):
    weighted = (tile * widen(scale, tile.shape[1])).astype(jnp.bfloat16)
    return lax.dot_general(latents, weighted, (((0,), (0,)), ((), ())), preferred_element_type=jnp.float32)


def leave(pieces, sems, first):
    copies = [pltpu.make_async_copy(*piece, sems.at[first + i]) for i, piece in enumerate(pieces)]
    for copy in copies:
        copy.start()
    return copies


def targets_sent_kernel(where_ref, parts_ref, latents_ref, tile_ref, after_ref, out_ref, tiles_ref, done_ref, sems):
    del after_ref
    wait = fetch([[(tile_ref.at[where_ref[3] * X + (where_ref[1] ^ s)], tiles_ref.at[s])] for s in range(X)], sems)
    scale = row_scale_of(parts_ref)
    latents = latents_ref[...]
    copies = []
    for s in range(X):
        wait(s)
        done_ref[s] = targets_part(tiles_ref[s], scale, latents)
        copies += leave([(done_ref.at[s], out_ref.at[s])], sems, X + s)
    for copy in copies:
        copy.wait()


def targets_kept_kernel(
    where_ref, parts_ref, latents_ref, tile_ref, added_ref, after_ref,
    one_ref, two_ref, own_one_ref, own_two_ref, tiles_ref, more_ref, done_ref, sems,
):
    del after_ref
    steps = [
        [(tile_ref.at[where_ref[0] * X + (where_ref[1] ^ s)], tiles_ref.at[s]), (added_ref.at[s], more_ref.at[s])]
        for s in range(X)
    ]
    wait = fetch(steps, sems)
    scale = row_scale_of(parts_ref)
    latents = latents_ref[...]
    half = latents.shape[1] // 2
    uppers = (own_one_ref.at[0], one_ref.at[0], one_ref.at[1], own_one_ref.at[1])
    lowers = (own_two_ref.at[0], own_two_ref.at[1], two_ref.at[1], two_ref.at[0])
    copies = []
    for s in range(X):
        wait(s)
        done_ref[s] = targets_part(tiles_ref[s], scale, latents) + more_ref[s]
        pieces = [(done_ref.at[s, :half], uppers[s]), (done_ref.at[s, half:], lowers[s])]
        copies += leave(pieces, sems, 2 * X + 2 * s)
    for copy in copies:
        copy.wait()


def sum_kernel(parts_ref, *refs):
    out_ref = refs[-1]
    out_ref[...] = jnp.broadcast_to(jnp.sum(parts_ref[...], axis=0, keepdims=True), out_ref.shape)


def gather_kernel(parts_ref, after_ref, out_ref):
    del after_ref
    out_ref[...] = jnp.sum(parts_ref[...], axis=0)


def inverse_kernel(factor, parts_ref, *refs):
    out_ref = refs[-1]
    out_ref[...] = jnp.broadcast_to(factor / jnp.sum(parts_ref[...], axis=0, keepdims=True), out_ref.shape)


def kept_kernel(near_ref, out_ref):
    out_ref[...] = near_ref[...]


def join_kernel(kept_ref, came_ref, after_ref, spread_ref, mass_ref):
    del after_ref
    total = kept_ref[...] + came_ref[...]
    group = spread_ref.shape[1]
    spread_ref[...] = jnp.broadcast_to(total[None, :group], spread_ref.shape)
    mass_ref[...] = total[group:]


def turn_kernel(where_ref, own_one_ref, one_ref, more_one_ref, own_two_ref, two_ref, more_two_ref, *refs):
    send_ref, keep_ref, turned_ref = refs
    upper = own_one_ref[0] + one_ref[0] + more_one_ref[...]
    lower = own_two_ref[0] + two_ref[0] + more_two_ref[...]
    turned_ref[...] = jnp.concatenate([upper, lower], axis=0).T
    share = send_ref.shape[1]
    for i, slot in enumerate((0, 4, 2, 6)):
        for ref, s in ((keep_ref, slot), (send_ref, slot + 1)):
            start = pl.multiple_of((where_ref[2] ^ s) * share, share)
            ref[i] = turned_ref[pl.ds(start, share), :]


def final_kernel(
    parts_ref, columns_ref, codes_ref, tile_ref, more_one_ref, more_two_ref,
    out_ref, held_ref, tiles_ref, numer_ref, sems,
):
    del more_one_ref, more_two_ref
    steps = [
        [(tile_ref.at[b], tiles_ref.at[b]), (codes_ref.at[:, place(b)], held_ref.at[b])] for b in range(BLOCKS)
    ]
    wait = fetch(steps, sems)
    tokens, width = numer_ref.shape
    scale = row_scale_of(parts_ref)
    total = jnp.zeros(scale.shape, jnp.float32)
    for b in range(BLOCKS):
        wait(b)
        tile = tiles_ref[b]
        plan = (widen(scale, tile.shape[1]) * tile * columns_ref[b]).astype(jnp.bfloat16)
        total += fold(plan.astype(jnp.float32))
        part = jnp.dot(plan, held_ref[b].reshape(-1, width), preferred_element_type=jnp.float32)
        numer_ref[...] = part if b == 0 else numer_ref[...] + part
    group = tokens // Y
    mass = row_of(total)
    mass = jnp.concatenate([mass, jnp.zeros((1, 2 * width - tokens), jnp.float32)], axis=1)
    extra = jnp.concatenate(
        [mass[:, :width], mass[:, width:], jnp.zeros((PAD - 2, width), jnp.float32)], axis=0
    )
    for y in range(Y):
        out_ref[y, :group, :] = numer_ref[y * group : (y + 1) * group, :]
        out_ref[y, group:, :] = extra


def f32(*shape):
    return jax.ShapeDtypeStruct(shape, jnp.float32)


def cost(flops, moved, exps=0):
    return pl.CostEstimate(flops=flops, bytes_accessed=moved, transcendentals=exps)


def per_device(latents, codebook):
    token_count, width = latents.shape
    code_count = codebook.shape[0]
    total_tokens = token_count * Z * X * C
    total_codes = code_count * H * Y
    share = code_count // (Z * X * C)
    block = code_count // BLOCKS
    size = token_count * code_count

    codes = codebook.reshape(Z, X * C, share, width)
    vmem = pl.BlockSpec(memory_space=pltpu.VMEM)
    smem = pl.BlockSpec(memory_space=pltpu.SMEM)
    hbm = pl.BlockSpec(memory_space=pltpu.HBM)
    anywhere = pl.BlockSpec(memory_space=pl.ANY)
    held = pltpu.VMEM((BLOCKS, Z, share, width), jnp.bfloat16)
    tiles = functools.partial(pltpu.VMEM, dtype=jnp.float32)
    rows_shape = f32(H * Y, 1, token_count)
    columns_shape = f32(BLOCKS, 1, block)

    core, x, z = (lax.axis_index(axis) for axis in ("c", "x", "z"))
    where = jnp.stack([core, x, z, 1 - core, z * share])

    tile, part = pl.pallas_call(
        setup_kernel,
        in_specs=[smem, vmem, vmem],
        out_specs=[vmem, vmem],
        out_shape=[f32(BLOCKS, token_count, block), rows_shape],
        compiler_params=params(40_000_000),
        cost_estimate=cost(2 * size * width, 4 * size, size),
        name="setup",
    )(where, latents, codes)

    def sweep(kernel, name, given, shape):
        return pl.pallas_call(
            kernel,
            in_specs=[vmem, vmem],
            out_specs=vmem,
            out_shape=shape,
            compiler_params=params(),
            cost_estimate=cost(2 * size, 4 * size),
            name=name,
        )(given, tile)

    def rows(columns):
        return sweep(rows_kernel, "rows", columns, rows_shape)

    def columns(parts):
        return sweep(columns_kernel, "columns", parts, columns_shape)

    def targets_sent(parts, after):
        return pl.pallas_call(
            targets_sent_kernel,
            in_specs=[smem, vmem, vmem, hbm, anywhere],
            out_specs=hbm,
            out_shape=f32(X, width, block),
            scratch_shapes=[
                tiles((X, token_count, block)),
                tiles((X, width, block)),
                pltpu.SemaphoreType.DMA((2 * X,)),
            ],
            compiler_params=params(FETCHES),
            cost_estimate=cost(size * width, 4 * size),
            name="targets_sent",
        )(where, parts, latents, tile, after)

    def targets_kept(parts, added, after):
        return pl.pallas_call(
            targets_kept_kernel,
            in_specs=[smem, vmem, vmem, hbm, anywhere, anywhere],
            out_specs=[hbm] * 4,
            out_shape=[f32(2, width // 2, block)] * 4,
            scratch_shapes=[
                tiles((X, token_count, block)),
                tiles((X, width, block)),
                tiles((X, width, block)),
                pltpu.SemaphoreType.DMA((4 * X,)),
            ],
            compiler_params=params(FETCHES_BESIDE_SUMS),
            cost_estimate=cost(size * width, 4 * size),
            name="targets_kept",
        )(where, parts, latents, tile, added, after)

    def small(kernel, name, count, weight, parts, *after):
        return pl.pallas_call(
            kernel,
            in_specs=[vmem] + [anywhere] * len(after),
            out_specs=vmem,
            out_shape=f32(count, 1, block),
            compiler_params=params(),
            cost_estimate=cost(weight * parts.size, 4 * parts.size),
            name=name,
        )(parts, *after)

    inverse = functools.partial(inverse_kernel, total_tokens / total_codes)
    def swap(value, axis, count, bits):
        return lax.ppermute(value, axis, [(i, i ^ bits) for i in range(count)])

    for sweep_index in range(ITERS):
        last = sweep_index == ITERS - 1
        parts = exchange(part, ("h", "y"))
        column_sums = columns(parts)
        if last:
            sent = targets_sent(parts, column_sums)
        sums = small(sum_kernel, "sums", Z, 20_000_000 if last else 1, exchange(column_sums, ("c", "x")))
        if last:
            kept = targets_kept(parts, swap(sent, "c", C, 1), sums)
        after = (kept[0],) if last else ()
        mine = small(inverse, "inverse", BLOCKS, 2_000_000 if last else 1, exchange(sums, "z"), *after)
        col_scale = exchange(mine, ("c", "x"))
        if not last:
            part = rows(col_scale)

    one, two, own_one, own_two = kept
    one, two = swap(one, "x", X, 1), swap(two, "x", X, 3)
    more_one, more_two = own_one[1] + one[1], own_two[1] + two[1]

    group = token_count // Y
    packed = pl.pallas_call(
        final_kernel,
        in_specs=[vmem, vmem, hbm, hbm, anywhere, anywhere],
        out_specs=vmem,
        out_shape=f32(Y, group + PAD, width),
        scratch_shapes=[
            held,
            tiles((BLOCKS, token_count, block)),
            tiles((token_count, width)),
            pltpu.SemaphoreType.DMA((2 * BLOCKS,)),
        ],
        compiler_params=params(FETCHES),
        cost_estimate=cost(12 * size * width, 4 * size),
        name="final",
    )(parts, col_scale, codes, tile, more_one, more_two)
    more_one, more_two = swap(more_one, "x", X, 3), swap(more_two, "x", X, 1)
    away, near = pl.pallas_call(
        turn_kernel,
        in_specs=[smem] + [vmem] * 6,
        out_specs=[vmem] * 2,
        out_shape=[f32(Z // 2, share, width)] * 2,
        scratch_shapes=[pltpu.VMEM((block, width), jnp.float32)],
        compiler_params=params(16 << 20),
        cost_estimate=cost(3 * block * width, 12 * block * width),
        name="turn",
    )(where, own_one, one, more_one, own_two, two, more_two)
    packed = pl.pallas_call(
        gather_kernel,
        in_specs=[vmem, anywhere],
        out_specs=vmem,
        out_shape=f32(group + PAD, width),
        compiler_params=params(),
        cost_estimate=cost(packed.size, 4 * packed.size),
        name="gathered",
    )(exchange(packed, "y"), away)
    near = near + swap(away, "z", Z, 1)
    came = swap(near[2:], "z", Z, 2)
    near = pl.pallas_call(
        kept_kernel,
        in_specs=[vmem],
        out_specs=vmem,
        out_shape=f32(2, share, width),
        compiler_params=params(),
        cost_estimate=cost(400_000 * share * width, 16 * share * width),
        name="kept",
    )(near[:2]) + came
    numer, mass = pl.pallas_call(
        join_kernel,
        in_specs=[vmem] * 2 + [anywhere],
        out_specs=[vmem] * 2,
        out_shape=[f32(Y, group, width), f32(PAD, width)],
        compiler_params=params(),
        cost_estimate=cost(400_000 * token_count * width, 8 * token_count * width),
        name="join",
    )(packed, swap(packed, "h", H, 1), near)
    summed = near[0] + swap(near[1], "z", Z, 4)
    own = lax.dynamic_slice(mine, (0, 0, where[4]), (1, 1, share)).reshape(share)
    targets = summed * (own * (total_codes / total_tokens))[:, None]
    mass = mass[:2].reshape(2 * width)[:token_count]
    rebuilt = exchange(numer, "y").reshape(token_count, width) / mass[:, None]
    return (targets, rebuilt)


def solution(mesh):
    fine = Mesh(mesh.devices.reshape(Z, X, C, H, Y), AXES)
    return jax.shard_map(
        per_device,
        mesh=fine,
        in_specs=(P(("z", "x", "c"), None), P(("h", "y"), None)),
        out_specs=(P(("h", "y", "z", "x", "c"), None), P(("z", "x", "c"), None)),
        check_vma=False,
    )
```

```python
import functools

import jax
import jax.numpy as jnp
from jax import lax
from jax.experimental import pallas as pl
from jax.experimental.pallas import tpu as pltpu
from jax.sharding import Mesh, PartitionSpec as P

ITERS = 3
SHARP = 48.0
EPSILON = 1e-06

AXES = ("z", "x", "c", "h", "y")
Z, X, C, H, Y = 8, 4, 2, 2, 4
BLOCKS = C * X
LANES = 128
PAD = 8


def exchange(blocks, axes):
    return lax.all_to_all(blocks, axes, 0, 0, tiled=True)


FETCHES = 55_500_000
FETCHES_BESIDE_SUMS = 53_000_000


def params(limit=8 << 20):
    return pltpu.CompilerParams(vmem_limit_bytes=limit)


def column_of(row):
    return jnp.broadcast_to(row, (LANES, row.shape[1])).T


def row_of(partial):
    return jnp.sum(partial.T, axis=0, keepdims=True)


def fold(product):
    total = product[:, :LANES]
    for start in range(LANES, product.shape[1], LANES):
        total = total + product[:, start : start + LANES]
    return total


def widen(column, width):
    return jnp.concatenate([column] * (width // LANES), axis=1)


def place(b):
    return (b % X) * C + b // X


AHEAD = 2


def fetch(steps, sems):
    copies, count = [], 0
    for pairs in steps:
        copies.append([pltpu.make_async_copy(*pair, sems.at[count + i]) for i, pair in enumerate(pairs)])
        count += len(pairs)

    def start(step):
        for copy in copies[step]:
            copy.start()

    def wait(step):
        if step + AHEAD < len(copies):
            start(step + AHEAD)
        for copy in copies[step]:
            copy.wait()

    for step in range(min(AHEAD, len(copies))):
        start(step)
    return wait


def setup_kernel(where_ref, latents_ref, codes_ref, tile_ref, rows_ref):
    del where_ref
    latents = latents_ref[...]
    width = latents.shape[1]
    floats = latents.astype(jnp.float32)
    mean = jnp.sum(floats * floats, axis=1, keepdims=True) * (1.0 / width)
    scale = jnp.broadcast_to(lax.rsqrt(mean + EPSILON) * (SHARP / width), (latents.shape[0], LANES))
    total = jnp.zeros(scale.shape, jnp.float32)
    across = (((1,), (1,)), ((), ()))
    for b in range(BLOCKS):
        codes = codes_ref[:, place(b)].reshape(-1, width)
        floats = codes.astype(jnp.float32)
        code_norm = lax.rsqrt(row_of(fold(floats * floats)) * (1.0 / width) + EPSILON)
        inner = lax.dot_general(latents, codes, across, preferred_element_type=jnp.float32)
        tile = jnp.exp(inner * widen(scale, codes.shape[0]) * code_norm)
        tile_ref[b] = tile
        total += fold(tile)
    rows_ref[...] = jnp.broadcast_to(row_of(total)[None], rows_ref.shape)


def rows_kernel(columns_ref, tile_ref, rows_ref):
    total = fold(tile_ref[0] * columns_ref[0])
    for b in range(1, BLOCKS):
        total += fold(tile_ref[b] * columns_ref[b])
    rows_ref[...] = jnp.broadcast_to(row_of(total)[None], rows_ref.shape)


def row_scale_of(parts_ref):
    return column_of(1.0 / jnp.sum(parts_ref[...], axis=0))


def columns_kernel(parts_ref, tile_ref, columns_ref):
    scale = row_scale_of(parts_ref)
    for b in range(BLOCKS):
        tile = tile_ref[b]
        columns_ref[b] = jnp.sum(tile * widen(scale, tile.shape[1]), axis=0, keepdims=True)


def targets_part(tile, scale, latents):
    weighted = (tile * widen(scale, tile.shape[1])).astype(jnp.bfloat16)
    return lax.dot_general(latents, weighted, (((0,), (0,)), ((), ())), preferred_element_type=jnp.float32)


def leave(pieces, sems, first):
    copies = [pltpu.make_async_copy(*piece, sems.at[first + i]) for i, piece in enumerate(pieces)]
    for copy in copies:
        copy.start()
    return copies


def targets_sent_kernel(where_ref, parts_ref, latents_ref, tile_ref, after_ref, out_ref, tiles_ref, done_ref, sems):
    del after_ref
    wait = fetch([[(tile_ref.at[where_ref[3] * X + (where_ref[1] ^ s)], tiles_ref.at[s])] for s in range(X)], sems)
    scale = row_scale_of(parts_ref)
    latents = latents_ref[...]
    copies = []
    for s in range(X):
        wait(s)
        done_ref[s] = targets_part(tiles_ref[s], scale, latents)
        copies += leave([(done_ref.at[s], out_ref.at[s])], sems, X + s)
    for copy in copies:
        copy.wait()


def targets_kept_kernel(
    where_ref, parts_ref, latents_ref, tile_ref, added_ref, after_ref,
    one_ref, two_ref, own_one_ref, own_two_ref, tiles_ref, more_ref, done_ref, sems,
):
    del after_ref
    steps = [
        [(tile_ref.at[where_ref[0] * X + (where_ref[1] ^ s)], tiles_ref.at[s]), (added_ref.at[s], more_ref.at[s])]
        for s in range(X)
    ]
    wait = fetch(steps, sems)
    scale = row_scale_of(parts_ref)
    latents = latents_ref[...]
    half = latents.shape[1] // 2
    uppers = (own_one_ref.at[0], one_ref.at[0], one_ref.at[1], own_one_ref.at[1])
    lowers = (own_two_ref.at[0], own_two_ref.at[1], two_ref.at[1], two_ref.at[0])
    copies = []
    for s in range(X):
        wait(s)
        done_ref[s] = targets_part(tiles_ref[s], scale, latents) + more_ref[s]
        pieces = [(done_ref.at[s, :half], uppers[s]), (done_ref.at[s, half:], lowers[s])]
        copies += leave(pieces, sems, 2 * X + 2 * s)
    for copy in copies:
        copy.wait()


def sum_kernel(parts_ref, *refs):
    out_ref = refs[-1]
    out_ref[...] = jnp.broadcast_to(jnp.sum(parts_ref[...], axis=0, keepdims=True), out_ref.shape)


def gather_kernel(parts_ref, after_ref, out_ref):
    del after_ref
    out_ref[...] = jnp.sum(parts_ref[...], axis=0)


def inverse_kernel(factor, parts_ref, *refs):
    out_ref = refs[-1]
    out_ref[...] = jnp.broadcast_to(factor / jnp.sum(parts_ref[...], axis=0, keepdims=True), out_ref.shape)


def join_kernel(kept_ref, came_ref, after_ref, spread_ref, mass_ref):
    del after_ref
    total = kept_ref[...] + came_ref[...]
    group = spread_ref.shape[1]
    spread_ref[...] = jnp.broadcast_to(total[None, :group], spread_ref.shape)
    mass_ref[...] = total[group:]


def turn_kernel(where_ref, own_one_ref, one_ref, more_one_ref, own_two_ref, two_ref, more_two_ref, *refs):
    send_ref, keep_ref, turned_ref = refs
    upper = own_one_ref[0] + one_ref[0] + more_one_ref[...]
    lower = own_two_ref[0] + two_ref[0] + more_two_ref[...]
    turned_ref[...] = jnp.concatenate([upper, lower], axis=0).T
    share = send_ref.shape[1]
    for i, slot in enumerate((0, 4, 2, 6)):
        for ref, s in ((keep_ref, slot), (send_ref, slot + 1)):
            start = pl.multiple_of((where_ref[2] ^ s) * share, share)
            ref[i] = turned_ref[pl.ds(start, share), :]


def final_kernel(
    parts_ref, columns_ref, codes_ref, tile_ref, more_one_ref, more_two_ref,
    out_ref, held_ref, tiles_ref, numer_ref, sems,
):
    del more_one_ref, more_two_ref
    steps = [
        [(tile_ref.at[b], tiles_ref.at[b]), (codes_ref.at[:, place(b)], held_ref.at[b])] for b in range(BLOCKS)
    ]
    wait = fetch(steps, sems)
    tokens, width = numer_ref.shape
    scale = row_scale_of(parts_ref)
    total = jnp.zeros(scale.shape, jnp.float32)
    for b in range(BLOCKS):
        wait(b)
        tile = tiles_ref[b]
        plan = (widen(scale, tile.shape[1]) * tile * columns_ref[b]).astype(jnp.bfloat16)
        total += fold(plan.astype(jnp.float32))
        part = jnp.dot(plan, held_ref[b].reshape(-1, width), preferred_element_type=jnp.float32)
        numer_ref[...] = part if b == 0 else numer_ref[...] + part
    group = tokens // Y
    mass = row_of(total)
    mass = jnp.concatenate([mass, jnp.zeros((1, 2 * width - tokens), jnp.float32)], axis=1)
    extra = jnp.concatenate(
        [mass[:, :width], mass[:, width:], jnp.zeros((PAD - 2, width), jnp.float32)], axis=0
    )
    for y in range(Y):
        out_ref[y, :group, :] = numer_ref[y * group : (y + 1) * group, :]
        out_ref[y, group:, :] = extra


def f32(*shape):
    return jax.ShapeDtypeStruct(shape, jnp.float32)


def cost(flops, moved, exps=0):
    return pl.CostEstimate(flops=flops, bytes_accessed=moved, transcendentals=exps)


def per_device(latents, codebook):
    token_count, width = latents.shape
    code_count = codebook.shape[0]
    total_tokens = token_count * Z * X * C
    total_codes = code_count * H * Y
    share = code_count // (Z * X * C)
    block = code_count // BLOCKS
    size = token_count * code_count

    codes = codebook.reshape(Z, X * C, share, width)
    vmem = pl.BlockSpec(memory_space=pltpu.VMEM)
    smem = pl.BlockSpec(memory_space=pltpu.SMEM)
    hbm = pl.BlockSpec(memory_space=pltpu.HBM)
    anywhere = pl.BlockSpec(memory_space=pl.ANY)
    held = pltpu.VMEM((BLOCKS, Z, share, width), jnp.bfloat16)
    tiles = functools.partial(pltpu.VMEM, dtype=jnp.float32)
    rows_shape = f32(H * Y, 1, token_count)
    columns_shape = f32(BLOCKS, 1, block)

    core, x, z = (lax.axis_index(axis) for axis in ("c", "x", "z"))
    where = jnp.stack([core, x, z, 1 - core, z * share])

    tile, part = pl.pallas_call(
        setup_kernel,
        in_specs=[smem, vmem, vmem],
        out_specs=[vmem, vmem],
        out_shape=[f32(BLOCKS, token_count, block), rows_shape],
        compiler_params=params(40_000_000),
        cost_estimate=cost(2 * size * width, 4 * size, size),
        name="setup",
    )(where, latents, codes)

    def sweep(kernel, name, given, shape):
        return pl.pallas_call(
            kernel,
            in_specs=[vmem, vmem],
            out_specs=vmem,
            out_shape=shape,
            compiler_params=params(),
            cost_estimate=cost(2 * size, 4 * size),
            name=name,
        )(given, tile)

    def rows(columns):
        return sweep(rows_kernel, "rows", columns, rows_shape)

    def columns(parts):
        return sweep(columns_kernel, "columns", parts, columns_shape)

    def targets_sent(parts, after):
        return pl.pallas_call(
            targets_sent_kernel,
            in_specs=[smem, vmem, vmem, hbm, anywhere],
            out_specs=hbm,
            out_shape=f32(X, width, block),
            scratch_shapes=[
                tiles((X, token_count, block)),
                tiles((X, width, block)),
                pltpu.SemaphoreType.DMA((2 * X,)),
            ],
            compiler_params=params(FETCHES),
            cost_estimate=cost(size * width, 4 * size),
            name="targets_sent",
        )(where, parts, latents, tile, after)

    def targets_kept(parts, added, after):
        return pl.pallas_call(
            targets_kept_kernel,
            in_specs=[smem, vmem, vmem, hbm, anywhere, anywhere],
            out_specs=[hbm] * 4,
            out_shape=[f32(2, width // 2, block)] * 4,
            scratch_shapes=[
                tiles((X, token_count, block)),
                tiles((X, width, block)),
                tiles((X, width, block)),
                pltpu.SemaphoreType.DMA((4 * X,)),
            ],
            compiler_params=params(FETCHES_BESIDE_SUMS),
            cost_estimate=cost(size * width, 4 * size),
            name="targets_kept",
        )(where, parts, latents, tile, added, after)

    def small(kernel, name, count, weight, parts, *after):
        return pl.pallas_call(
            kernel,
            in_specs=[vmem] + [anywhere] * len(after),
            out_specs=vmem,
            out_shape=f32(count, 1, block),
            compiler_params=params(),
            cost_estimate=cost(weight * parts.size, 4 * parts.size),
            name=name,
        )(parts, *after)

    inverse = functools.partial(inverse_kernel, total_tokens / total_codes)
    def swap(value, axis, count, bits):
        return lax.ppermute(value, axis, [(i, i ^ bits) for i in range(count)])

    for sweep_index in range(ITERS):
        last = sweep_index == ITERS - 1
        parts = exchange(part, ("h", "y"))
        column_sums = columns(parts)
        if last:
            sent = targets_sent(parts, column_sums)
        sums = small(sum_kernel, "sums", Z, 20_000_000 if last else 1, exchange(column_sums, ("c", "x")))
        if last:
            kept = targets_kept(parts, swap(sent, "c", C, 1), sums)
        after = (kept[0],) if last else ()
        mine = small(inverse, "inverse", BLOCKS, 2_000_000 if last else 1, exchange(sums, "z"), *after)
        col_scale = exchange(mine, ("c", "x"))
        if not last:
            part = rows(col_scale)

    one, two, own_one, own_two = kept
    one, two = swap(one, "x", X, 1), swap(two, "x", X, 3)
    more_one, more_two = own_one[1] + one[1], own_two[1] + two[1]

    group = token_count // Y
    packed = pl.pallas_call(
        final_kernel,
        in_specs=[vmem, vmem, hbm, hbm, anywhere, anywhere],
        out_specs=vmem,
        out_shape=f32(Y, group + PAD, width),
        scratch_shapes=[
            held,
            tiles((BLOCKS, token_count, block)),
            tiles((token_count, width)),
            pltpu.SemaphoreType.DMA((2 * BLOCKS,)),
        ],
        compiler_params=params(FETCHES),
        cost_estimate=cost(12 * size * width, 4 * size),
        name="final",
    )(parts, col_scale, codes, tile, more_one, more_two)
    more_one, more_two = swap(more_one, "x", X, 3), swap(more_two, "x", X, 1)
    away, near = pl.pallas_call(
        turn_kernel,
        in_specs=[smem] + [vmem] * 6,
        out_specs=[vmem] * 2,
        out_shape=[f32(Z // 2, share, width)] * 2,
        scratch_shapes=[pltpu.VMEM((block, width), jnp.float32)],
        compiler_params=params(16 << 20),
        cost_estimate=cost(3 * block * width, 12 * block * width),
        name="turn",
    )(where, own_one, one, more_one, own_two, two, more_two)
    packed = pl.pallas_call(
        gather_kernel,
        in_specs=[vmem, anywhere],
        out_specs=vmem,
        out_shape=f32(group + PAD, width),
        compiler_params=params(),
        cost_estimate=cost(packed.size, 4 * packed.size),
        name="gathered",
    )(exchange(packed, "y"), away)
    near = near + swap(away, "z", Z, 1)
    numer, mass = pl.pallas_call(
        join_kernel,
        in_specs=[vmem] * 2 + [anywhere],
        out_specs=[vmem] * 2,
        out_shape=[f32(Y, group, width), f32(PAD, width)],
        compiler_params=params(),
        cost_estimate=cost(20000 * token_count * width, 8 * token_count * width),
        name="join",
    )(packed, swap(packed, "h", H, 1), near)
    near = near[:2] + swap(near[2:], "z", Z, 2)
    summed = near[0] + swap(near[1], "z", Z, 4)
    own = lax.dynamic_slice(mine, (0, 0, where[4]), (1, 1, share)).reshape(share)
    targets = summed * (own * (total_codes / total_tokens))[:, None]
    mass = mass[:2].reshape(2 * width)[:token_count]
    rebuilt = exchange(numer, "y").reshape(token_count, width) / mass[:, None]
    return (targets, rebuilt)


def solution(mesh):
    fine = Mesh(mesh.devices.reshape(Z, X, C, H, Y), AXES)
    return jax.shard_map(
        per_device,
        mesh=fine,
        in_specs=(P(("z", "x", "c"), None), P(("h", "y"), None)),
        out_specs=(P(("h", "y", "z", "x", "c"), None), P(("z", "x", "c"), None)),
        check_vma=False,
    )
```
